32 devices in a mesh: dp: 16 (over z, y, x), tensor: 2 (over core).
Axes of the slice: x: 2, y: 2, z: 4, core: 2. Of those that a mesh axis runs over, the one named last changes fastest.
Arguments:
- tokens: bfloat16 [16, 1024, 1024], P('dp'), may hold values from -6 to 6
- cotangent: bfloat16 [16, 1024, 1024], P('dp'), may hold values from -6 to 6
- lengths: int32 [16], P('dp'), may hold values from 128 to 1024, as said below
- noise_times: int32 [16], P('dp'), may hold values from 0 to 255
- query_weight: bfloat16 [1024, 1024], P(None, 'tensor'), may hold values from -0.1875 to 0.1875
- key_weight: bfloat16 [1024, 1024], P(None, 'tensor'), may hold values from -0.1875 to 0.1875
- value_weight: bfloat16 [1024, 1024], P(None, 'tensor'), may hold values from -0.1875 to 0.1875
- merge_weight: bfloat16 [1024, 1024], P('tensor'), may hold values from -0.75 to 0.75
- up_weight: bfloat16 [1024, 4096], P(None, 'tensor'), may hold values from -0.1875 to 0.1875
- down_weight: bfloat16 [4096, 1024], P('tensor'), may hold values from -0.09375 to 0.09375
- first_scales: float32 [256, 1024], replicated, may hold values from 0.1 to 1.9
- second_scales: float32 [256, 1024], replicated, may hold values from 0.1 to 1.9
Outputs:
- layer_output: bfloat16 [16, 1024, 1024], P('dp')
- grad_tokens: bfloat16 [16, 1024, 1024], P('dp')
- grad_query: float32 [1024, 1024], P('dp', 'tensor')
- grad_key: float32 [1024, 1024], P('dp', 'tensor')
- grad_value: float32 [1024, 1024], P('dp', 'tensor')
- grad_merge: float32 [1024, 1024], P('tensor', 'dp')
- grad_up: float32 [1024, 4096], P('dp', 'tensor')
- grad_down: float32 [4096, 1024], P('tensor', 'dp')
- grad_first: float32 [256, 1024], P(None, 'dp')
- grad_second: float32 [256, 1024], P(None, 'dp')
The draws below stay inside these ranges and needn't reach their ends.
Inputs may be any that keep to these rules, and one draw needn't show every extreme that they name: `lengths`: some sequence has exactly 1024 tokens; the others have at least 128.
All inputs are finite; a program needn't handle non-finite values.
Results may differ from the reference program's by a relative error of at most 0.014.
Values sent between devices are 32-bit elements; how exact they have to be, the bound alone decides.
A program may use at most 192 MiB of HBM per device.

```python
import math
import jax
import jax.numpy as jnp
from jax import lax

D = 1024
HEADS = 16
FF = 4096
HEAD = 64
TSTEPS = 256
LEN = 1024
SEQS = 16


def draw_lengths(key, part):
    key = jax.random.fold_in(key, 11)
    first_key, second_key = jax.random.split(key)
    drawn = jax.random.randint(first_key, (SEQS,), max(1, LEN // 8), LEN + 1)
    chosen = jax.random.randint(second_key, (), 0, SEQS)
    return jnp.where(jnp.arange(SEQS) == chosen, LEN, drawn).astype(jnp.int32)


def with_ends(entries, rng, smallest, top_value):
    longest = entries.shape.index(max(entries.shape))
    spots = []
    for shift in (0, 1):
        where = [jax.random.randint(jax.random.fold_in(rng, axis), (), 0, length) for axis, length in enumerate(entries.shape)]
        where[longest] = (where[longest] + shift) % entries.shape[longest]
        spots.append(tuple(where))
    return entries.at[spots[0]].set(smallest).at[spots[1]].set(top_value)


def raised(values, key, source, target, parts, factor):
    def block_of(position):
        return (jnp.arange(values.shape[position]) // (values.shape[position] // parts)).reshape((-1,) + (1,) * (values.ndim - 1 - position))

    first = jax.random.permutation(key, parts)[block_of(target)]
    other_side = (block_of(target) + parts // 2) % parts
    return jnp.where((block_of(source) == first) | (block_of(source) == other_side), factor * values, values)


def level_of(key, dims, shards, low, high):
    level = 1.0
    for axis_at, parts in shards:
        steps = jax.random.uniform(jax.random.fold_in(jax.random.fold_in(key, 6), axis_at), (parts,), jnp.float32, low / len(shards), high / len(shards))
        level = level * jnp.repeat(jnp.exp(steps), dims[axis_at] // parts).reshape((-1,) + (1,) * (len(dims) - 1 - axis_at))
    return level


def bell_draw(rng, shape, scale, reach, cuts=(), kind=jnp.bfloat16):
    values = scale * jax.random.normal(rng, shape, jnp.float32)
    if cuts:
        values = values * level_of(rng, shape, cuts, -0.22, 0.18)
    return jnp.clip(values, -reach, reach).astype(kind)


def gaussian_with(own_key, shape, width, reach, cuts, heavy, kind=jnp.bfloat16):
    array = width * jax.random.normal(own_key, shape, jnp.float32)
    if cuts:
        array = array * level_of(own_key, shape, cuts, -0.22, 0.18)
    return jnp.clip(raised(array, jax.random.fold_in(own_key, 3), *heavy), -reach, reach).astype(kind)


def setup_inputs(seed: int = 0) -> dict:
    splits = jax.random.split(jax.random.key(seed), 13)
    return {
        "tokens": bell_draw(splits[0], (SEQS, LEN, D), 1.0, 6.0, ((0, 16),)),
        "cotangent": gaussian_with(splits[1], (SEQS, LEN, D), 1.0, 6.0, ((0, 16),), (0, 2, 16, 2.0)),
        "lengths": draw_lengths(jax.random.fold_in(splits[12], 71), 0),
        "noise_times": with_ends(jax.random.randint(splits[3], (SEQS,), 0, TSTEPS), jax.random.fold_in(splits[3], 1), 0, TSTEPS - 1).astype(jnp.int32),
        "query_weight": bell_draw(splits[4], (D, D), D ** -0.5, 0.1875, ((1, 2),)),
        "key_weight": bell_draw(splits[5], (D, D), D ** -0.5, 0.1875, ((1, 2),)),
        "value_weight": bell_draw(splits[6], (D, D), D ** -0.5, 0.1875, ((1, 2),)),
        "merge_weight": bell_draw(splits[7], (D, D), (D // 16) ** -0.5, 0.75, ((0, 2),)),
        "up_weight": bell_draw(splits[8], (D, FF), D ** -0.5, 0.1875, ((1, 2),)),
        "down_weight": bell_draw(splits[9], (FF, D), FF ** -0.5, 0.09375, ((0, 2),)),
        "first_scales": jnp.clip(1.0 + 0.18 * jax.random.normal(splits[10], (TSTEPS, D), jnp.float32), 0.1, 1.9),
        "second_scales": jnp.clip(1.0 + 0.18 * jax.random.normal(splits[11], (TSTEPS, D), jnp.float32), 0.1, 1.9),
    }


epsilon = 1e-05
highest = lax.Precision.HIGHEST

@jax.custom_vjp
def low(v):
    return lax.optimization_barrier(v.astype(jnp.bfloat16)).astype(jnp.float32)

@jax.custom_vjp
def low_back(v):
    return v

def low_keep(v):
    return (low(v), None)

def low_pass(kept, grad):
    return (grad,)

def back_keep(v):
    return (v, None)

def back_low(kept, grad):
    return (low(grad),)
low.defvjp(low_keep, low_pass)
low_back.defvjp(back_keep, back_low)

def matmul(left, right):
    return jnp.dot(left, right, precision=highest)

def gelu_tanh(values):
    return 0.5 * values * (1.0 + jnp.tanh(0.7978845608028654 * (values + 0.044715 * values * values * values)))

def rope_tables(length, head_size):
    halves = head_size // 2
    places = jnp.arange(length, dtype=jnp.float32)[:, None]
    frequency = jnp.exp(jnp.arange(halves, dtype=jnp.float32) * (-2.0 * math.log(10000.0) / head_size))
    angles = places * frequency[None, :]
    return (jnp.cos(angles), jnp.sin(angles))

def rotate(values, cos_table, sin_table):
    halves = values.shape[-1] // 2
    first_half = values[..., :halves]
    second_half = values[..., halves:]
    cosine = cos_table[:, None, :]
    sine_part = sin_table[:, None, :]
    return jnp.concatenate([first_half * cosine - second_half * sine_part, second_half * cosine + first_half * sine_part], axis=-1)

def normalize(values):
    centred = values - lax.optimization_barrier(jnp.mean(values, axis=-1, keepdims=True))
    return centred * lax.rsqrt(lax.optimization_barrier(jnp.mean(centred * centred, axis=-1, keepdims=True)) + epsilon)

def attend_block(query_block, key_rot, value_rows, key_bias):
    scores = low_back(jnp.einsum('qhd,khd->hqk', query_block, key_rot, precision=highest) * (1.0 / math.sqrt(HEAD)))
    scores = scores + key_bias[None, None, :]
    peak_score = lax.optimization_barrier(jnp.max(scores, axis=-1, keepdims=True))
    exponent = jnp.exp(scores - peak_score)
    soft = exponent / lax.optimization_barrier(jnp.sum(exponent, axis=-1, keepdims=True))
    return jnp.einsum('hqk,khd->qhd', low(soft), value_rows, precision=highest)

def sequence_forward(inputs_raw, row_mask, scale_one, scale_two, query_weight, key_weight, value_weight, merge_weight, up_weight, down_weight, cos_table, sin_table):
    length = inputs_raw.shape[0]
    inputs = inputs_raw * row_mask[:, None]
    normal_in = low(normalize(inputs) * scale_one[None, :])
    queries = low_back(matmul(normal_in, query_weight)).reshape(length, HEADS, HEAD)
    key_proj = low_back(matmul(normal_in, key_weight)).reshape(length, HEADS, HEAD)
    value_rows = low(low_back(matmul(normal_in, value_weight))).reshape(length, HEADS, HEAD)
    query_rot = low(rotate(queries, cos_table, sin_table))
    key_rot = low(rotate(key_proj, cos_table, sin_table))
    key_bias = (row_mask - 1.0) * 1000000000.0
    block_rows = min(512, length)
    checked = jax.checkpoint(attend_block)
    blocks = query_rot.reshape(length // block_rows, block_rows, HEADS, HEAD)
    attended = lax.map(lambda query_block: checked(query_block, key_rot, value_rows, key_bias), blocks)
    heads_out = low(low_back(attended.reshape(length, HEADS * HEAD)))
    hidden_one = inputs + low_back(matmul(heads_out, merge_weight))
    normal_mid = low(normalize(hidden_one) * scale_two[None, :])
    pre_act = low_back(matmul(normal_mid, up_weight))
    activated = low(gelu_tanh(pre_act))
    return (hidden_one + low_back(matmul(activated, down_weight))) * row_mask[:, None]

def reference(tokens, cotangent, lengths, noise_times, query_weight, key_weight, value_weight, merge_weight, up_weight, down_weight, first_scales, second_scales):
    weights = tuple((matrix.astype(jnp.float32) for matrix in (query_weight, key_weight, value_weight, merge_weight, up_weight, down_weight)))
    cos_table, sin_table = rope_tables(LEN, HEAD)

    def one_sequence(carry, seq_index):
        row_mask = (jnp.arange(LEN, dtype=jnp.int32) < lengths[seq_index]).astype(jnp.float32)
        moment = noise_times[seq_index]

        def forward(inputs_raw, table_one, table_two, *params):
            return sequence_forward(inputs_raw, row_mask, table_one[moment], table_two[moment], *params, cos_table, sin_table)
        result, backward = jax.vjp(forward, tokens[seq_index].astype(jnp.float32), first_scales.astype(jnp.float32), second_scales.astype(jnp.float32), *weights)
        gradients = backward(cotangent[seq_index].astype(jnp.float32))
        updated = tuple((running + gradient_part for running, gradient_part in zip(carry, gradients[1:])))
        return (updated, (result.astype(jnp.bfloat16), gradients[0].astype(jnp.bfloat16)))
    initial = tuple((jnp.zeros(matrix.shape, jnp.float32) for matrix in (first_scales, second_scales) + weights))
    sums, (outputs, grad_inputs) = lax.scan(one_sequence, initial, jnp.arange(SEQS, dtype=jnp.int32))
    return (outputs, grad_inputs, sums[2], sums[3], sums[4], sums[5], sums[6], sums[7], sums[0], sums[1])
```

```python
import functools
import math

import jax
import jax.numpy as jnp
from jax import lax
from jax.experimental import pallas as pl
from jax.experimental.pallas import tpu as pltpu
from jax.sharding import PartitionSpec as P

HEAD = 64
MESH = pl.DeviceIdType.MESH

NI = 24
TILE = 256
SR = 6
LAGS = (4, 7, 9, 11)

def group_of(i):
    one = lambda k: jnp.where(i >= k, 1, 0)
    return one(8) + one(16) + one(18)

def flip(d, w):
    return d + w * (1 - 2 * (lax.rem(lax.div(d, w), 2)))

def weight(c, s):
    k = lax.rem(c + s, 3)
    return 1 + (k * (k + 1)) // 2

def color_of(i):
    return lax.rem(lax.rem(i, 8), 3)

def grads_kernel(names, l0, l1, l2, l3, r0, r1, r2, r3, out,
           L, S1, R1, R2, R3, R4, rb, lsem, rsem, ssem, csem):
    d = lax.axis_index(names[0])
    t = lax.axis_index(names[1])
    lrefs = (l0, l1, l2, l3)
    rrefs = (r0, r1, r2, r3)
    def absolute(r):
        o = 0
        for b in range(4):
            db = lax.rem(lax.div(d, 2 ** b), 2)
            o = o + (2 ** b) * (db if not (r >> b) & 1 else 1 - db)
        return o
    loads = []
    for g in range(4):
        for r in range(16):
            c = pltpu.make_async_copy(lrefs[g].at[absolute(r)], L.at[g, r], lsem.at[g])
            c.start()
    bar = pltpu.get_barrier_semaphore()
    for w in (1, 2, 4, 8):
        pl.semaphore_signal(bar, inc=1, device_id=(flip(d, w), t), device_id_type=MESH)
    pl.semaphore_wait(bar, 4)

    def fetch(i, lane):
        firsts = (0, 8, 16, 18, 24)
        for g in range(4):
            @pl.when((i >= firsts[g]) & (i < firsts[g + 1]))
            def _():
                col = pl.multiple_of((i - firsts[g]) * TILE, TILE)
                pltpu.make_async_copy(rrefs[g].at[:, pl.ds(col, TILE)], rb.at[lane, lax.rem(i, 2)], rsem.at[lane, lax.rem(i, 2)]).start()
    def fetched(i, lane):
        pltpu.make_async_copy(r0.at[:, pl.ds(0, TILE)], rb.at[lane, lax.rem(i, 2)], rsem.at[lane, lax.rem(i, 2)]).wait()

    def product(i, first, lane):
        c = color_of(i)
        g = group_of(i)
        ws = [weight(c, s) for s in range(3)] + [8]
        rows = []
        for b2 in (0, 1):
            for b3 in (0, 1):
                for b4 in (0, 1):
                    r = first * ws[0] + b2 * ws[1] + b3 * ws[2] + b4 * ws[3]
                    rows.append(L[g, r])
        lhs = jnp.concatenate(rows, axis=0)
        return jnp.dot(lhs, rb[lane, lax.rem(i, 2)], preferred_element_type=jnp.float32).reshape(8, 64, TILE)

    def copy(i, s):
        c = color_of(i)
        w = weight(c, s) if s < 3 else 8
        src = (S1.at[lax.rem(i, SR)], R1.at[i, pl.ds(4, 4)], R2.at[i, pl.ds(2, 2)], R3.at[i, pl.ds(1, 1)])[s]
        dst = (R1.at[i], R2.at[i], R3.at[i], R4.at[i])[s]
        return pltpu.make_async_remote_copy(src_ref=src, dst_ref=dst, send_sem=ssem.at[s, i], recv_sem=csem.at[s, i],
                                            device_id=(flip(d, w), t), device_id_type=MESH)

    fetch(0, 0)
    fetch(0, 1)
    for g in range(4):
        pltpu.make_async_copy(L.at[g], L.at[g], lsem.at[g]).wait()

    def body(i, _):
        @pl.when(i < NI)
        def _():
            @pl.when(i + 1 < NI)
            def _():
                fetch(i + 1, 0)
            @pl.when(i >= SR)
            def _():
                copy(i - SR, 0).wait_send()
            fetched(i, 0)
            S1[lax.rem(i, SR)] = product(i, 1, 0)
            copy(i, 0).start()
        j = i - LAGS[0]
        @pl.when((j >= 0) & (j < NI))
        def _():
            @pl.when(j + 1 < NI)
            def _():
                fetch(j + 1, 1)
            fetched(j, 1)
            copy(j, 0).wait_recv()
            R1[j] += product(j, 0, 1)
            copy(j, 1).start()
        k = i - LAGS[1]
        @pl.when((k >= 0) & (k < NI))
        def _():
            copy(k, 1).wait_recv()
            R2[k] += R1[k, 0:4]
            copy(k, 2).start()
        m = i - LAGS[2]
        @pl.when((m >= 0) & (m < NI))
        def _():
            copy(m, 2).wait_recv()
            R3[m] += R2[m, 0:2]
            copy(m, 3).start()
        n = i - LAGS[3]
        @pl.when((n >= 0) & (n < NI))
        def _():
            copy(n, 3).wait_recv()
            out[n] = R4[n, 0] + R3[n, 0]
        return 0
    lax.fori_loop(0, NI + LAGS[3], body, 0)
    def drain(i, _):
        @pl.when(i >= NI - SR)
        def _():
            copy(i, 0).wait_send()
        for s in (1, 2, 3):
            copy(i, s).wait_send()
        return 0
    lax.fori_loop(0, NI, drain, 0)

def reduce_grads(names, lhs, rhs):
    ANY = pl.BlockSpec(memory_space=pl.ANY)
    return pl.pallas_call(
        functools.partial(grads_kernel, names),
        out_shape=jax.ShapeDtypeStruct((NI, 64, TILE), jnp.float32),
        in_specs=[ANY] * 8,
        out_specs=pl.BlockSpec(memory_space=pltpu.VMEM),
        scratch_shapes=[
            pltpu.VMEM((4, 16, 64, 1024), jnp.bfloat16),
            pltpu.VMEM((SR, 8, 64, TILE), jnp.float32),
            pltpu.VMEM((NI, 8, 64, TILE), jnp.float32),
            pltpu.VMEM((NI, 4, 64, TILE), jnp.float32),
            pltpu.VMEM((NI, 2, 64, TILE), jnp.float32),
            pltpu.VMEM((NI, 1, 64, TILE), jnp.float32),
            pltpu.VMEM((2, 2, 1024, TILE), jnp.bfloat16),
            pltpu.SemaphoreType.DMA((4,)),
            pltpu.SemaphoreType.DMA((2, 2)),
            pltpu.SemaphoreType.DMA((4, NI)),
            pltpu.SemaphoreType.DMA((4, NI)),
        ],
        compiler_params=pltpu.CompilerParams(collective_id=0, has_side_effects=True, vmem_limit_bytes=56 * 2**20),
        name="grads",
    )(*lhs, *rhs)


epsilon = 1e-05
highest = lax.Precision.HIGHEST


def gelu_tanh(values):
    return (
        0.5
        * values
        * (1.0 + jnp.tanh(0.7978845608028654 * (values + 0.044715 * values * values * values)))
    )


def rope_tables(length, head_size):
    halves = head_size // 2
    places = jnp.arange(length, dtype=jnp.float32)[:, None]
    frequency = jnp.exp(
        jnp.arange(halves, dtype=jnp.float32) * (-2.0 * math.log(10000.0) / head_size)
    )
    angles = places * frequency[None, :]
    return (jnp.cos(angles), jnp.sin(angles))


def rotate(values, cos_table, sin_table):
    halves = values.shape[-1] // 2
    first_half = values[..., :halves]
    second_half = values[..., halves:]
    cosine = cos_table[:, None, :]
    sine_part = sin_table[:, None, :]
    return jnp.concatenate(
        [
            first_half * cosine - second_half * sine_part,
            second_half * cosine + first_half * sine_part,
        ],
        axis=-1,
    )


def unrotate(gradient, cos_table, sin_table):
    halves = gradient.shape[-1] // 2
    first_half = gradient[..., :halves]
    second_half = gradient[..., halves:]
    cosine = cos_table[:, None, :]
    sine_part = sin_table[:, None, :]
    return jnp.concatenate(
        [
            first_half * cosine + second_half * sine_part,
            second_half * cosine - first_half * sine_part,
        ],
        axis=-1,
    )


def normalize(values):
    centred = values - jnp.mean(values, axis=-1, keepdims=True)
    inv_std = lax.rsqrt(jnp.mean(centred * centred, axis=-1, keepdims=True) + epsilon)
    return (centred * inv_std, inv_std)


def norm_back(grad_norm, normed, inv_std, scale_rows):
    grad_hat = grad_norm * scale_rows[:, None, :]
    grad_scale = jnp.sum(grad_norm * normed, axis=1)
    mean_grad = jnp.mean(grad_hat, axis=-1, keepdims=True)
    mean_cross = jnp.mean(grad_hat * normed, axis=-1, keepdims=True)
    return (inv_std * (grad_hat - mean_grad - normed * mean_cross), grad_scale)


def block_scores(query_block, key_rot, key_bias, scale_factor):
    scores = jnp.einsum("sqhd,skhd->shqk", query_block, key_rot, preferred_element_type=jnp.float32)
    return scores * scale_factor + key_bias[:, None, None, :]


def body(
    tokens,
    cotangent,
    lengths,
    noise_times,
    query_weight,
    key_weight,
    value_weight,
    merge_weight,
    up_weight,
    down_weight,
    first_scales,
    second_scales,
):
    seq_count, length, width = tokens.shape
    local_width = query_weight.shape[1]
    local_heads = local_width // HEAD
    table_rows = first_scales.shape[0]
    flat_rows = seq_count * length
    scale_factor = 1.0 / math.sqrt(HEAD)
    block_rows = min(512, length)
    head_shape = (seq_count, length, local_heads, HEAD)
    row_mask = (jnp.arange(length, dtype=jnp.int32)[None, :] < lengths[:, None]).astype(jnp.float32)
    key_bias = (row_mask - 1.0) * 1000000000.0
    one_hot = (noise_times[:, None] == jnp.arange(table_rows, dtype=jnp.int32)[None, :]).astype(
        jnp.float32
    )
    scale_one = jnp.dot(one_hot, first_scales, precision=highest)
    scale_two = jnp.dot(one_hot, second_scales, precision=highest)
    cos_table, sin_table = rope_tables(length, HEAD)
    inputs = tokens.astype(jnp.float32) * row_mask[:, :, None]
    normed_one, inv_one = normalize(inputs)
    normal_in = (normed_one * scale_one[:, None, :]).astype(jnp.bfloat16).reshape(flat_rows, width)
    queries = jnp.dot(normal_in, query_weight, preferred_element_type=jnp.float32).reshape(
        head_shape
    )
    key_proj = jnp.dot(normal_in, key_weight, preferred_element_type=jnp.float32).reshape(
        head_shape
    )
    value_rows = (
        jnp.dot(normal_in, value_weight, preferred_element_type=jnp.float32)
        .astype(jnp.bfloat16)
        .reshape(head_shape)
    )
    query_rot = rotate(queries, cos_table, sin_table).astype(jnp.bfloat16)
    key_rot = rotate(key_proj, cos_table, sin_table).astype(jnp.bfloat16)
    attended = []
    log_sums = []
    for offset in range(0, length, block_rows):
        scores = block_scores(
            query_rot[:, offset : offset + block_rows], key_rot, key_bias, scale_factor
        )
        peak_score = jnp.max(scores, axis=-1, keepdims=True)
        exponent = jnp.exp(scores - peak_score)
        totals = jnp.sum(exponent, axis=-1, keepdims=True)
        soft_weights = (exponent / totals).astype(jnp.bfloat16)
        log_sums.append(peak_score + jnp.log(totals))
        attended.append(
            jnp.einsum(
                "shqk,skhd->sqhd", soft_weights, value_rows, preferred_element_type=jnp.float32
            )
        )
    heads_out = (
        jnp.concatenate(attended, axis=1).astype(jnp.bfloat16).reshape(flat_rows, local_width)
    )
    attn_part = jnp.dot(heads_out, merge_weight, preferred_element_type=jnp.float32)
    attn_total = lax.psum(attn_part, "tensor")
    hidden_one = inputs + attn_total.reshape(seq_count, length, width)
    normed_two, inv_two = normalize(hidden_one)
    normal_mid = (normed_two * scale_two[:, None, :]).astype(jnp.bfloat16).reshape(flat_rows, width)
    pre_act = jnp.dot(normal_mid, up_weight, preferred_element_type=jnp.float32)
    activated = gelu_tanh(pre_act).astype(jnp.bfloat16)
    mlp_part = jnp.dot(activated, down_weight, preferred_element_type=jnp.float32)
    mlp_total = lax.psum(mlp_part, "tensor")
    layer_output = (
        (hidden_one + mlp_total.reshape(seq_count, length, width)) * row_mask[:, :, None]
    ).astype(jnp.bfloat16)
    grad_final = cotangent.astype(jnp.float32) * row_mask[:, :, None]
    grad_mlp = grad_final.astype(jnp.bfloat16).reshape(flat_rows, width)
    grad_act = jnp.dot(grad_mlp, down_weight.T, preferred_element_type=jnp.float32)
    unused_value, gelu_back = jax.vjp(gelu_tanh, pre_act)
    grad_pre = gelu_back(grad_act)[0].astype(jnp.bfloat16)
    mid_part = jnp.dot(grad_pre, up_weight.T, preferred_element_type=jnp.float32)
    grad_mid = lax.psum(mid_part, "tensor").reshape(seq_count, length, width)
    grad_hat_two, scale_grad_two = norm_back(grad_mid, normed_two, inv_two, scale_two)
    grad_hidden = grad_final + grad_hat_two
    grad_attn = grad_hidden.astype(jnp.bfloat16).reshape(flat_rows, width)
    grad_heads = (
        jnp.dot(grad_attn, merge_weight.T, preferred_element_type=jnp.float32)
        .astype(jnp.bfloat16)
        .reshape(head_shape)
    )
    grad_keys = jnp.zeros(head_shape, jnp.float32)
    grad_values = jnp.zeros(head_shape, jnp.float32)
    query_grads = []
    for block_index in range(len(log_sums)):
        offset = block_index * block_rows
        query_block = query_rot[:, offset : offset + block_rows]
        grad_block = grad_heads[:, offset : offset + block_rows]
        scores = block_scores(query_block, key_rot, key_bias, scale_factor)
        soft_weights = jnp.exp(scores - log_sums[block_index])
        grad_soft = jnp.einsum(
            "sqhd,skhd->shqk", grad_block, value_rows, preferred_element_type=jnp.float32
        )
        grad_values = grad_values + jnp.einsum(
            "shqk,sqhd->skhd",
            soft_weights.astype(jnp.bfloat16),
            grad_block,
            preferred_element_type=jnp.float32,
        )
        grad_scores = (
            soft_weights * (grad_soft - jnp.sum(soft_weights * grad_soft, axis=-1, keepdims=True))
        ).astype(jnp.bfloat16)
        query_grads.append(
            jnp.einsum("shqk,skhd->sqhd", grad_scores, key_rot, preferred_element_type=jnp.float32)
            * scale_factor
        )
        grad_keys = (
            grad_keys
            + jnp.einsum(
                "shqk,sqhd->skhd", grad_scores, query_block, preferred_element_type=jnp.float32
            )
            * scale_factor
        )
    query_back = (
        unrotate(jnp.concatenate(query_grads, axis=1), cos_table, sin_table)
        .astype(jnp.bfloat16)
        .reshape(flat_rows, local_width)
    )
    key_back = (
        unrotate(grad_keys, cos_table, sin_table)
        .astype(jnp.bfloat16)
        .reshape(flat_rows, local_width)
    )
    value_back = grad_values.astype(jnp.bfloat16).reshape(flat_rows, local_width)
    inner_part = jnp.dot(query_back, query_weight.T, preferred_element_type=jnp.float32)
    inner_part = inner_part + jnp.dot(key_back, key_weight.T, preferred_element_type=jnp.float32)
    inner_part = inner_part + jnp.dot(
        value_back, value_weight.T, preferred_element_type=jnp.float32
    )
    grad_inner = lax.psum(inner_part, "tensor").reshape(seq_count, length, width)
    grad_hat_one, scale_grad_one = norm_back(grad_inner, normed_one, inv_one, scale_one)
    grad_tokens = ((grad_hidden + grad_hat_one) * row_mask[:, :, None]).astype(jnp.bfloat16)
    lhs = (grad_mlp, normal_mid, grad_attn, normal_in)
    rhs = (activated, grad_pre, heads_out, jnp.concatenate([query_back, key_back, value_back], axis=1))
    chunks = lax.axis_size("dp")
    if chunks == 16:
        pieces = reduce_grads(
            ("dp", "tensor"), [a.T.reshape(chunks, width // chunks, flat_rows) for a in lhs], rhs
        )
        wide = lambda a: a.transpose(1, 0, 2).reshape(width // chunks, -1)
        sums = [wide(pieces[a:b]) for a, b in ((0, 8), (8, 16), (16, 18), (18, 24))]
    else:
        sums = [
            lax.psum_scatter(
                jnp.dot(a.T, b, preferred_element_type=jnp.float32), "dp", scatter_dimension=0, tiled=True
            )
            for a, b in zip(lhs, rhs)
        ]
    grad_down, grad_up, grad_merge, grad_qkv = sums
    grad_query, grad_key, grad_value = jnp.split(grad_qkv, 3, axis=1)
    table_terms = jnp.concatenate(
        [scale_grad_one, scale_grad_two, jnp.zeros((seq_count, 128), jnp.float32) + noise_times.astype(jnp.float32)[:, None]], axis=1
    )
    gathered = lax.all_gather(table_terms, "dp", axis=0, tiled=True)
    mine = lax.axis_index("dp") * (width // chunks)
    hits = (gathered[:, 2 * width][None, :] == jnp.arange(table_rows, dtype=jnp.float32)[:, None]).astype(jnp.float32)
    columns = jnp.concatenate(
        [lax.dynamic_slice_in_dim(gathered, k * width + mine, width // chunks, axis=1) for k in (0, 1)], axis=1
    )
    tables = jnp.dot(hits, columns, precision=highest)
    grad_first, grad_second = jnp.split(tables, 2, axis=1)
    return (
        layer_output,
        grad_tokens,
        grad_query,
        grad_key,
        grad_value,
        grad_merge.T,
        grad_up,
        grad_down.T,
        grad_first,
        grad_second,
    )


def solution(mesh):
    return jax.shard_map(
        body,
        mesh=mesh,
        in_specs=(
            P("dp", None, None),
            P("dp", None, None),
            P("dp"),
            P("dp"),
            P(None, "tensor"),
            P(None, "tensor"),
            P(None, "tensor"),
            P("tensor", None),
            P(None, "tensor"),
            P("tensor", None),
            P(),
            P(),
        ),
        out_specs=(
            P("dp", None, None),
            P("dp", None, None),
            P("dp", "tensor"),
            P("dp", "tensor"),
            P("dp", "tensor"),
            P("tensor", "dp"),
            P("dp", "tensor"),
            P("tensor", "dp"),
            P(None, "dp"),
            P(None, "dp"),
        ),
        check_vma=False,
    )
```

```python
import functools
import math

import jax
import jax.numpy as jnp
import numpy as np
from jax import lax
from jax.experimental import pallas as pl
from jax.experimental.pallas import tpu as pltpu
from jax.sharding import PartitionSpec as P

HEAD = 64
MESH = pl.DeviceIdType.MESH


epsilon = 1e-05
highest = lax.Precision.HIGHEST


def gelu_tanh(values):
    return (
        0.5
        * values
        * (1.0 + jnp.tanh(0.7978845608028654 * (values + 0.044715 * values * values * values)))
    )


def rope_tables(length, head_size):
    halves = head_size // 2
    places = jnp.arange(length, dtype=jnp.float32)[:, None]
    frequency = jnp.exp(
        jnp.arange(halves, dtype=jnp.float32) * (-2.0 * math.log(10000.0) / head_size)
    )
    angles = places * frequency[None, :]
    return (jnp.cos(angles), jnp.sin(angles))


def rotate(values, cos_table, sin_table):
    halves = values.shape[-1] // 2
    first_half = values[..., :halves]
    second_half = values[..., halves:]
    cosine = cos_table[:, None, :]
    sine_part = sin_table[:, None, :]
    return jnp.concatenate(
        [
            first_half * cosine - second_half * sine_part,
            second_half * cosine + first_half * sine_part,
        ],
        axis=-1,
    )


def unrotate(gradient, cos_table, sin_table):
    halves = gradient.shape[-1] // 2
    first_half = gradient[..., :halves]
    second_half = gradient[..., halves:]
    cosine = cos_table[:, None, :]
    sine_part = sin_table[:, None, :]
    return jnp.concatenate(
        [
            first_half * cosine + second_half * sine_part,
            second_half * cosine - first_half * sine_part,
        ],
        axis=-1,
    )


def normalize(values):
    centred = values - jnp.mean(values, axis=-1, keepdims=True)
    inv_std = lax.rsqrt(jnp.mean(centred * centred, axis=-1, keepdims=True) + epsilon)
    return (centred * inv_std, inv_std)


def norm_back(grad_norm, normed, inv_std, scale_rows):
    grad_hat = grad_norm * scale_rows[:, None, :]
    grad_scale = jnp.sum(grad_norm * normed, axis=1)
    mean_grad = jnp.mean(grad_hat, axis=-1, keepdims=True)
    mean_cross = jnp.mean(grad_hat * normed, axis=-1, keepdims=True)
    return (inv_std * (grad_hat - mean_grad - normed * mean_cross), grad_scale)


def block_scores(query_block, key_rot, key_bias, scale_factor):
    scores = jnp.einsum("sqhd,skhd->shqk", query_block, key_rot, preferred_element_type=jnp.float32)
    return scores * scale_factor + key_bias[:, None, None, :]


def rope_lanes(length):
    halves = HEAD // 2
    places = np.arange(length, dtype=np.float64)[:, None]
    frequency = np.exp(np.arange(halves) * (-2.0 * math.log(10000.0) / HEAD))
    angles = places * frequency[None, :]
    cosine, sine = np.cos(angles), np.sin(angles)
    return (
        np.concatenate([cosine] * 4, axis=1).astype(np.float32),
        np.concatenate([-sine, sine] * 2, axis=1).astype(np.float32),
    )


def swap_halves(values):
    lanes = lax.broadcasted_iota(jnp.int32, values.shape, 1)
    first = lax.rem(lanes, HEAD) < HEAD // 2
    half = HEAD // 2
    return jnp.where(first, pltpu.roll(values, 128 - half, 1), pltpu.roll(values, half, 1))


def centre(values):
    middle = jnp.mean(values, axis=1, keepdims=True)
    centred = values - middle
    inverse = lax.rsqrt(jnp.mean(centred * centred, axis=1, keepdims=True) + epsilon)
    return centred * inverse


NT = (((1,), (1,)), ((), ()))


def mm(a, b):
    return jnp.dot(a, b, preferred_element_type=jnp.float32)


def mm_nt(a, b):
    return lax.dot_general(a, b, NT, preferred_element_type=jnp.float32)


def forward_kernel(
    names, length_ref, tokens, scale_one, scale_two, cosine, sine, wq, wk, wv, wm, wu,
    nin, q_out, k_out, v_out, heads, heads_t, lse, hidden, mid, act, slope,
    vq, vk, vv, vm, vu, other_m, v_t, send_m, recv_m, send_o, recv_o, bias, wsem, ssem, rsem,
):
    rows, width = tokens.shape
    pairs = q_out.shape[0]
    here = {n: lax.axis_index(n) for n in names}
    other = {**here, names[1]: 1 - here[names[1]]}
    other = tuple(other[n] for n in names)
    loads = [
        pltpu.make_async_copy(a, b, wsem.at[i])
        for i, (a, b) in enumerate(((wq, vq), (wk, vk), (wv, vv), (wm, vm), (wu, vu)))
    ]
    for c in loads:
        c.start()
    barrier = pltpu.get_barrier_semaphore()
    pl.semaphore_signal(barrier, inc=1, device_id=other, device_id_type=MESH)
    pl.semaphore_wait(barrier, 1)
    length = length_ref[0]

    def place(start, count):
        return start + lax.broadcasted_iota(jnp.int32, (count, 1), 0)

    def mask_of(start, count):
        return jnp.where(place(start, count) < length, 1.0, 0.0)

    bias[...] = jnp.broadcast_to((mask_of(0, rows) - 1.0) * 1000000000.0, (rows, 128))

    def norm_rows(i, _):
        at = pl.multiple_of(i * 128, 128)
        x = tokens[pl.ds(at, 128), :].astype(jnp.float32) * mask_of(at, 128)
        nin[pl.ds(at, 128), :] = (centre(x) * scale_one[...]).astype(jnp.bfloat16)
        return 0

    lax.fori_loop(0, rows // 128, norm_rows, 0)
    for c in loads[:4]:
        c.wait()
    send_m[...] = vm[...].astype(jnp.float32)
    merge_copy = pltpu.make_async_remote_copy(
        src_ref=send_m, dst_ref=recv_m, send_sem=ssem.at[0], recv_sem=rsem.at[0],
        device_id=other, device_id_type=MESH,
    )
    merge_copy.start()

    def project(i, _):
        at = pl.multiple_of(i * 256, 256)
        own = pl.ds(at, 256)
        x = nin[own, :]
        c, s = cosine[own, :], sine[own, :]
        for ref, w in ((q_out, vq), (k_out, vk)):
            y = mm(x, w[...])
            for p in range(pairs):
                part = y[:, 128 * p : 128 * p + 128]
                ref[p, own, :] = (part * c + swap_halves(part) * s).astype(jnp.bfloat16)
        y = mm(x, vv[...])
        for p in range(pairs):
            part = y[:, 128 * p : 128 * p + 128]
            v_out[p, own, :] = part.astype(jnp.bfloat16)
            v_t[p, :, own] = part.T.astype(jnp.bfloat16)
        return 0

    lax.fori_loop(0, rows // 256, project, 0)

    def o_copy(p):
        return pltpu.make_async_remote_copy(
            src_ref=send_o.at[p], dst_ref=recv_o.at[p], send_sem=ssem.at[1 + p], recv_sem=rsem.at[1 + p],
            device_id=other, device_id_type=MESH,
        )

    lane = lax.broadcasted_iota(jnp.int32, (rows, 128), 1)
    block = 512

    def attend(p, _):
        for h in range(2):
            keys = jnp.where((lane < HEAD) == (h == 0), k_out[p] * 0.125, 0.0).astype(jnp.bfloat16)
            values_t = v_t[p, pl.ds(HEAD * h, HEAD), :]
            for b in range(rows // block):
                cols = pl.ds(b * block, block)
                s = mm_nt(keys, q_out[p, cols, :]) + bias[:, :1]
                peak = jnp.max(s, axis=0, keepdims=True)
                e = jnp.exp(s - peak)
                total = jnp.sum(e, axis=0, keepdims=True)
                o = mm(values_t, e.astype(jnp.bfloat16)) / total
                heads_t[p, pl.ds(HEAD * h, HEAD), cols] = o.astype(jnp.bfloat16)
                lse[pl.ds(2 * p + h, 1), cols] = peak + jnp.log(total)
        o = heads_t[p].astype(jnp.float32).T
        send_o[p] = o
        heads[p] = o.astype(jnp.bfloat16)
        o_copy(p).start()
        return 0

    lax.fori_loop(0, pairs, attend, 0)
    merge_copy.wait()
    other_m[...] = recv_m[...].astype(jnp.bfloat16)
    for p in range(pairs):
        o_copy(p).wait()
    loads[4].wait()

    def finish(i, _):
        at = pl.multiple_of(i * 256, 256)
        own = pl.ds(at, 256)
        mine = jnp.concatenate([heads[p, own, :] for p in range(pairs)], axis=1)
        theirs = jnp.concatenate([recv_o[p, own, :].astype(jnp.bfloat16) for p in range(pairs)], axis=1)
        attn = mm(mine, vm[...]) + mm(theirs, other_m[...])
        one = tokens[own, :].astype(jnp.float32) * mask_of(at, 256) + attn
        hidden[own, :] = one
        normal = (centre(one) * scale_two[...]).astype(jnp.bfloat16)
        mid[own, :] = normal
        for j in range(0, vu.shape[1], 512):
            v = mm(normal, vu[:, j : j + 512])
            square = v * v
            t = jnp.tanh(0.7978845608028654 * v * (1.0 + 0.044715 * square))
            up = 0.5 * (1.0 + t)
            act[own, j : j + 512] = (v * up).astype(jnp.bfloat16)
            slope[own, j : j + 512] = (
                up + 0.5 * v * (1.0 - t * t) * (0.7978845608028654 * (1.0 + 0.134145 * square))
            ).astype(jnp.bfloat16)
        return 0

    lax.fori_loop(0, rows // 256, finish, 0)


def forward(names, length, tokens, scale_one, scale_two, cosine, sine, wq, wk, wv, wm, wu):
    rows, width = tokens.shape
    local, units = wq.shape[1], wu.shape[1]
    pairs = local // 128
    vmem = pl.BlockSpec(memory_space=pltpu.VMEM)
    hbm = pl.BlockSpec(memory_space=pl.ANY)
    half = jnp.bfloat16
    full = jnp.float32
    shapes = [
        ((rows, width), half),
        ((pairs, rows, 128), half),
        ((pairs, rows, 128), half),
        ((pairs, rows, 128), half),
        ((pairs, rows, 128), half),
        ((pairs, 128, rows), half),
        ((2 * pairs, rows), full),
        ((rows, width), full),
        ((rows, width), half),
        ((rows, units), half),
        ((rows, units), half),
    ]
    return pl.pallas_call(
        functools.partial(forward_kernel, names),
        out_shape=[jax.ShapeDtypeStruct(*s) for s in shapes],
        in_specs=[pl.BlockSpec(memory_space=pltpu.SMEM)] + [vmem] * 5 + [hbm] * 5,
        out_specs=[vmem] * len(shapes),
        scratch_shapes=[
            pltpu.VMEM(wq.shape, half),
            pltpu.VMEM(wk.shape, half),
            pltpu.VMEM(wv.shape, half),
            pltpu.VMEM(wm.shape, half),
            pltpu.VMEM(wu.shape, half),
            pltpu.VMEM(wm.shape, half),
            pltpu.VMEM((pairs, 128, rows), half),
            pltpu.VMEM(wm.shape, full),
            pltpu.VMEM(wm.shape, full),
            pltpu.VMEM((pairs, rows, 128), full),
            pltpu.VMEM((pairs, rows, 128), full),
            pltpu.VMEM((rows, 128), full),
            pltpu.SemaphoreType.DMA((5,)),
            pltpu.SemaphoreType.DMA((1 + pairs,)),
            pltpu.SemaphoreType.DMA((1 + pairs,)),
        ],
        compiler_params=pltpu.CompilerParams(collective_id=1, has_side_effects=True, vmem_limit_bytes=58 * 2**20),
        name="forward",
    )(length, tokens, scale_one, scale_two, cosine, sine, wq, wk, wv, wm, wu)


ITEMS = 24
TILE = 256
RING = 6
HELD = 12
LAGS = (4, 7, 9, 11)
FIRSTS = (0, 8, 16, 18, 24)


def count_from(i, starts):
    total = 0
    for start in starts:
        total = total + jnp.where(i >= start, 1, 0)
    return total


def flip(index, weight):
    return index + weight * (1 - 2 * lax.rem(lax.div(index, weight), 2))


def weight_of(color, stage):
    k = lax.rem(color + stage, 3)
    return 1 + (k * (k + 1)) // 2


def color_of(i):
    return lax.rem(lax.rem(i, 8), 3)


def slot_of(i):
    return count_from(i, (8, 16)) - 2 * count_from(i, (18,))


def backward_kernel(
    names, length_ref, term_two, moment, scale_one,
    l_down, l_up, l_merge, l_qkv, r_down, r_up, heads, q_in, k_in, v_in, heads_t, lse_in, cosine, sine,
    attn_in, merge_in, wq, wk, wv, tokens, hidden_in,
    out, tokens_out, rows_out,
    left, s1, r1, r2, r3, r4, rb, qkv, recv_p, terms, lsem, fsem, ssem, csem, psem, qsem, gsem, jsem, credit,
):
    here = {n: lax.axis_index(n) for n in names}
    d = here[names[0]]

    def device(**moved):
        at = {**here, **moved}
        return tuple(at[n] for n in names)

    core = device(**{names[1]: 1 - here[names[1]]})

    def across(weight):
        return device(**{names[0]: flip(d, weight)})

    def absolute(r):
        total = 0
        for b in range(4):
            bit = lax.rem(lax.div(d, 2**b), 2)
            total = total + (2**b) * (1 - bit if (r >> b) & 1 else bit)
        return total

    def load_left(source, slot):
        for r in range(16):
            pltpu.make_async_copy(source.at[absolute(r)], left.at[slot, r], lsem.at[slot]).start()

    def left_loaded(slot):
        pltpu.make_async_copy(left.at[slot], left.at[slot], lsem.at[slot]).wait()

    load_left(l_down, 0)
    load_left(l_up, 1)
    load_left(l_merge, 2)
    barrier = pltpu.get_barrier_semaphore()
    for weight in (1, 2, 4, 8):
        pl.semaphore_signal(barrier, inc=1, device_id=across(weight), device_id_type=MESH)
    pl.semaphore_signal(barrier, inc=1, device_id=core, device_id_type=MESH)
    pl.semaphore_wait(barrier, 5)

    def fetch(i, lane):
        slot = lax.rem(i, 2)
        target, sem = rb.at[lane, slot], fsem.at[lane, slot]
        for g, source in ((0, r_down), (1, r_up)):
            @pl.when((i >= FIRSTS[g]) & (i < FIRSTS[g + 1]))
            def _():
                col = pl.multiple_of((i - FIRSTS[g]) * TILE, TILE)
                pltpu.make_async_copy(source.at[:, pl.ds(col, TILE)], target, sem).start()

        @pl.when((i >= FIRSTS[2]) & (i < FIRSTS[3]))
        def _():
            for k in range(2):
                pltpu.make_async_copy(
                    heads.at[2 * (i - FIRSTS[2]) + k], target.at[:, pl.ds(128 * k, 128)], sem
                ).start()

        @pl.when(i >= FIRSTS[3])
        def _():
            pltpu.make_async_copy(qkv.at[i - FIRSTS[3]], target, sem).start()

    def fetched(i, lane):
        slot = lax.rem(i, 2)
        pltpu.make_async_copy(rb.at[lane, slot], rb.at[lane, slot], fsem.at[lane, slot]).wait()

    def product(i, first, lane):
        color, slot = color_of(i), slot_of(i)
        weights = [weight_of(color, s) for s in range(3)] + [8]
        rows = []
        for bits in range(8):
            r = first * weights[0] + sum(((bits >> (2 - k)) & 1) * weights[1 + k] for k in range(3))
            rows.append(left[slot, r])
        lhs = jnp.concatenate(rows, axis=0)
        return mm(lhs, rb[lane, lax.rem(i, 2)]).reshape(8, 64, TILE)

    def copy(i, s):
        weight = weight_of(color_of(i), s) if s < 3 else 8
        src = (s1.at[lax.rem(i, RING)], r1.at[lax.rem(i, HELD), pl.ds(4, 4)], r2.at[i, pl.ds(2, 2)], r3.at[i, pl.ds(1, 1)])[s]
        dst = (r1.at[lax.rem(i, HELD)], r2.at[i], r3.at[i], r4.at[i])[s]
        return pltpu.make_async_remote_copy(
            src_ref=src, dst_ref=dst, send_sem=ssem.at[s, i], recv_sem=csem.at[s, i],
            device_id=across(weight), device_id_type=MESH,
        )

    def tick(i):
        @pl.when(i < ITEMS)
        def _():
            @pl.when(i >= RING)
            def _():
                copy(i - RING, 0).wait_send()

            fetched(i, 0)
            s1[lax.rem(i, RING)] = product(i, 1, 0)

            @pl.when(i >= HELD)
            def _():
                pl.semaphore_wait(credit.at[color_of(i)], 1)

            copy(i, 0).start()

            @pl.when((i + 2 < ITEMS))
            def _():
                fetch(i + 2, 0)

        a = i - LAGS[0]

        @pl.when((a >= 0) & (a < ITEMS))
        def _():
            fetched(a, 1)
            copy(a, 0).wait_recv()
            r1[lax.rem(a, HELD)] += product(a, 0, 1)
            copy(a, 1).start()

            @pl.when(a + 2 < ITEMS)
            def _():
                fetch(a + 2, 1)

        b = i - LAGS[1]

        @pl.when((b >= 0) & (b < ITEMS))
        def _():
            copy(b, 1).wait_recv()
            r2[b] += r1[lax.rem(b, HELD), 0:4]
            copy(b, 2).start()
            copy(b, 1).wait_send()

            @pl.when(b + HELD < ITEMS)
            def _():
                color = color_of(b + HELD)
                pl.semaphore_signal(
                    credit.at[color], inc=1, device_id=across(weight_of(color, 0)), device_id_type=MESH
                )

        c = i - LAGS[2]

        @pl.when((c >= 0) & (c < ITEMS))
        def _():
            copy(c, 2).wait_recv()
            r3[c] += r2[c, 0:2]
            copy(c, 3).start()

        e = i - LAGS[3]

        @pl.when((e >= 0) & (e < ITEMS))
        def _():
            copy(e, 3).wait_recv()
            out[e] = r4[e, 0] + r3[e, 0]

    for lane in range(2):
        fetch(jnp.int32(0), lane)
        fetch(jnp.int32(1), lane)
    rows, width = tokens.shape
    pairs = q_in.shape[0]
    length = length_ref[0]

    def attention(q, k, v, o_t, lse, ga, wm, cos, sin, bias, do, do_t, kh, vh, k_t, dq_t, asem):
        loads = [
            pltpu.make_async_copy(a, b, asem.at[n])
            for n, (a, b) in enumerate(
                ((q_in, q), (k_in, k), (v_in, v), (heads_t, o_t), (lse_in, lse), (attn_in, ga), (merge_in, wm),
                 (cosine, cos), (sine, sin))
            )
        ]
        for x in loads:
            x.start()
        left_loaded(0)
        lax.fori_loop(0, 4, lambda i, _: (tick(i), 0)[1], 0)
        for x in loads:
            x.wait()
        left_loaded(1)
        left_loaded(2)
        place = lax.broadcasted_iota(jnp.int32, (rows, 128), 0)
        bias[...] = (jnp.where(place < length, 1.0, 0.0) - 1.0) * 1000000000.0
        lane = lax.broadcasted_iota(jnp.int32, (rows, 128), 1) < HEAD
        block = 256

        def unrotate_lanes(y):
            return (y * cos[...] - swap_halves(y) * sin[...]).astype(jnp.bfloat16)

        def pair(p, _):
            weight = wm[pl.ds(pl.multiple_of(128 * p, 128), 128), :]
            do[...] = mm_nt(ga[...], weight).astype(jnp.bfloat16)
            do_t[...] = mm_nt(weight, ga[...]).astype(jnp.bfloat16)
            k_t[...] = (k[p].astype(jnp.float32) * 0.125).T.astype(jnp.bfloat16)
            product_t = do_t[...].astype(jnp.float32) * o_t[p].astype(jnp.float32)
            dks, dvs = [], []
            for h in range(2):
                tick(4 + 2 * p + h)
                delta = jnp.sum(product_t[HEAD * h : HEAD * h + HEAD], axis=0, keepdims=True)
                own = lane == (h == 0)
                kh[...] = jnp.where(own, k[p].astype(jnp.float32) * 0.125, 0.0).astype(jnp.bfloat16)
                vh[...] = jnp.where(own, v[p].astype(jnp.float32), 0.0).astype(jnp.bfloat16)
                dk = jnp.zeros((rows, 128), jnp.float32)
                dv = jnp.zeros((rows, 128), jnp.float32)
                for b in range(0, rows, block):
                    cols = slice(b, b + block)
                    qb = q[p, cols, :]
                    s = mm_nt(kh[...], qb) + bias[:, :1]
                    soft = jnp.exp(s - lse[pl.ds(2 * p + h, 1), cols])
                    ds = soft * (mm(vh[...], do_t[:, cols]) - delta[:, cols])
                    ds = ds.astype(jnp.bfloat16)
                    dv = dv + mm(soft.astype(jnp.bfloat16), do[cols, :])
                    dk = dk + mm(ds, qb)
                    dq_t[HEAD * h : HEAD * h + HEAD, cols] = mm(k_t[HEAD * h : HEAD * h + HEAD, :], ds)
                dks.append(dk)
                dvs.append(dv)
            quad = 3 * lax.div(p, 2)
            at = pl.ds(pl.multiple_of(128 * lax.rem(p, 2), 128), 128)
            qkv[quad, :, at] = unrotate_lanes(dq_t[...].T)
            qkv[quad + 1, :, at] = unrotate_lanes(jnp.where(lane, dks[0], dks[1]) * 0.125)
            qkv[quad + 2, :, at] = jnp.where(lane, dvs[0], dvs[1]).astype(jnp.bfloat16)
            return 0

        lax.fori_loop(0, pairs, pair, 0)

    half, full = jnp.bfloat16, jnp.float32
    pl.run_scoped(
        attention,
        pltpu.VMEM((pairs, rows, 128), half),
        pltpu.VMEM((pairs, rows, 128), half),
        pltpu.VMEM((pairs, rows, 128), half),
        pltpu.VMEM((pairs, 128, rows), half),
        pltpu.VMEM((2 * pairs, rows), full),
        pltpu.VMEM((rows, width), half),
        pltpu.VMEM(merge_in.shape, half),
        pltpu.VMEM((rows, 128), full),
        pltpu.VMEM((rows, 128), full),
        pltpu.VMEM((rows, 128), full),
        pltpu.VMEM((rows, 128), half),
        pltpu.VMEM((128, rows), half),
        pltpu.VMEM((rows, 128), half),
        pltpu.VMEM((rows, 128), half),
        pltpu.VMEM((128, rows), half),
        pltpu.VMEM((128, rows), full),
        pltpu.SemaphoreType.DMA((10,)),
    )
    load_left(l_qkv, 0)
    part = 256
    parts = rows // part

    def core_copy(i, send_p):
        return pltpu.make_async_remote_copy(
            src_ref=send_p.at[i], dst_ref=recv_p.at[i], send_sem=psem.at[i], recv_sem=qsem.at[i],
            device_id=core, device_id_type=MESH,
        )

    def inner(vq, vk, vv, x_in, gh, send_p, sem, hsem):
        loads = [pltpu.make_async_copy(a, b, sem.at[n]) for n, (a, b) in enumerate(((wq, vq), (wk, vk), (wv, vv), (tokens, x_in)))]
        for x in loads:
            x.start()
        for x in loads:
            x.wait()

        def send(i, _):
            own = pl.ds(pl.multiple_of(i * part, part), part)
            total = None
            for quad in range(2):
                for n, w in enumerate((vq, vk, vv)):
                    term = mm_nt(qkv[3 * quad + n, own, :], w[:, TILE * quad : TILE * quad + TILE])
                    total = term if total is None else total + term

            send_p[i] = total
            core_copy(i, send_p).start()
            tick(12 + i)
            return 0

        lax.fori_loop(0, parts, send, 0)
        left_loaded(0)

        def take(i, total):
            at = pl.multiple_of(i * part, part)
            own = pl.ds(at, part)
            hidden_copy = pltpu.make_async_copy(hidden_in.at[own, :], gh, hsem)
            hidden_copy.start()
            core_copy(i, send_p).wait_recv()
            grad = send_p[i] + recv_p[i]
            keep = jnp.where(at + lax.broadcasted_iota(jnp.int32, (part, 1), 0) < length, 1.0, 0.0)
            x = x_in[own, :].astype(jnp.float32) * keep
            centred = x - jnp.mean(x, axis=1, keepdims=True)
            inverse = lax.rsqrt(jnp.mean(centred * centred, axis=1, keepdims=True) + epsilon)
            normed = centred * inverse
            hat = grad * scale_one[...]
            back = inverse * (
                hat - jnp.mean(hat, axis=1, keepdims=True) - normed * jnp.mean(hat * normed, axis=1, keepdims=True)
            )
            hidden_copy.wait()
            tokens_out[own, :] = ((gh[...] + back) * keep).astype(jnp.bfloat16)
            tick(12 + parts + i)
            return total + jnp.sum(grad * normed, axis=0, keepdims=True)

        first = lax.fori_loop(0, parts, take, jnp.zeros((1, width), jnp.float32))
        for i in range(parts):
            core_copy(i, send_p).wait_send()
        for j in range(8):
            terms[0, j : j + 1, :] = first[:, 128 * j : 128 * j + 128]
            terms[0, 8 + j : 9 + j, :] = term_two[:, 128 * j : 128 * j + 128]
        terms[0, 16:24, :] = jnp.broadcast_to(moment[...], (8, 128))

    pl.run_scoped(
        inner,
        pltpu.VMEM(wq.shape, half),
        pltpu.VMEM(wk.shape, half),
        pltpu.VMEM(wv.shape, half),
        pltpu.VMEM((rows, width), half),
        pltpu.VMEM((part, width), full),
        pltpu.VMEM((parts, part, width), full),
        pltpu.SemaphoreType.DMA((4,)),
        pltpu.SemaphoreType.DMA,
    )
    done = 12 + 2 * parts
    for stage in range(4):
        held = 2**stage
        exchange = pltpu.make_async_remote_copy(
            src_ref=terms.at[pl.ds(0, held)], dst_ref=terms.at[pl.ds(held, held)],
            send_sem=gsem.at[stage], recv_sem=jsem.at[stage], device_id=across(held), device_id_type=MESH,
        )
        exchange.start()
        tick(jnp.int32(done + stage))
        exchange.wait()
    rows_out[...] = terms[...]
    lax.fori_loop(done + 4, ITEMS + LAGS[3], lambda i, _: (tick(i), 0)[1], 0)

    def drain(i, _):
        @pl.when(i >= ITEMS - RING)
        def _():
            copy(i, 0).wait_send()

        for s in (2, 3):
            copy(i, s).wait_send()
        return 0

    lax.fori_loop(0, ITEMS, drain, 0)


def backward(names, length, term_two, moment, scale_one, *arrays):
    tokens = arrays[-2]
    rows, width = tokens.shape
    smem = pl.BlockSpec(memory_space=pltpu.SMEM)
    vmem = pl.BlockSpec(memory_space=pltpu.VMEM)
    hbm = pl.BlockSpec(memory_space=pl.ANY)
    half, full = jnp.bfloat16, jnp.float32
    return pl.pallas_call(
        functools.partial(backward_kernel, names),
        out_shape=[
            jax.ShapeDtypeStruct((ITEMS, 64, TILE), full),
            jax.ShapeDtypeStruct((rows, width), half),
            jax.ShapeDtypeStruct((16, 24, 128), full),
        ],
        in_specs=[smem] + [vmem] * 3 + [hbm] * len(arrays),
        out_specs=[vmem] * 3,
        scratch_shapes=[
            pltpu.VMEM((3, 16, 64, rows), half),
            pltpu.VMEM((RING, 8, 64, TILE), full),
            pltpu.VMEM((HELD, 8, 64, TILE), full),
            pltpu.VMEM((ITEMS, 4, 64, TILE), full),
            pltpu.VMEM((ITEMS, 2, 64, TILE), full),
            pltpu.VMEM((ITEMS, 1, 64, TILE), full),
            pltpu.VMEM((2, 2, rows, TILE), half),
            pltpu.VMEM((6, rows, TILE), half),
            pltpu.VMEM((rows // 256, 256, width), full),
            pltpu.VMEM((16, 24, 128), full),
            pltpu.SemaphoreType.DMA((3,)),
            pltpu.SemaphoreType.DMA((2, 2)),
            pltpu.SemaphoreType.DMA((4, ITEMS)),
            pltpu.SemaphoreType.DMA((4, ITEMS)),
            pltpu.SemaphoreType.DMA((4,)),
            pltpu.SemaphoreType.DMA((4,)),
            pltpu.SemaphoreType.DMA((4,)),
            pltpu.SemaphoreType.DMA((4,)),
            pltpu.SemaphoreType.REGULAR((3,)),
        ],
        compiler_params=pltpu.CompilerParams(
            collective_id=0, has_side_effects=True, vmem_limit_bytes=60 * 2**20
        ),
        name="backward",
    )(length, term_two, moment, scale_one, *arrays)


def both(part):
    return part + lax.ppermute(part, "tensor", [(0, 1), (1, 0)])


def fast_body(
    tokens,
    cotangent,
    lengths,
    noise_times,
    query_weight,
    key_weight,
    value_weight,
    merge_weight,
    up_weight,
    down_weight,
    first_scales,
    second_scales,
):
    tokens, cotangent = tokens[0], cotangent[0]
    rows, width = tokens.shape
    table_rows = first_scales.shape[0]
    chunks = lax.axis_size("dp")
    names = ("dp", "tensor")
    keep = (jnp.arange(rows, dtype=jnp.int32)[:, None] < lengths[0]).astype(jnp.float32)
    moment = noise_times[0]
    scale_one = lax.dynamic_slice_in_dim(first_scales, moment, 1, axis=0)
    scale_two = lax.dynamic_slice_in_dim(second_scales, moment, 1, axis=0)
    cosine, sine = (jnp.asarray(a) for a in rope_lanes(rows))
    normal_in, query, key, value, heads, heads_t, lse, hidden, normal_mid, activated, slope = forward(
        names, lengths, tokens, scale_one, scale_two, cosine, sine,
        query_weight, key_weight, value_weight, merge_weight, up_weight,
    )
    mlp_total = both(mm(activated, down_weight))
    layer_output = ((hidden + mlp_total) * keep).astype(jnp.bfloat16)
    grad_final = cotangent.astype(jnp.float32) * keep
    grad_mlp = grad_final.astype(jnp.bfloat16)
    grad_pre = (mm(grad_mlp, down_weight.T) * slope.astype(jnp.float32)).astype(jnp.bfloat16)
    grad_mid = both(mm(grad_pre, up_weight.T))
    normed_two, inv_two = normalize(hidden)
    grad_hat, term_two = norm_back(grad_mid[None], normed_two[None], inv_two[None], scale_two)
    grad_hidden = grad_final + grad_hat[0]
    grad_attn = grad_hidden.astype(jnp.bfloat16)
    chunked = lambda a: a.T.reshape(chunks, width // chunks, rows)
    pieces, grad_tokens, gathered = backward(
        names, lengths, term_two, jnp.full((1, 128), 1.0, jnp.float32) * moment.astype(jnp.float32), scale_one,
        chunked(grad_mlp), chunked(normal_mid), chunked(grad_attn), chunked(normal_in),
        activated, grad_pre, heads, query, key, value, heads_t, lse, cosine, sine,
        grad_attn, merge_weight, query_weight, key_weight, value_weight, tokens, grad_hidden,
    )
    wide = lambda a: a.transpose(1, 0, 2).reshape(width // chunks, -1)
    tall = lambda a: a.transpose(0, 2, 1).reshape(-1, width // chunks)
    grad_query, grad_key, grad_value = (wide(pieces[18 + k :: 3]) for k in range(3))
    hits = (gathered[:, 16, :1] == jnp.arange(table_rows, dtype=jnp.float32)[None, :]).astype(jnp.float32)
    mine = lax.axis_index("dp") * (width // chunks)
    terms = gathered[:, :16].reshape(chunks, 2, width)
    columns = lax.dynamic_slice_in_dim(terms, mine, width // chunks, axis=2).reshape(chunks, -1)
    tables = jnp.dot(hits.T, columns, precision=highest)
    grad_first, grad_second = jnp.split(tables, 2, axis=1)
    return (
        layer_output[None],
        grad_tokens[None],
        grad_query,
        grad_key,
        grad_value,
        tall(pieces[16:18]),
        wide(pieces[8:16]),
        tall(pieces[:8]),
        grad_first,
        grad_second,
    )


def body(
    tokens,
    cotangent,
    lengths,
    noise_times,
    query_weight,
    key_weight,
    value_weight,
    merge_weight,
    up_weight,
    down_weight,
    first_scales,
    second_scales,
):
    seq_count, length, width = tokens.shape
    local_width = query_weight.shape[1]
    local_heads = local_width // HEAD
    table_rows = first_scales.shape[0]
    flat_rows = seq_count * length
    scale_factor = 1.0 / math.sqrt(HEAD)
    block_rows = min(512, length)
    head_shape = (seq_count, length, local_heads, HEAD)
    row_mask = (jnp.arange(length, dtype=jnp.int32)[None, :] < lengths[:, None]).astype(jnp.float32)
    key_bias = (row_mask - 1.0) * 1000000000.0
    one_hot = (noise_times[:, None] == jnp.arange(table_rows, dtype=jnp.int32)[None, :]).astype(
        jnp.float32
    )
    scale_one = jnp.dot(one_hot, first_scales, precision=highest)
    scale_two = jnp.dot(one_hot, second_scales, precision=highest)
    cos_table, sin_table = rope_tables(length, HEAD)
    inputs = tokens.astype(jnp.float32) * row_mask[:, :, None]
    normed_one, inv_one = normalize(inputs)
    normal_in = (normed_one * scale_one[:, None, :]).astype(jnp.bfloat16).reshape(flat_rows, width)
    queries = jnp.dot(normal_in, query_weight, preferred_element_type=jnp.float32).reshape(
        head_shape
    )
    key_proj = jnp.dot(normal_in, key_weight, preferred_element_type=jnp.float32).reshape(
        head_shape
    )
    value_rows = (
        jnp.dot(normal_in, value_weight, preferred_element_type=jnp.float32)
        .astype(jnp.bfloat16)
        .reshape(head_shape)
    )
    query_rot = rotate(queries, cos_table, sin_table).astype(jnp.bfloat16)
    key_rot = rotate(key_proj, cos_table, sin_table).astype(jnp.bfloat16)
    attended = []
    log_sums = []
    for offset in range(0, length, block_rows):
        scores = block_scores(
            query_rot[:, offset : offset + block_rows], key_rot, key_bias, scale_factor
        )
        peak_score = jnp.max(scores, axis=-1, keepdims=True)
        exponent = jnp.exp(scores - peak_score)
        totals = jnp.sum(exponent, axis=-1, keepdims=True)
        soft_weights = (exponent / totals).astype(jnp.bfloat16)
        log_sums.append(peak_score + jnp.log(totals))
        attended.append(
            jnp.einsum(
                "shqk,skhd->sqhd", soft_weights, value_rows, preferred_element_type=jnp.float32
            )
        )
    heads_out = (
        jnp.concatenate(attended, axis=1).astype(jnp.bfloat16).reshape(flat_rows, local_width)
    )
    attn_part = jnp.dot(heads_out, merge_weight, preferred_element_type=jnp.float32)
    attn_total = lax.psum(attn_part, "tensor")
    hidden_one = inputs + attn_total.reshape(seq_count, length, width)
    normed_two, inv_two = normalize(hidden_one)
    normal_mid = (normed_two * scale_two[:, None, :]).astype(jnp.bfloat16).reshape(flat_rows, width)
    pre_act = jnp.dot(normal_mid, up_weight, preferred_element_type=jnp.float32)
    activated = gelu_tanh(pre_act).astype(jnp.bfloat16)
    mlp_part = jnp.dot(activated, down_weight, preferred_element_type=jnp.float32)
    mlp_total = lax.psum(mlp_part, "tensor")
    layer_output = (
        (hidden_one + mlp_total.reshape(seq_count, length, width)) * row_mask[:, :, None]
    ).astype(jnp.bfloat16)
    grad_final = cotangent.astype(jnp.float32) * row_mask[:, :, None]
    grad_mlp = grad_final.astype(jnp.bfloat16).reshape(flat_rows, width)
    grad_down = jnp.dot(activated.T, grad_mlp, preferred_element_type=jnp.float32)
    grad_act = jnp.dot(grad_mlp, down_weight.T, preferred_element_type=jnp.float32)
    unused_value, gelu_back = jax.vjp(gelu_tanh, pre_act)
    grad_pre = gelu_back(grad_act)[0].astype(jnp.bfloat16)
    grad_up = jnp.dot(normal_mid.T, grad_pre, preferred_element_type=jnp.float32)
    mid_part = jnp.dot(grad_pre, up_weight.T, preferred_element_type=jnp.float32)
    grad_mid = lax.psum(mid_part, "tensor").reshape(seq_count, length, width)
    grad_hat_two, scale_grad_two = norm_back(grad_mid, normed_two, inv_two, scale_two)
    grad_hidden = grad_final + grad_hat_two
    grad_second = jnp.dot(one_hot.T, scale_grad_two, precision=highest)
    grad_attn = grad_hidden.astype(jnp.bfloat16).reshape(flat_rows, width)
    grad_merge = jnp.dot(heads_out.T, grad_attn, preferred_element_type=jnp.float32)
    grad_heads = (
        jnp.dot(grad_attn, merge_weight.T, preferred_element_type=jnp.float32)
        .astype(jnp.bfloat16)
        .reshape(head_shape)
    )
    grad_keys = jnp.zeros(head_shape, jnp.float32)
    grad_values = jnp.zeros(head_shape, jnp.float32)
    query_grads = []
    for block_index in range(len(log_sums)):
        offset = block_index * block_rows
        query_block = query_rot[:, offset : offset + block_rows]
        grad_block = grad_heads[:, offset : offset + block_rows]
        scores = block_scores(query_block, key_rot, key_bias, scale_factor)
        soft_weights = jnp.exp(scores - log_sums[block_index])
        grad_soft = jnp.einsum(
            "sqhd,skhd->shqk", grad_block, value_rows, preferred_element_type=jnp.float32
        )
        grad_values = grad_values + jnp.einsum(
            "shqk,sqhd->skhd",
            soft_weights.astype(jnp.bfloat16),
            grad_block,
            preferred_element_type=jnp.float32,
        )
        grad_scores = (
            soft_weights * (grad_soft - jnp.sum(soft_weights * grad_soft, axis=-1, keepdims=True))
        ).astype(jnp.bfloat16)
        query_grads.append(
            jnp.einsum("shqk,skhd->sqhd", grad_scores, key_rot, preferred_element_type=jnp.float32)
            * scale_factor
        )
        grad_keys = (
            grad_keys
            + jnp.einsum(
                "shqk,sqhd->skhd", grad_scores, query_block, preferred_element_type=jnp.float32
            )
            * scale_factor
        )
    query_back = (
        unrotate(jnp.concatenate(query_grads, axis=1), cos_table, sin_table)
        .astype(jnp.bfloat16)
        .reshape(flat_rows, local_width)
    )
    key_back = (
        unrotate(grad_keys, cos_table, sin_table)
        .astype(jnp.bfloat16)
        .reshape(flat_rows, local_width)
    )
    value_back = grad_values.astype(jnp.bfloat16).reshape(flat_rows, local_width)
    grad_query = jnp.dot(normal_in.T, query_back, preferred_element_type=jnp.float32)
    grad_key = jnp.dot(normal_in.T, key_back, preferred_element_type=jnp.float32)
    grad_value = jnp.dot(normal_in.T, value_back, preferred_element_type=jnp.float32)
    inner_part = jnp.dot(query_back, query_weight.T, preferred_element_type=jnp.float32)
    inner_part = inner_part + jnp.dot(key_back, key_weight.T, preferred_element_type=jnp.float32)
    inner_part = inner_part + jnp.dot(
        value_back, value_weight.T, preferred_element_type=jnp.float32
    )
    grad_inner = lax.psum(inner_part, "tensor").reshape(seq_count, length, width)
    grad_hat_one, scale_grad_one = norm_back(grad_inner, normed_one, inv_one, scale_one)
    grad_tokens = ((grad_hidden + grad_hat_one) * row_mask[:, :, None]).astype(jnp.bfloat16)
    grad_first = jnp.dot(one_hot.T, scale_grad_one, precision=highest)
    summed = (
        lax.psum_scatter(grad_query, "dp", scatter_dimension=0, tiled=True),
        lax.psum_scatter(grad_key, "dp", scatter_dimension=0, tiled=True),
        lax.psum_scatter(grad_value, "dp", scatter_dimension=0, tiled=True),
        lax.psum_scatter(grad_merge, "dp", scatter_dimension=1, tiled=True),
        lax.psum_scatter(grad_up, "dp", scatter_dimension=0, tiled=True),
        lax.psum_scatter(grad_down, "dp", scatter_dimension=1, tiled=True),
        lax.psum_scatter(grad_first, "dp", scatter_dimension=1, tiled=True),
        lax.psum_scatter(grad_second, "dp", scatter_dimension=1, tiled=True),
    )
    return (
        layer_output,
        grad_tokens,
        summed[0],
        summed[1],
        summed[2],
        summed[3],
        summed[4],
        summed[5],
        summed[6],
        summed[7],
    )


def solution(mesh):
    fast = mesh.shape["dp"] == 16 and mesh.shape["tensor"] == 2
    return jax.shard_map(
        fast_body if fast else body,
        mesh=mesh,
        in_specs=(
            P("dp", None, None),
            P("dp", None, None),
            P("dp"),
            P("dp"),
            P(None, "tensor"),
            P(None, "tensor"),
            P(None, "tensor"),
            P("tensor", None),
            P(None, "tensor"),
            P("tensor", None),
            P(),
            P(),
        ),
        out_specs=(
            P("dp", None, None),
            P("dp", None, None),
            P("dp", "tensor"),
            P("dp", "tensor"),
            P("dp", "tensor"),
            P("tensor", "dp"),
            P("dp", "tensor"),
            P("tensor", "dp"),
            P(None, "dp"),
            P(None, "dp"),
        ),
        check_vma=False,
    )
```

```python
import functools
import math

import jax
import jax.numpy as jnp
import numpy as np
from jax import lax
from jax.experimental import pallas as pl
from jax.experimental.pallas import tpu as pltpu
from jax.sharding import PartitionSpec as P

HEAD = 64
MESH = pl.DeviceIdType.MESH


epsilon = 1e-05
highest = lax.Precision.HIGHEST


def gelu_tanh(values):
    return (
        0.5
        * values
        * (1.0 + jnp.tanh(0.7978845608028654 * (values + 0.044715 * values * values * values)))
    )


def rope_tables(length, head_size):
    halves = head_size // 2
    places = jnp.arange(length, dtype=jnp.float32)[:, None]
    frequency = jnp.exp(
        jnp.arange(halves, dtype=jnp.float32) * (-2.0 * math.log(10000.0) / head_size)
    )
    angles = places * frequency[None, :]
    return (jnp.cos(angles), jnp.sin(angles))


def rotate(values, cos_table, sin_table):
    halves = values.shape[-1] // 2
    first_half = values[..., :halves]
    second_half = values[..., halves:]
    cosine = cos_table[:, None, :]
    sine_part = sin_table[:, None, :]
    return jnp.concatenate(
        [
            first_half * cosine - second_half * sine_part,
            second_half * cosine + first_half * sine_part,
        ],
        axis=-1,
    )


def unrotate(gradient, cos_table, sin_table):
    halves = gradient.shape[-1] // 2
    first_half = gradient[..., :halves]
    second_half = gradient[..., halves:]
    cosine = cos_table[:, None, :]
    sine_part = sin_table[:, None, :]
    return jnp.concatenate(
        [
            first_half * cosine + second_half * sine_part,
            second_half * cosine - first_half * sine_part,
        ],
        axis=-1,
    )


def normalize(values):
    centred = values - jnp.mean(values, axis=-1, keepdims=True)
    inv_std = lax.rsqrt(jnp.mean(centred * centred, axis=-1, keepdims=True) + epsilon)
    return (centred * inv_std, inv_std)


def norm_back(grad_norm, normed, inv_std, scale_rows):
    grad_hat = grad_norm * scale_rows[:, None, :]
    grad_scale = jnp.sum(grad_norm * normed, axis=1)
    mean_grad = jnp.mean(grad_hat, axis=-1, keepdims=True)
    mean_cross = jnp.mean(grad_hat * normed, axis=-1, keepdims=True)
    return (inv_std * (grad_hat - mean_grad - normed * mean_cross), grad_scale)


def block_scores(query_block, key_rot, key_bias, scale_factor):
    scores = jnp.einsum("sqhd,skhd->shqk", query_block, key_rot, preferred_element_type=jnp.float32)
    return scores * scale_factor + key_bias[:, None, None, :]


def rope_lanes(length):
    halves = HEAD // 2
    places = np.arange(length, dtype=np.float64)[:, None]
    frequency = np.exp(np.arange(halves) * (-2.0 * math.log(10000.0) / HEAD))
    angles = places * frequency[None, :]
    cosine, sine = np.cos(angles), np.sin(angles)
    return (
        np.concatenate([cosine] * 4, axis=1).astype(np.float32),
        np.concatenate([-sine, sine] * 2, axis=1).astype(np.float32),
    )


def swap_halves(values):
    lanes = lax.broadcasted_iota(jnp.int32, values.shape, 1)
    first = lax.rem(lanes, HEAD) < HEAD // 2
    half = HEAD // 2
    return jnp.where(first, pltpu.roll(values, 128 - half, 1), pltpu.roll(values, half, 1))


def centre(values):
    middle = jnp.mean(values, axis=1, keepdims=True)
    centred = values - middle
    inverse = lax.rsqrt(jnp.mean(centred * centred, axis=1, keepdims=True) + epsilon)
    return centred * inverse


NT = (((1,), (1,)), ((), ()))


def mm(a, b):
    return jnp.dot(a, b, preferred_element_type=jnp.float32)


def mm_nt(a, b):
    return lax.dot_general(a, b, NT, preferred_element_type=jnp.float32)


def forward_kernel(
    names, length_ref, tokens, cotangent, scale_one, scale_two, cosine, sine, wq, wk, wv, wm, wu,
    q_out, k_out, v_out, heads, heads_t, lse, hidden, act, slope, mlp_t,
    nin, vq, vk, vv, vm, vu, other_m, v_t, send_m, recv_m, send_o, recv_o, bias, wsem, ssem, rsem,
):
    rows, width = tokens.shape
    pairs = q_out.shape[0]
    here = {n: lax.axis_index(n) for n in names}
    other = {**here, names[1]: 1 - here[names[1]]}
    other = tuple(other[n] for n in names)
    loads = [
        pltpu.make_async_copy(a, b, wsem.at[i])
        for i, (a, b) in enumerate(((wq, vq), (wk, vk), (wv, vv), (wm, vm), (wu, vu)))
    ]
    for c in loads:
        c.start()
    barrier = pltpu.get_barrier_semaphore()
    pl.semaphore_signal(barrier, inc=1, device_id=other, device_id_type=MESH)
    pl.semaphore_wait(barrier, 1)
    length = length_ref[0]

    def place(start, count):
        return start + lax.broadcasted_iota(jnp.int32, (count, 1), 0)

    def mask_of(start, count):
        return jnp.where(place(start, count) < length, 1.0, 0.0)

    bias[...] = jnp.broadcast_to((mask_of(0, rows) - 1.0) * 1000000000.0, (rows, 128))

    def norm_rows(i, _):
        at = pl.multiple_of(i * 128, 128)
        x = tokens[pl.ds(at, 128), :].astype(jnp.float32) * mask_of(at, 128)
        nin[pl.ds(at, 128), :] = (centre(x) * scale_one[...]).astype(jnp.bfloat16)
        return 0

    lax.fori_loop(0, rows // 128, norm_rows, 0)
    for c in loads[:4]:
        c.wait()
    send_m[...] = vm[...].astype(jnp.float32)
    merge_copy = pltpu.make_async_remote_copy(
        src_ref=send_m, dst_ref=recv_m, send_sem=ssem.at[0], recv_sem=rsem.at[0],
        device_id=other, device_id_type=MESH,
    )
    merge_copy.start()

    def project(i, _):
        at = pl.multiple_of(i * 256, 256)
        own = pl.ds(at, 256)
        x = nin[own, :]
        c, s = cosine[own, :], sine[own, :]
        for ref, w in ((q_out, vq), (k_out, vk)):
            y = mm(x, w[...])
            for p in range(pairs):
                part = y[:, 128 * p : 128 * p + 128]
                ref[p, own, :] = (part * c + swap_halves(part) * s).astype(jnp.bfloat16)
        y = mm(x, vv[...])
        for p in range(pairs):
            part = y[:, 128 * p : 128 * p + 128]
            v_out[p, own, :] = part.astype(jnp.bfloat16)
            v_t[p, :, own] = part.T.astype(jnp.bfloat16)
        return 0

    lax.fori_loop(0, rows // 256, project, 0)

    def o_copy(p):
        return pltpu.make_async_remote_copy(
            src_ref=send_o.at[p], dst_ref=recv_o.at[p], send_sem=ssem.at[1 + p], recv_sem=rsem.at[1 + p],
            device_id=other, device_id_type=MESH,
        )

    lane = lax.broadcasted_iota(jnp.int32, (rows, 128), 1)
    block = 512

    def attend(p, _):
        for h in range(2):
            keys = jnp.where((lane < HEAD) == (h == 0), k_out[p] * 0.125, 0.0).astype(jnp.bfloat16)
            values_t = v_t[p, pl.ds(HEAD * h, HEAD), :]
            for b in range(rows // block):
                cols = pl.ds(b * block, block)
                s = mm_nt(keys, q_out[p, cols, :]) + bias[:, :1]
                peak = jnp.max(s, axis=0, keepdims=True)
                e = jnp.exp(s - peak)
                total = jnp.sum(e, axis=0, keepdims=True)
                o = mm(values_t, e.astype(jnp.bfloat16)) / total
                heads_t[p, pl.ds(HEAD * h, HEAD), cols] = o.astype(jnp.bfloat16)
                lse[pl.ds(2 * p + h, 1), cols] = peak + jnp.log(total)
        o = heads_t[p].astype(jnp.float32).T
        send_o[p] = o
        heads[p] = o.astype(jnp.bfloat16)
        o_copy(p).start()
        count = rows // pairs
        at = pl.multiple_of(p * count, count)
        turned = (cotangent[pl.ds(at, count), :].astype(jnp.float32) * mask_of(at, count)).T
        mlp_t[:, :, pl.ds(at, count)] = turned.astype(jnp.bfloat16).reshape(mlp_t.shape[0], mlp_t.shape[1], count)
        return 0

    lax.fori_loop(0, pairs, attend, 0)
    merge_copy.wait()
    other_m[...] = recv_m[...].astype(jnp.bfloat16)
    for p in range(pairs):
        o_copy(p).wait()
    loads[4].wait()

    def finish(i, _):
        at = pl.multiple_of(i * 256, 256)
        own = pl.ds(at, 256)
        mine = jnp.concatenate([heads[p, own, :] for p in range(pairs)], axis=1)
        theirs = jnp.concatenate([recv_o[p, own, :].astype(jnp.bfloat16) for p in range(pairs)], axis=1)
        attn = mm(mine, vm[...]) + mm(theirs, other_m[...])
        one = tokens[own, :].astype(jnp.float32) * mask_of(at, 256) + attn
        hidden[own, :] = one
        normal = (centre(one) * scale_two[...]).astype(jnp.bfloat16)
        for j in range(0, vu.shape[1], 512):
            v = mm(normal, vu[:, j : j + 512])
            square = v * v
            t = jnp.tanh(0.7978845608028654 * v * (1.0 + 0.044715 * square))
            up = 0.5 * (1.0 + t)
            act[own, j : j + 512] = (v * up).astype(jnp.bfloat16)
            slope[own, j : j + 512] = (
                up + 0.5 * v * (1.0 - t * t) * (0.7978845608028654 * (1.0 + 0.134145 * square))
            ).astype(jnp.bfloat16)
        return 0

    lax.fori_loop(0, rows // 256, finish, 0)


def forward(names, length, tokens, cotangent, scale_one, scale_two, cosine, sine, wq, wk, wv, wm, wu):
    rows, width = tokens.shape
    local, units = wq.shape[1], wu.shape[1]
    pairs = local // 128
    vmem = pl.BlockSpec(memory_space=pltpu.VMEM)
    hbm = pl.BlockSpec(memory_space=pl.ANY)
    half = jnp.bfloat16
    full = jnp.float32
    shapes = [
        ((pairs, rows, 128), half),
        ((pairs, rows, 128), half),
        ((pairs, rows, 128), half),
        ((pairs, rows, 128), half),
        ((pairs, 128, rows), half),
        ((2 * pairs, rows), full),
        ((rows, width), full),
        ((rows, units), half),
        ((rows, units), half),
        ((16, width // 16, rows), half),
    ]
    return pl.pallas_call(
        functools.partial(forward_kernel, names),
        out_shape=[jax.ShapeDtypeStruct(*s) for s in shapes],
        in_specs=[pl.BlockSpec(memory_space=pltpu.SMEM)] + [vmem] * 6 + [hbm] * 5,
        out_specs=[vmem] * len(shapes),
        scratch_shapes=[
            pltpu.VMEM((rows, width), half),
            pltpu.VMEM(wq.shape, half),
            pltpu.VMEM(wk.shape, half),
            pltpu.VMEM(wv.shape, half),
            pltpu.VMEM(wm.shape, half),
            pltpu.VMEM(wu.shape, half),
            pltpu.VMEM(wm.shape, half),
            pltpu.VMEM((pairs, 128, rows), half),
            pltpu.VMEM(wm.shape, full),
            pltpu.VMEM(wm.shape, full),
            pltpu.VMEM((pairs, rows, 128), full),
            pltpu.VMEM((pairs, rows, 128), full),
            pltpu.VMEM((rows, 128), full),
            pltpu.SemaphoreType.DMA((5,)),
            pltpu.SemaphoreType.DMA((1 + pairs,)),
            pltpu.SemaphoreType.DMA((1 + pairs,)),
        ],
        compiler_params=pltpu.CompilerParams(collective_id=1, has_side_effects=True, vmem_limit_bytes=58 * 2**20),
        name="forward",
    )(length, tokens, cotangent, scale_one, scale_two, cosine, sine, wq, wk, wv, wm, wu)


ITEMS = 24
TILE = 256
RING = 5
HELD = 12
LAGS = (4, 7, 9, 11)
FIRSTS = (0, 8, 16, 18, 24)


def count_from(i, starts):
    total = 0
    for start in starts:
        total = total + jnp.where(i >= start, 1, 0)
    return total


def flip(index, weight):
    return index + weight * (1 - 2 * lax.rem(lax.div(index, weight), 2))


def weight_of(color, stage):
    k = lax.rem(color + stage, 3)
    return 1 + (k * (k + 1)) // 2


def color_of(i):
    return lax.rem(lax.rem(i, 8), 3)


def slot_of(i):
    return count_from(i, (8, 16)) - 2 * count_from(i, (18,))


def backward_kernel(
    names, length_ref, moment, scale_one, scale_two,
    l_down, r_down, heads, q_in, k_in, v_in, heads_t, lse_in, cosine, sine,
    merge_in, wq, wk, wv, tokens, hidden, slope, cotangent, wu, wd,
    out, rows_out, tokens_out, layer_out, r_up, hidden_grad,
    left, s1, r1, r2, r3, r4, rb, qkv, send_p, recv_p, ga, terms,
    lsem, fsem, ssem, csem, psem, qsem, gsem, jsem, credit, credit_two, core_free,
):
    here = {n: lax.axis_index(n) for n in names}
    d = here[names[0]]

    def device(**moved):
        at = {**here, **moved}
        return tuple(at[n] for n in names)

    core = device(**{names[1]: 1 - here[names[1]]})

    def across(weight):
        return device(**{names[0]: flip(d, weight)})

    def absolute(r):
        total = 0
        for b in range(4):
            bit = lax.rem(lax.div(d, 2**b), 2)
            total = total + (2**b) * (1 - bit if (r >> b) & 1 else bit)
        return total

    def load_left(source, slot):
        for r in range(16):
            pltpu.make_async_copy(source.at[absolute(r)], left.at[slot, r], lsem).start()

    def left_loaded(slot):
        pltpu.make_async_copy(left.at[slot], left.at[slot], lsem).wait()

    def turn(values, slot, own):
        turned = values.T.astype(jnp.bfloat16)
        for c in range(16):
            left[slot, absolute(c), :, own] = turned[64 * c : 64 * c + 64]

    load_left(l_down, 0)
    barrier = pltpu.get_barrier_semaphore()
    for weight in (1, 2, 4, 8):
        pl.semaphore_signal(barrier, inc=1, device_id=across(weight), device_id_type=MESH)
    pl.semaphore_signal(barrier, inc=1, device_id=core, device_id_type=MESH)
    pl.semaphore_wait(barrier, 5)

    def fetch(i, lane):
        slot = lax.rem(i, 2)
        target, sem = rb.at[lane, slot], fsem.at[lane, slot]
        for g, source in ((0, r_down), (1, r_up)):
            @pl.when((i >= FIRSTS[g]) & (i < FIRSTS[g + 1]))
            def _():
                col = pl.multiple_of((i - FIRSTS[g]) * TILE, TILE)
                pltpu.make_async_copy(source.at[:, pl.ds(col, TILE)], target, sem).start()

        @pl.when((i >= FIRSTS[2]) & (i < FIRSTS[3]))
        def _():
            for k in range(2):
                pltpu.make_async_copy(
                    heads.at[2 * (i - FIRSTS[2]) + k], target.at[:, pl.ds(128 * k, 128)], sem
                ).start()

        @pl.when(i >= FIRSTS[3])
        def _():
            pltpu.make_async_copy(qkv.at[i - FIRSTS[3]], target, sem).start()

    def fetched(i, lane):
        slot = lax.rem(i, 2)
        pltpu.make_async_copy(rb.at[lane, slot], rb.at[lane, slot], fsem.at[lane, slot]).wait()

    def product(i, first, lane):
        color, slot = color_of(i), slot_of(i)
        weights = [weight_of(color, s) for s in range(3)] + [8]
        rows = []
        for bits in range(8):
            r = first * weights[0] + sum(((bits >> (2 - k)) & 1) * weights[1 + k] for k in range(3))
            rows.append(left[slot, r])
        lhs = jnp.concatenate(rows, axis=0)
        return mm(lhs, rb[lane, lax.rem(i, 2)]).reshape(8, 64, TILE)

    def copy(i, s):
        weight = weight_of(color_of(i), s) if s < 3 else 8
        src = (s1.at[lax.rem(i, RING)], r1.at[lax.rem(i, HELD), pl.ds(4, 4)], r2.at[lax.rem(i, HELD), pl.ds(2, 2)], r3.at[i, pl.ds(1, 1)])[s]
        dst = (r1.at[lax.rem(i, HELD)], r2.at[lax.rem(i, HELD)], r3.at[i], r4.at[i])[s]
        return pltpu.make_async_remote_copy(
            src_ref=src, dst_ref=dst, send_sem=ssem.at[s, i], recv_sem=csem.at[s, i],
            device_id=across(weight), device_id_type=MESH,
        )

    def tick(i):
        @pl.when(i < ITEMS)
        def _():
            @pl.when(i >= RING)
            def _():
                copy(i - RING, 0).wait_send()

            fetched(i, 0)
            s1[lax.rem(i, RING)] = product(i, 1, 0)

            @pl.when(i >= HELD)
            def _():
                pl.semaphore_wait(credit.at[color_of(i)], 1)

            copy(i, 0).start()

            @pl.when((i + 2 < ITEMS))
            def _():
                fetch(i + 2, 0)

        a = i - LAGS[0]

        @pl.when((a >= 0) & (a < ITEMS))
        def _():
            fetched(a, 1)
            copy(a, 0).wait_recv()
            r1[lax.rem(a, HELD)] += product(a, 0, 1)

            @pl.when(a >= HELD)
            def _():
                pl.semaphore_wait(credit_two.at[color_of(a)], 1)

            copy(a, 1).start()

            @pl.when(a + 2 < ITEMS)
            def _():
                fetch(a + 2, 1)

        b = i - LAGS[1]

        @pl.when((b >= 0) & (b < ITEMS))
        def _():
            copy(b, 1).wait_recv()
            r2[lax.rem(b, HELD)] += r1[lax.rem(b, HELD), 0:4]
            copy(b, 2).start()
            copy(b, 1).wait_send()

            @pl.when(b + HELD < ITEMS)
            def _():
                color = color_of(b + HELD)
                pl.semaphore_signal(
                    credit.at[color], inc=1, device_id=across(weight_of(color, 0)), device_id_type=MESH
                )

        c = i - LAGS[2]

        @pl.when((c >= 0) & (c < ITEMS))
        def _():
            copy(c, 2).wait_recv()
            r3[c] += r2[lax.rem(c, HELD), 0:2]
            copy(c, 3).start()
            copy(c, 2).wait_send()

            @pl.when(c + HELD < ITEMS)
            def _():
                color = color_of(c + HELD)
                pl.semaphore_signal(
                    credit_two.at[color], inc=1, device_id=across(weight_of(color, 1)), device_id_type=MESH
                )

        e = i - LAGS[3]

        @pl.when((e >= 0) & (e < ITEMS))
        def _():
            copy(e, 3).wait_recv()
            out[e] = r4[e, 0] + r3[e, 0]

    for lane in range(2):
        fetch(jnp.int32(0), lane)
        fetch(jnp.int32(1), lane)
    rows, width = tokens.shape
    pairs = q_in.shape[0]
    length = length_ref[0]
    part = 256
    parts = rows // part
    half, full = jnp.bfloat16, jnp.float32

    def keep_of(at):
        return jnp.where(at + lax.broadcasted_iota(jnp.int32, (part, 1), 0) < length, 1.0, 0.0)

    def core_copy(use, i):
        return pltpu.make_async_remote_copy(
            src_ref=send_p.at[i], dst_ref=recv_p.at[i], send_sem=psem.at[use, i], recv_sem=qsem.at[use, i],
            device_id=core, device_id_type=MESH,
        )

    def core_sent(use):
        for i in range(parts):
            core_copy(use, i).wait_send()
        if use < 2:
            pl.semaphore_signal(core_free, inc=1, device_id=core, device_id_type=MESH)
            pl.semaphore_wait(core_free, 1)

    def norm_parts(values):
        centred = values - jnp.mean(values, axis=1, keepdims=True)
        inverse = lax.rsqrt(jnp.mean(centred * centred, axis=1, keepdims=True) + epsilon)
        return centred * inverse, inverse

    def norm_grad(grad, normed, inverse, scale):
        hat = grad * scale
        middle = jnp.mean(hat, axis=1, keepdims=True)
        return inverse * (hat - middle - normed * jnp.mean(hat * normed, axis=1, keepdims=True))

    def run_ticks(first, last):
        lax.fori_loop(first, last, lambda i, _: (tick(i), 0)[1], 0)

    def mlp(vu, vd, cot, wide, hid, gp, gh, wsem, tsem, osem):
        loads = [pltpu.make_async_copy(a, b, wsem.at[n]) for n, (a, b) in enumerate(((wd, vd), (wu, vu)))]
        for x in loads:
            x.start()

        def tile(source, target, n, i):
            own = pl.ds(pl.multiple_of(i * part, part), part)
            slot = lax.rem(i, 2)
            return pltpu.make_async_copy(source.at[own, :], target.at[slot], tsem.at[n, slot])

        def stream(sources, i, body):
            for n, source, target in sources:
                tile(source, target, n, i).wait()

                @pl.when(i + 1 < parts)
                def _():
                    tile(source, target, n, i + 1).start()

            return body(i, pl.multiple_of(i * part, part), lax.rem(i, 2))

        def begin(sources):
            for n, source, target in sources:
                tile(source, target, n, jnp.int32(0)).start()

        streams = ((0, cotangent, cot), (1, slope, wide))
        begin(streams)
        left_loaded(0)
        run_ticks(0, 4)
        for x in loads:
            x.wait()

        def store_pre(i):
            own = pl.ds(pl.multiple_of(i * part, part), part)
            return pltpu.make_async_copy(gp, r_up.at[own, :], osem.at[0])

        def first(i, at, slot):
            x = (cot[slot].astype(full) * keep_of(at)).astype(half)
            g = mm_nt(x, vd[...]) * wide[slot].astype(full)

            @pl.when(i > 0)
            def _():
                store_pre(i - 1).wait()

            gp[...] = g.astype(half)
            store_pre(i).start()
            send_p[i] = mm_nt(gp[...], vu[...])
            core_copy(0, i).start()

            @pl.when(lax.rem(i, 2) == 1)
            def _():
                tick(4 + lax.div(i, 2))

            return 0

        lax.fori_loop(0, parts, lambda i, _: stream(streams, i, first), 0)
        store_pre(parts - 1).wait()
        streams_two = ((0, cotangent, cot), (2, hidden, hid))
        begin(streams_two)

        def store_hidden(i):
            own = pl.ds(pl.multiple_of(i * part, part), part)
            return pltpu.make_async_copy(gh, hidden_grad.at[own, :], osem.at[1])

        def second(i, at, slot, total):
            own = pl.ds(at, part)
            normed, inverse = norm_parts(hid[slot])
            turn(normed * scale_two[...], 1, own)
            core_copy(0, i).wait_recv()
            grad = send_p[i] + recv_p[i]

            @pl.when(i > 0)
            def _():
                store_hidden(i - 1).wait()

            gh[...] = cot[slot].astype(full) * keep_of(at) + norm_grad(grad, normed, inverse, scale_two[...])
            store_hidden(i).start()
            ga[own, :] = gh[...].astype(half)
            turn(gh[...], 2, own)
            return total + jnp.sum(grad * normed, axis=0, keepdims=True)

        term = lax.fori_loop(
            0, parts, lambda i, total: stream(streams_two, i, functools.partial(second, total=total)),
            jnp.zeros((1, width), full),
        )
        for j in range(8):
            terms[0, 8 + j : 9 + j, :] = term[:, 128 * j : 128 * j + 128]
        store_hidden(parts - 1).wait()
        core_sent(0)
        tick(jnp.int32(6))
        streams_three = ((1, r_down, wide),)
        begin(streams_three)

        def third(i, at, slot):
            send_p[i] = mm(wide[slot], vd[...])
            core_copy(1, i).start()
            return 0

        lax.fori_loop(0, parts, lambda i, _: stream(streams_three, i, third), 0)
        streams_four = ((2, hidden, hid),)
        begin(streams_four)
        tick(jnp.int32(7))

        def store_layer(i):
            own = pl.ds(pl.multiple_of(i * part, part), part)
            return pltpu.make_async_copy(cot.at[0], layer_out.at[own, :], osem.at[0])

        def fourth(i, at, slot):
            core_copy(1, i).wait_recv()

            @pl.when(i > 0)
            def _():
                store_layer(i - 1).wait()

            cot[0] = ((hid[slot] + (send_p[i] + recv_p[i])) * keep_of(at)).astype(half)
            store_layer(i).start()
            return 0

        lax.fori_loop(0, parts, lambda i, _: stream(streams_four, i, fourth), 0)
        store_layer(parts - 1).wait()
        core_sent(1)

    pl.run_scoped(
        mlp,
        pltpu.VMEM(wu.shape, half),
        pltpu.VMEM(wd.shape, half),
        pltpu.VMEM((2, part, width), half),
        pltpu.VMEM((2, part, slope.shape[1]), half),
        pltpu.VMEM((2, part, width), full),
        pltpu.VMEM((part, slope.shape[1]), half),
        pltpu.VMEM((part, width), full),
        pltpu.SemaphoreType.DMA((2,)),
        pltpu.SemaphoreType.DMA((3, 2)),
        pltpu.SemaphoreType.DMA((2,)),
    )

    def attention(q, k, v, o_t, lse, wm, cos, sin, bias, do, do_t, kh, vh, k_t, dq_t, asem):
        loads = [
            pltpu.make_async_copy(a, b, asem.at[n])
            for n, (a, b) in enumerate(
                ((q_in, q), (k_in, k), (v_in, v), (heads_t, o_t), (lse_in, lse), (merge_in, wm),
                 (cosine, cos), (sine, sin))
            )
        ]
        for x in loads:
            x.start()
        for x in loads:
            x.wait()
        place = lax.broadcasted_iota(jnp.int32, (rows, 128), 0)
        bias[...] = (jnp.where(place < length, 1.0, 0.0) - 1.0) * 1000000000.0
        lane = lax.broadcasted_iota(jnp.int32, (rows, 128), 1) < HEAD
        block = 256

        def unrotate_lanes(y):
            return (y * cos[...] - swap_halves(y) * sin[...]).astype(jnp.bfloat16)

        def pair(p, _):
            weight = wm[pl.ds(pl.multiple_of(128 * p, 128), 128), :]
            do[...] = mm_nt(ga[...], weight).astype(jnp.bfloat16)
            do_t[...] = mm_nt(weight, ga[...]).astype(jnp.bfloat16)
            k_t[...] = (k[p].astype(jnp.float32) * 0.125).T.astype(jnp.bfloat16)
            product_t = do_t[...].astype(jnp.float32) * o_t[p].astype(jnp.float32)
            dks, dvs = [], []
            for h in range(2):
                tick(8 + 2 * p + h)
                delta = jnp.sum(product_t[HEAD * h : HEAD * h + HEAD], axis=0, keepdims=True)
                own = lane == (h == 0)
                kh[...] = jnp.where(own, k[p].astype(jnp.float32) * 0.125, 0.0).astype(jnp.bfloat16)
                vh[...] = jnp.where(own, v[p].astype(jnp.float32), 0.0).astype(jnp.bfloat16)
                dk = jnp.zeros((rows, 128), jnp.float32)
                dv = jnp.zeros((rows, 128), jnp.float32)
                for b in range(0, rows, block):
                    cols = slice(b, b + block)
                    qb = q[p, cols, :]
                    s = mm_nt(kh[...], qb) + bias[:, :1]
                    soft = jnp.exp(s - lse[pl.ds(2 * p + h, 1), cols])
                    ds = soft * (mm(vh[...], do_t[:, cols]) - delta[:, cols])
                    ds = ds.astype(jnp.bfloat16)
                    dv = dv + mm(soft.astype(jnp.bfloat16), do[cols, :])
                    dk = dk + mm(ds, qb)
                    dq_t[HEAD * h : HEAD * h + HEAD, cols] = mm(k_t[HEAD * h : HEAD * h + HEAD, :], ds)
                dks.append(dk)
                dvs.append(dv)
            quad = 3 * lax.div(p, 2)
            at = pl.ds(pl.multiple_of(128 * lax.rem(p, 2), 128), 128)
            qkv[quad, :, at] = unrotate_lanes(dq_t[...].T)
            qkv[quad + 1, :, at] = unrotate_lanes(jnp.where(lane, dks[0], dks[1]) * 0.125)
            qkv[quad + 2, :, at] = jnp.where(lane, dvs[0], dvs[1]).astype(jnp.bfloat16)
            return 0

        lax.fori_loop(0, pairs, pair, 0)

    pl.run_scoped(
        attention,
        pltpu.VMEM((pairs, rows, 128), half),
        pltpu.VMEM((pairs, rows, 128), half),
        pltpu.VMEM((pairs, rows, 128), half),
        pltpu.VMEM((pairs, 128, rows), half),
        pltpu.VMEM((2 * pairs, rows), full),
        pltpu.VMEM(merge_in.shape, half),
        pltpu.VMEM((rows, 128), full),
        pltpu.VMEM((rows, 128), full),
        pltpu.VMEM((rows, 128), full),
        pltpu.VMEM((rows, 128), half),
        pltpu.VMEM((128, rows), half),
        pltpu.VMEM((rows, 128), half),
        pltpu.VMEM((rows, 128), half),
        pltpu.VMEM((128, rows), half),
        pltpu.VMEM((128, rows), full),
        pltpu.SemaphoreType.DMA((10,)),
    )

    def inner(vq, vk, vv, x_in, gh, to, sem, hsem, osem):
        loads = [
            pltpu.make_async_copy(a, b, sem.at[n])
            for n, (a, b) in enumerate(((wq, vq), (wk, vk), (wv, vv), (tokens, x_in)))
        ]
        for x in loads:
            x.start()
        for x in loads:
            x.wait()

        def send(i, _):
            at = pl.multiple_of(i * part, part)
            own = pl.ds(at, part)
            total = None
            for quad in range(2):
                for n, w in enumerate((vq, vk, vv)):
                    term = mm_nt(qkv[3 * quad + n, own, :], w[:, TILE * quad : TILE * quad + TILE])
                    total = term if total is None else total + term
            send_p[i] = total
            core_copy(2, i).start()
            normed, _ = norm_parts(x_in[own, :].astype(full) * keep_of(at))
            turn(normed * scale_one[...], 0, own)

            @pl.when(lax.rem(i, 2) == 1)
            def _():
                tick(16 + lax.div(i, 2))

            return 0

        lax.fori_loop(0, parts, send, 0)

        def store_tokens(i):
            own = pl.ds(pl.multiple_of(i * part, part), part)
            return pltpu.make_async_copy(to, tokens_out.at[own, :], osem)

        def take(i, total):
            at = pl.multiple_of(i * part, part)
            own = pl.ds(at, part)
            hidden_copy = pltpu.make_async_copy(hidden_grad.at[own, :], gh, hsem)
            hidden_copy.start()
            core_copy(2, i).wait_recv()
            grad = send_p[i] + recv_p[i]
            keep = keep_of(at)
            normed, inverse = norm_parts(x_in[own, :].astype(full) * keep)
            back = norm_grad(grad, normed, inverse, scale_one[...])
            hidden_copy.wait()

            @pl.when(i > 0)
            def _():
                store_tokens(i - 1).wait()

            to[...] = ((gh[...] + back) * keep).astype(half)
            store_tokens(i).start()
            return total + jnp.sum(grad * normed, axis=0, keepdims=True)

        first = lax.fori_loop(0, parts, take, jnp.zeros((1, width), full))
        store_tokens(parts - 1).wait()
        core_sent(2)
        for j in range(8):
            terms[0, j : j + 1, :] = first[:, 128 * j : 128 * j + 128]
        terms[0, 16:24, :] = jnp.broadcast_to(moment[...], (8, 128))

    pl.run_scoped(
        inner,
        pltpu.VMEM(wq.shape, half),
        pltpu.VMEM(wk.shape, half),
        pltpu.VMEM(wv.shape, half),
        pltpu.VMEM((rows, width), half),
        pltpu.VMEM((part, width), full),
        pltpu.VMEM((part, width), half),
        pltpu.SemaphoreType.DMA((4,)),
        pltpu.SemaphoreType.DMA,
        pltpu.SemaphoreType.DMA,
    )
    done = 18
    for stage in range(4):
        held = 2**stage
        exchange = pltpu.make_async_remote_copy(
            src_ref=terms.at[pl.ds(0, held)], dst_ref=terms.at[pl.ds(held, held)],
            send_sem=gsem.at[stage], recv_sem=jsem.at[stage], device_id=across(held), device_id_type=MESH,
        )
        exchange.start()
        tick(jnp.int32(done + stage))
        exchange.wait()
    rows_out[...] = terms[...]
    run_ticks(done + 4, ITEMS + LAGS[3])

    def drain(i, _):
        @pl.when(i >= ITEMS - RING)
        def _():
            copy(i, 0).wait_send()

        copy(i, 3).wait_send()
        return 0

    lax.fori_loop(0, ITEMS, drain, 0)


def backward(names, length, moment, scale_one, scale_two, *arrays):
    tokens, slope = arrays[-6], arrays[-4]
    rows, width = tokens.shape
    smem = pl.BlockSpec(memory_space=pltpu.SMEM)
    vmem = pl.BlockSpec(memory_space=pltpu.VMEM)
    hbm = pl.BlockSpec(memory_space=pl.ANY)
    half, full = jnp.bfloat16, jnp.float32
    dma = pltpu.SemaphoreType.DMA
    return pl.pallas_call(
        functools.partial(backward_kernel, names),
        out_shape=[
            jax.ShapeDtypeStruct((ITEMS, 64, TILE), full),
            jax.ShapeDtypeStruct((16, 24, 128), full),
            jax.ShapeDtypeStruct((rows, width), half),
            jax.ShapeDtypeStruct((rows, width), half),
            jax.ShapeDtypeStruct(slope.shape, half),
            jax.ShapeDtypeStruct((rows, width), full),
        ],
        in_specs=[smem] + [vmem] * 3 + [hbm] * len(arrays),
        out_specs=[vmem] * 2 + [hbm] * 4,
        scratch_shapes=[
            pltpu.VMEM((3, 16, 64, rows), half),
            pltpu.VMEM((RING, 8, 64, TILE), full),
            pltpu.VMEM((HELD, 8, 64, TILE), full),
            pltpu.VMEM((HELD, 4, 64, TILE), full),
            pltpu.VMEM((ITEMS, 2, 64, TILE), full),
            pltpu.VMEM((ITEMS, 1, 64, TILE), full),
            pltpu.VMEM((2, 2, rows, TILE), half),
            pltpu.VMEM((6, rows, TILE), half),
            pltpu.VMEM((rows // 256, 256, width), full),
            pltpu.VMEM((rows // 256, 256, width), full),
            pltpu.VMEM((rows, width), half),
            pltpu.VMEM((16, 24, 128), full),
            dma,
            dma((2, 2)),
            dma((4, ITEMS)),
            dma((4, ITEMS)),
            dma((3, 4)),
            dma((3, 4)),
            dma((4,)),
            dma((4,)),
            pltpu.SemaphoreType.REGULAR((3,)),
            pltpu.SemaphoreType.REGULAR((3,)),
            pltpu.SemaphoreType.REGULAR,
        ],
        compiler_params=pltpu.CompilerParams(
            collective_id=0, has_side_effects=True, vmem_limit_bytes=60 * 2**20
        ),
        name="backward",
    )(length, moment, scale_one, scale_two, *arrays)


def fast_body(
    tokens,
    cotangent,
    lengths,
    noise_times,
    query_weight,
    key_weight,
    value_weight,
    merge_weight,
    up_weight,
    down_weight,
    first_scales,
    second_scales,
):
    tokens, cotangent = tokens[0], cotangent[0]
    rows, width = tokens.shape
    table_rows = first_scales.shape[0]
    chunks = lax.axis_size("dp")
    names = ("dp", "tensor")
    moment = noise_times[0]
    scale_one = lax.dynamic_slice_in_dim(first_scales, moment, 1, axis=0)
    scale_two = lax.dynamic_slice_in_dim(second_scales, moment, 1, axis=0)
    cosine, sine = (jnp.asarray(a) for a in rope_lanes(rows))
    query, key, value, heads, heads_t, lse, hidden, activated, slope, mlp_t = forward(
        names, lengths, tokens, cotangent, scale_one, scale_two, cosine, sine,
        query_weight, key_weight, value_weight, merge_weight, up_weight,
    )
    pieces, gathered, grad_tokens, layer_output, _, _ = backward(
        names, lengths, jnp.full((1, 128), 1.0, jnp.float32) * moment.astype(jnp.float32), scale_one, scale_two,
        mlp_t, activated, heads, query, key, value, heads_t, lse, cosine, sine,
        merge_weight, query_weight, key_weight, value_weight, tokens, hidden, slope, cotangent, up_weight, down_weight,
    )
    wide = lambda a: a.transpose(1, 0, 2).reshape(width // chunks, -1)
    tall = lambda a: a.transpose(0, 2, 1).reshape(-1, width // chunks)
    grad_query, grad_key, grad_value = (wide(pieces[18 + k :: 3]) for k in range(3))
    hits = (gathered[:, 16, :1] == jnp.arange(table_rows, dtype=jnp.float32)[None, :]).astype(jnp.float32)
    mine = lax.axis_index("dp") * (width // chunks)
    terms = gathered[:, :16].reshape(chunks, 2, width)
    columns = lax.dynamic_slice_in_dim(terms, mine, width // chunks, axis=2).reshape(chunks, -1)
    tables = jnp.dot(hits.T, columns, precision=highest)
    grad_first, grad_second = jnp.split(tables, 2, axis=1)
    return (
        layer_output[None],
        grad_tokens[None],
        grad_query,
        grad_key,
        grad_value,
        tall(pieces[16:18]),
        wide(pieces[8:16]),
        tall(pieces[:8]),
        grad_first,
        grad_second,
    )


def body(
    tokens,
    cotangent,
    lengths,
    noise_times,
    query_weight,
    key_weight,
    value_weight,
    merge_weight,
    up_weight,
    down_weight,
    first_scales,
    second_scales,
):
    seq_count, length, width = tokens.shape
    local_width = query_weight.shape[1]
    local_heads = local_width // HEAD
    table_rows = first_scales.shape[0]
    flat_rows = seq_count * length
    scale_factor = 1.0 / math.sqrt(HEAD)
    block_rows = min(512, length)
    head_shape = (seq_count, length, local_heads, HEAD)
    row_mask = (jnp.arange(length, dtype=jnp.int32)[None, :] < lengths[:, None]).astype(jnp.float32)
    key_bias = (row_mask - 1.0) * 1000000000.0
    one_hot = (noise_times[:, None] == jnp.arange(table_rows, dtype=jnp.int32)[None, :]).astype(
        jnp.float32
    )
    scale_one = jnp.dot(one_hot, first_scales, precision=highest)
    scale_two = jnp.dot(one_hot, second_scales, precision=highest)
    cos_table, sin_table = rope_tables(length, HEAD)
    inputs = tokens.astype(jnp.float32) * row_mask[:, :, None]
    normed_one, inv_one = normalize(inputs)
    normal_in = (normed_one * scale_one[:, None, :]).astype(jnp.bfloat16).reshape(flat_rows, width)
    queries = jnp.dot(normal_in, query_weight, preferred_element_type=jnp.float32).reshape(
        head_shape
    )
    key_proj = jnp.dot(normal_in, key_weight, preferred_element_type=jnp.float32).reshape(
        head_shape
    )
    value_rows = (
        jnp.dot(normal_in, value_weight, preferred_element_type=jnp.float32)
        .astype(jnp.bfloat16)
        .reshape(head_shape)
    )
    query_rot = rotate(queries, cos_table, sin_table).astype(jnp.bfloat16)
    key_rot = rotate(key_proj, cos_table, sin_table).astype(jnp.bfloat16)
    attended = []
    log_sums = []
    for offset in range(0, length, block_rows):
        scores = block_scores(
            query_rot[:, offset : offset + block_rows], key_rot, key_bias, scale_factor
        )
        peak_score = jnp.max(scores, axis=-1, keepdims=True)
        exponent = jnp.exp(scores - peak_score)
        totals = jnp.sum(exponent, axis=-1, keepdims=True)
        soft_weights = (exponent / totals).astype(jnp.bfloat16)
        log_sums.append(peak_score + jnp.log(totals))
        attended.append(
            jnp.einsum(
                "shqk,skhd->sqhd", soft_weights, value_rows, preferred_element_type=jnp.float32
            )
        )
    heads_out = (
        jnp.concatenate(attended, axis=1).astype(jnp.bfloat16).reshape(flat_rows, local_width)
    )
    attn_part = jnp.dot(heads_out, merge_weight, preferred_element_type=jnp.float32)
    attn_total = lax.psum(attn_part, "tensor")
    hidden_one = inputs + attn_total.reshape(seq_count, length, width)
    normed_two, inv_two = normalize(hidden_one)
    normal_mid = (normed_two * scale_two[:, None, :]).astype(jnp.bfloat16).reshape(flat_rows, width)
    pre_act = jnp.dot(normal_mid, up_weight, preferred_element_type=jnp.float32)
    activated = gelu_tanh(pre_act).astype(jnp.bfloat16)
    mlp_part = jnp.dot(activated, down_weight, preferred_element_type=jnp.float32)
    mlp_total = lax.psum(mlp_part, "tensor")
    layer_output = (
        (hidden_one + mlp_total.reshape(seq_count, length, width)) * row_mask[:, :, None]
    ).astype(jnp.bfloat16)
    grad_final = cotangent.astype(jnp.float32) * row_mask[:, :, None]
    grad_mlp = grad_final.astype(jnp.bfloat16).reshape(flat_rows, width)
    grad_down = jnp.dot(activated.T, grad_mlp, preferred_element_type=jnp.float32)
    grad_act = jnp.dot(grad_mlp, down_weight.T, preferred_element_type=jnp.float32)
    unused_value, gelu_back = jax.vjp(gelu_tanh, pre_act)
    grad_pre = gelu_back(grad_act)[0].astype(jnp.bfloat16)
    grad_up = jnp.dot(normal_mid.T, grad_pre, preferred_element_type=jnp.float32)
    mid_part = jnp.dot(grad_pre, up_weight.T, preferred_element_type=jnp.float32)
    grad_mid = lax.psum(mid_part, "tensor").reshape(seq_count, length, width)
    grad_hat_two, scale_grad_two = norm_back(grad_mid, normed_two, inv_two, scale_two)
    grad_hidden = grad_final + grad_hat_two
    grad_second = jnp.dot(one_hot.T, scale_grad_two, precision=highest)
    grad_attn = grad_hidden.astype(jnp.bfloat16).reshape(flat_rows, width)
    grad_merge = jnp.dot(heads_out.T, grad_attn, preferred_element_type=jnp.float32)
    grad_heads = (
        jnp.dot(grad_attn, merge_weight.T, preferred_element_type=jnp.float32)
        .astype(jnp.bfloat16)
        .reshape(head_shape)
    )
    grad_keys = jnp.zeros(head_shape, jnp.float32)
    grad_values = jnp.zeros(head_shape, jnp.float32)
    query_grads = []
    for block_index in range(len(log_sums)):
        offset = block_index * block_rows
        query_block = query_rot[:, offset : offset + block_rows]
        grad_block = grad_heads[:, offset : offset + block_rows]
        scores = block_scores(query_block, key_rot, key_bias, scale_factor)
        soft_weights = jnp.exp(scores - log_sums[block_index])
        grad_soft = jnp.einsum(
            "sqhd,skhd->shqk", grad_block, value_rows, preferred_element_type=jnp.float32
        )
        grad_values = grad_values + jnp.einsum(
            "shqk,sqhd->skhd",
            soft_weights.astype(jnp.bfloat16),
            grad_block,
            preferred_element_type=jnp.float32,
        )
        grad_scores = (
            soft_weights * (grad_soft - jnp.sum(soft_weights * grad_soft, axis=-1, keepdims=True))
        ).astype(jnp.bfloat16)
        query_grads.append(
            jnp.einsum("shqk,skhd->sqhd", grad_scores, key_rot, preferred_element_type=jnp.float32)
            * scale_factor
        )
        grad_keys = (
            grad_keys
            + jnp.einsum(
                "shqk,sqhd->skhd", grad_scores, query_block, preferred_element_type=jnp.float32
            )
            * scale_factor
        )
    query_back = (
        unrotate(jnp.concatenate(query_grads, axis=1), cos_table, sin_table)
        .astype(jnp.bfloat16)
        .reshape(flat_rows, local_width)
    )
    key_back = (
        unrotate(grad_keys, cos_table, sin_table)
        .astype(jnp.bfloat16)
        .reshape(flat_rows, local_width)
    )
    value_back = grad_values.astype(jnp.bfloat16).reshape(flat_rows, local_width)
    grad_query = jnp.dot(normal_in.T, query_back, preferred_element_type=jnp.float32)
    grad_key = jnp.dot(normal_in.T, key_back, preferred_element_type=jnp.float32)
    grad_value = jnp.dot(normal_in.T, value_back, preferred_element_type=jnp.float32)
    inner_part = jnp.dot(query_back, query_weight.T, preferred_element_type=jnp.float32)
    inner_part = inner_part + jnp.dot(key_back, key_weight.T, preferred_element_type=jnp.float32)
    inner_part = inner_part + jnp.dot(
        value_back, value_weight.T, preferred_element_type=jnp.float32
    )
    grad_inner = lax.psum(inner_part, "tensor").reshape(seq_count, length, width)
    grad_hat_one, scale_grad_one = norm_back(grad_inner, normed_one, inv_one, scale_one)
    grad_tokens = ((grad_hidden + grad_hat_one) * row_mask[:, :, None]).astype(jnp.bfloat16)
    grad_first = jnp.dot(one_hot.T, scale_grad_one, precision=highest)
    summed = (
        lax.psum_scatter(grad_query, "dp", scatter_dimension=0, tiled=True),
        lax.psum_scatter(grad_key, "dp", scatter_dimension=0, tiled=True),
        lax.psum_scatter(grad_value, "dp", scatter_dimension=0, tiled=True),
        lax.psum_scatter(grad_merge, "dp", scatter_dimension=1, tiled=True),
        lax.psum_scatter(grad_up, "dp", scatter_dimension=0, tiled=True),
        lax.psum_scatter(grad_down, "dp", scatter_dimension=1, tiled=True),
        lax.psum_scatter(grad_first, "dp", scatter_dimension=1, tiled=True),
        lax.psum_scatter(grad_second, "dp", scatter_dimension=1, tiled=True),
    )
    return (
        layer_output,
        grad_tokens,
        summed[0],
        summed[1],
        summed[2],
        summed[3],
        summed[4],
        summed[5],
        summed[6],
        summed[7],
    )


def solution(mesh):
    fast = mesh.shape["dp"] == 16 and mesh.shape["tensor"] == 2
    return jax.shard_map(
        fast_body if fast else body,
        mesh=mesh,
        in_specs=(
            P("dp", None, None),
            P("dp", None, None),
            P("dp"),
            P("dp"),
            P(None, "tensor"),
            P(None, "tensor"),
            P(None, "tensor"),
            P("tensor", None),
            P(None, "tensor"),
            P("tensor", None),
            P(),
            P(),
        ),
        out_specs=(
            P("dp", None, None),
            P("dp", None, None),
            P("dp", "tensor"),
            P("dp", "tensor"),
            P("dp", "tensor"),
            P("tensor", "dp"),
            P("dp", "tensor"),
            P("tensor", "dp"),
            P(None, "dp"),
            P(None, "dp"),
        ),
        check_vma=False,
    )
```

```python
import functools
import math

import jax
import jax.numpy as jnp
import numpy as np
from jax import lax
from jax.experimental import pallas as pl
from jax.experimental.pallas import tpu as pltpu
from jax.sharding import PartitionSpec as P

HEAD = 64
MESH = pl.DeviceIdType.MESH


epsilon = 1e-05
highest = lax.Precision.HIGHEST


def gelu_tanh(values):
    return (
        0.5
        * values
        * (1.0 + jnp.tanh(0.7978845608028654 * (values + 0.044715 * values * values * values)))
    )


def rope_tables(length, head_size):
    halves = head_size // 2
    places = jnp.arange(length, dtype=jnp.float32)[:, None]
    frequency = jnp.exp(
        jnp.arange(halves, dtype=jnp.float32) * (-2.0 * math.log(10000.0) / head_size)
    )
    angles = places * frequency[None, :]
    return (jnp.cos(angles), jnp.sin(angles))


def rotate(values, cos_table, sin_table):
    halves = values.shape[-1] // 2
    first_half = values[..., :halves]
    second_half = values[..., halves:]
    cosine = cos_table[:, None, :]
    sine_part = sin_table[:, None, :]
    return jnp.concatenate(
        [
            first_half * cosine - second_half * sine_part,
            second_half * cosine + first_half * sine_part,
        ],
        axis=-1,
    )


def unrotate(gradient, cos_table, sin_table):
    halves = gradient.shape[-1] // 2
    first_half = gradient[..., :halves]
    second_half = gradient[..., halves:]
    cosine = cos_table[:, None, :]
    sine_part = sin_table[:, None, :]
    return jnp.concatenate(
        [
            first_half * cosine + second_half * sine_part,
            second_half * cosine - first_half * sine_part,
        ],
        axis=-1,
    )


def normalize(values):
    centred = values - jnp.mean(values, axis=-1, keepdims=True)
    inv_std = lax.rsqrt(jnp.mean(centred * centred, axis=-1, keepdims=True) + epsilon)
    return (centred * inv_std, inv_std)


def norm_back(grad_norm, normed, inv_std, scale_rows):
    grad_hat = grad_norm * scale_rows[:, None, :]
    grad_scale = jnp.sum(grad_norm * normed, axis=1)
    mean_grad = jnp.mean(grad_hat, axis=-1, keepdims=True)
    mean_cross = jnp.mean(grad_hat * normed, axis=-1, keepdims=True)
    return (inv_std * (grad_hat - mean_grad - normed * mean_cross), grad_scale)


def block_scores(query_block, key_rot, key_bias, scale_factor):
    scores = jnp.einsum("sqhd,skhd->shqk", query_block, key_rot, preferred_element_type=jnp.float32)
    return scores * scale_factor + key_bias[:, None, None, :]


def rope_lanes(length):
    halves = HEAD // 2
    places = np.arange(length, dtype=np.float64)[:, None]
    frequency = np.exp(np.arange(halves) * (-2.0 * math.log(10000.0) / HEAD))
    angles = places * frequency[None, :]
    cosine, sine = np.cos(angles), np.sin(angles)
    return (
        np.concatenate([cosine] * 4, axis=1).astype(np.float32),
        np.concatenate([-sine, sine] * 2, axis=1).astype(np.float32),
    )


def swap_halves(values):
    lanes = lax.broadcasted_iota(jnp.int32, values.shape, 1)
    first = lax.rem(lanes, HEAD) < HEAD // 2
    half = HEAD // 2
    return jnp.where(first, pltpu.roll(values, 128 - half, 1), pltpu.roll(values, half, 1))


def centre(values):
    middle = jnp.mean(values, axis=1, keepdims=True)
    centred = values - middle
    inverse = lax.rsqrt(jnp.mean(centred * centred, axis=1, keepdims=True) + epsilon)
    return centred * inverse


NT = (((1,), (1,)), ((), ()))


def mm(a, b):
    return jnp.dot(a, b, preferred_element_type=jnp.float32)


def mm_nt(a, b):
    return lax.dot_general(a, b, NT, preferred_element_type=jnp.float32)


def forward_kernel(
    names, length_ref, tokens, scale_one, scale_two, cotangent_in, cosine_in, sine_in, wq, wk, wv, wm,
    q_hbm, k_hbm, v_hbm, heads_hbm, heads_t_hbm, lse_hbm, hidden_hbm, mid_hbm, mlp_t_hbm,
    q_out, k_out, v_out, heads, heads_t, lse, hidden, mid, mlp_t, cotangent, cosine, sine,
    nin, vq, vk, vv, vm, other_m, v_t, send_m, recv_m, send_o, recv_o, bias, wsem, osem, tsem, ssem, rsem,
):
    rows, width = tokens.shape
    pairs = q_out.shape[0]
    here = {n: lax.axis_index(n) for n in names}
    other = {**here, names[1]: 1 - here[names[1]]}
    other = tuple(other[n] for n in names)
    loads = [
        pltpu.make_async_copy(a, b, wsem.at[i])
        for i, (a, b) in enumerate(
            ((wq, vq), (wk, vk), (wv, vv), (cosine_in, cosine), (sine_in, sine), (wm, vm), (cotangent_in, cotangent))
        )
    ]
    for c in loads:
        c.start()
    barrier = pltpu.get_barrier_semaphore()
    pl.semaphore_signal(barrier, inc=1, device_id=other, device_id_type=MESH)
    pl.semaphore_wait(barrier, 1)
    length = length_ref[0]

    def place(start, count):
        return start + lax.broadcasted_iota(jnp.int32, (count, 1), 0)

    def mask_of(start, count):
        return jnp.where(place(start, count) < length, 1.0, 0.0)

    bias[...] = jnp.broadcast_to((mask_of(0, rows) - 1.0) * 1000000000.0, (rows, 128))

    def norm_rows(i, _):
        at = pl.multiple_of(i * 128, 128)
        x = tokens[pl.ds(at, 128), :].astype(jnp.float32) * mask_of(at, 128)
        nin[pl.ds(at, 128), :] = (centre(x) * scale_one[...]).astype(jnp.bfloat16)
        return 0

    lax.fori_loop(0, rows // 128, norm_rows, 0)
    for c in loads:
        c.wait()
    send_m[...] = vm[...].astype(jnp.float32)
    merge_copy = pltpu.make_async_remote_copy(
        src_ref=send_m, dst_ref=recv_m, send_sem=ssem.at[0], recv_sem=rsem.at[0],
        device_id=other, device_id_type=MESH,
    )
    merge_copy.start()

    def project(i, _):
        at = pl.multiple_of(i * 256, 256)
        own = pl.ds(at, 256)
        x = nin[own, :]
        c, s = cosine[own, :], sine[own, :]
        for ref, w in ((q_out, vq), (k_out, vk)):
            y = mm(x, w[...])
            for p in range(pairs):
                part = y[:, 128 * p : 128 * p + 128]
                ref[p, own, :] = (part * c + swap_halves(part) * s).astype(jnp.bfloat16)
        y = mm(x, vv[...])
        for p in range(pairs):
            part = y[:, 128 * p : 128 * p + 128]
            v_out[p, own, :] = part.astype(jnp.bfloat16)
            v_t[p, :, own] = part.T.astype(jnp.bfloat16)
        return 0

    lax.fori_loop(0, rows // 256, project, 0)
    stores = [
        pltpu.make_async_copy(a, b, osem.at[i])
        for i, (a, b) in enumerate(
            ((q_out, q_hbm), (k_out, k_hbm), (v_out, v_hbm), (heads, heads_hbm), (heads_t, heads_t_hbm), (lse, lse_hbm),
             (mlp_t, mlp_t_hbm))
        )
    ]
    for c in stores[:3]:
        c.start()

    def o_copy(p):
        return pltpu.make_async_remote_copy(
            src_ref=send_o.at[p], dst_ref=recv_o.at[p], send_sem=ssem.at[1 + p], recv_sem=rsem.at[1 + p],
            device_id=other, device_id_type=MESH,
        )

    lane = lax.broadcasted_iota(jnp.int32, (rows, 128), 1)
    block = 512

    def attend(p, _):
        for h in range(2):
            keys = jnp.where((lane < HEAD) == (h == 0), k_out[p] * 0.125, 0.0).astype(jnp.bfloat16)
            values_t = v_t[p, pl.ds(HEAD * h, HEAD), :]
            for b in range(rows // block):
                cols = pl.ds(b * block, block)
                s = mm_nt(keys, q_out[p, cols, :]) + bias[:, :1]
                peak = jnp.max(s, axis=0, keepdims=True)
                e = jnp.exp(s - peak)
                total = jnp.sum(e, axis=0, keepdims=True)
                o = mm(values_t, e.astype(jnp.bfloat16)) / total
                heads_t[p, pl.ds(HEAD * h, HEAD), cols] = o.astype(jnp.bfloat16)
                lse[pl.ds(2 * p + h, 1), cols] = peak + jnp.log(total)
        o = heads_t[p].astype(jnp.float32).T
        send_o[p] = o
        heads[p] = o.astype(jnp.bfloat16)
        o_copy(p).start()
        count = rows // pairs
        at = pl.multiple_of(p * count, count)
        turned = (cotangent[pl.ds(at, count), :].astype(jnp.float32) * mask_of(at, count)).T
        mlp_t[:, :, pl.ds(at, count)] = turned.astype(jnp.bfloat16).reshape(mlp_t.shape[0], mlp_t.shape[1], count)
        return 0

    lax.fori_loop(0, pairs, attend, 0)
    for c in stores[3:]:
        c.start()
    merge_copy.wait()
    other_m[...] = recv_m[...].astype(jnp.bfloat16)
    for p in range(pairs):
        o_copy(p).wait()

    def tile_stores(i):
        own = pl.ds(pl.multiple_of(i * 256, 256), 256)
        return [
            pltpu.make_async_copy(hidden.at[own, :], hidden_hbm.at[own, :], tsem.at[0, i]),
            pltpu.make_async_copy(mid.at[own, :], mid_hbm.at[own, :], tsem.at[1, i]),
        ]

    def finish(i, _):
        at = pl.multiple_of(i * 256, 256)
        own = pl.ds(at, 256)
        mine = jnp.concatenate([heads[p, own, :] for p in range(pairs)], axis=1)
        theirs = jnp.concatenate([recv_o[p, own, :].astype(jnp.bfloat16) for p in range(pairs)], axis=1)
        attn = mm(mine, vm[...]) + mm(theirs, other_m[...])
        one = tokens[own, :].astype(jnp.float32) * mask_of(at, 256) + attn
        hidden[own, :] = one
        mid[own, :] = (centre(one) * scale_two[...]).astype(jnp.bfloat16)
        for c in tile_stores(i):
            c.start()
        return 0

    lax.fori_loop(0, rows // 256, finish, 0)
    for c in stores:
        c.wait()
    for i in range(rows // 256):
        for c in tile_stores(i):
            c.wait()


def forward(names, length, tokens, scale_one, scale_two, cotangent, cosine, sine, wq, wk, wv, wm):
    rows, width = tokens.shape
    local = wq.shape[1]
    pairs = local // 128
    vmem = pl.BlockSpec(memory_space=pltpu.VMEM)
    hbm = pl.BlockSpec(memory_space=pl.ANY)
    half = jnp.bfloat16
    full = jnp.float32
    shapes = [
        ((pairs, rows, 128), half),
        ((pairs, rows, 128), half),
        ((pairs, rows, 128), half),
        ((pairs, rows, 128), half),
        ((pairs, 128, rows), half),
        ((2 * pairs, rows), full),
        ((rows, width), full),
        ((rows, width), half),
        ((16, width // 16, rows), half),
    ]
    return pl.pallas_call(
        functools.partial(forward_kernel, names),
        out_shape=[jax.ShapeDtypeStruct(*s) for s in shapes],
        in_specs=[pl.BlockSpec(memory_space=pltpu.SMEM)] + [vmem] * 3 + [hbm] * 7,
        out_specs=[hbm] * len(shapes),
        scratch_shapes=[pltpu.VMEM(*s) for s in shapes]
        + [
            pltpu.VMEM((rows, width), half),
            pltpu.VMEM((rows, 128), full),
            pltpu.VMEM((rows, 128), full),
            pltpu.VMEM((rows, width), half),
            pltpu.VMEM(wq.shape, half),
            pltpu.VMEM(wk.shape, half),
            pltpu.VMEM(wv.shape, half),
            pltpu.VMEM(wm.shape, half),
            pltpu.VMEM(wm.shape, half),
            pltpu.VMEM((pairs, 128, rows), half),
            pltpu.VMEM(wm.shape, full),
            pltpu.VMEM(wm.shape, full),
            pltpu.VMEM((pairs, rows, 128), full),
            pltpu.VMEM((pairs, rows, 128), full),
            pltpu.VMEM((rows, 128), full),
            pltpu.SemaphoreType.DMA((7,)),
            pltpu.SemaphoreType.DMA((7,)),
            pltpu.SemaphoreType.DMA((2, 4)),
            pltpu.SemaphoreType.DMA((1 + pairs,)),
            pltpu.SemaphoreType.DMA((1 + pairs,)),
        ],
        compiler_params=pltpu.CompilerParams(collective_id=1, has_side_effects=True, vmem_limit_bytes=58 * 2**20),
        name="forward",
    )(length, tokens, scale_one, scale_two, cotangent, cosine, sine, wq, wk, wv, wm)


ITEMS = 24
TILE = 256
RING = 5
HELD = 12
LAGS = (4, 6, 8, 10)
FIRSTS = (0, 8, 16, 18, 24)


def count_from(i, starts):
    total = 0
    for start in starts:
        total = total + jnp.where(i >= start, 1, 0)
    return total


def flip(index, weight):
    return index + weight * (1 - 2 * lax.rem(lax.div(index, weight), 2))


def weight_of(color, stage):
    k = lax.rem(color + stage, 3)
    return 1 + (k * (k + 1)) // 2


def color_of(i):
    turn = i - lax.div(i + 2, 5)
    return jnp.where(lax.rem(i, 5) == 2, 2, lax.rem(turn, 2))


def slot_of(i):
    return count_from(i, (8, 16)) - 2 * count_from(i, (18,))


def backward_kernel(
    names, length_ref, moment, scale_one, scale_two,
    l_down, mid_in, heads, q_in, k_in, v_in, heads_t, lse_in, cosine, sine,
    merge_in, wq, wk, wv, tokens, hidden, cotangent, wu, wd,
    out, rows_out, tokens_out, layer_out, r_down, slope, r_up, hidden_grad,
    left, s1, r1, r2, r3, r4, rb, qkv, send_p, recv_p, ga, terms,
    lsem, fsem, ssem, csem, psem, qsem, gsem, jsem, credit, credit_two, core_free,
):
    here = {n: lax.axis_index(n) for n in names}
    d = here[names[0]]

    def device(**moved):
        at = {**here, **moved}
        return tuple(at[n] for n in names)

    core = device(**{names[1]: 1 - here[names[1]]})

    def across(weight):
        return device(**{names[0]: flip(d, weight)})

    def absolute(r):
        total = 0
        for b in range(4):
            bit = lax.rem(lax.div(d, 2**b), 2)
            total = total + (2**b) * (1 - bit if (r >> b) & 1 else bit)
        return total

    def load_left(source, slot):
        for r in range(16):
            pltpu.make_async_copy(source.at[absolute(r)], left.at[slot, r], lsem).start()

    def left_loaded(slot):
        pltpu.make_async_copy(left.at[slot], left.at[slot], lsem).wait()

    def turn(values, slot, own):
        turned = values.T.astype(jnp.bfloat16)
        for c in range(16):
            left[slot, absolute(c), :, own] = turned[64 * c : 64 * c + 64]

    load_left(l_down, 0)
    barrier = pltpu.get_barrier_semaphore()
    for weight in (1, 2, 4, 8):
        pl.semaphore_signal(barrier, inc=1, device_id=across(weight), device_id_type=MESH)
    pl.semaphore_signal(barrier, inc=1, device_id=core, device_id_type=MESH)
    pl.semaphore_wait(barrier, 5)

    def fetch(i, lane):
        slot = lax.rem(i, 2)
        target, sem = rb.at[lane, slot], fsem.at[lane, slot]
        for g, source in ((0, r_down), (1, r_up)):
            @pl.when((i >= FIRSTS[g]) & (i < FIRSTS[g + 1]))
            def _():
                col = pl.multiple_of((i - FIRSTS[g]) * TILE, TILE)
                pltpu.make_async_copy(source.at[:, pl.ds(col, TILE)], target, sem).start()

        @pl.when((i >= FIRSTS[2]) & (i < FIRSTS[3]))
        def _():
            for k in range(2):
                pltpu.make_async_copy(
                    heads.at[2 * (i - FIRSTS[2]) + k], target.at[:, pl.ds(128 * k, 128)], sem
                ).start()

        @pl.when(i >= FIRSTS[3])
        def _():
            pltpu.make_async_copy(qkv.at[i - FIRSTS[3]], target, sem).start()

    def fetched(i, lane):
        slot = lax.rem(i, 2)
        pltpu.make_async_copy(rb.at[lane, slot], rb.at[lane, slot], fsem.at[lane, slot]).wait()

    def product(i, first, lane):
        color, slot = color_of(i), slot_of(i)
        weights = [weight_of(color, s) for s in range(3)] + [8]
        rows = []
        for bits in range(8):
            r = first * weights[0] + sum(((bits >> (2 - k)) & 1) * weights[1 + k] for k in range(3))
            rows.append(left[slot, r])
        lhs = jnp.concatenate(rows, axis=0)
        return mm(lhs, rb[lane, lax.rem(i, 2)]).reshape(8, 64, TILE)

    def copy(i, s):
        weight = weight_of(color_of(i), s) if s < 3 else 8
        src = (s1.at[lax.rem(i, RING)], r1.at[lax.rem(i, HELD), pl.ds(4, 4)], r2.at[lax.rem(i, HELD), pl.ds(2, 2)], r3.at[i, pl.ds(1, 1)])[s]
        dst = (r1.at[lax.rem(i, HELD)], r2.at[lax.rem(i, HELD)], r3.at[i], r4.at[i])[s]
        return pltpu.make_async_remote_copy(
            src_ref=src, dst_ref=dst, send_sem=ssem.at[s, i], recv_sem=csem.at[s, i],
            device_id=across(weight), device_id_type=MESH,
        )

    def tick(i):
        a = i - LAGS[0]

        @pl.when((a >= 0) & (a < ITEMS))
        def _():
            fetched(a, 1)
            copy(a, 0).wait_recv()
            r1[lax.rem(a, HELD)] += product(a, 0, 1)

            @pl.when(a >= HELD)
            def _():
                pl.semaphore_wait(credit_two.at[color_of(a)], 1)

            copy(a, 1).start()

            @pl.when(a + 2 < ITEMS)
            def _():
                fetch(a + 2, 1)

        b = i - LAGS[1]

        @pl.when((b >= 0) & (b < ITEMS))
        def _():
            copy(b, 1).wait_recv()
            r2[lax.rem(b, HELD)] += r1[lax.rem(b, HELD), 0:4]
            copy(b, 2).start()
            copy(b, 1).wait_send()

            @pl.when(b + HELD < ITEMS)
            def _():
                color = color_of(b + HELD)
                pl.semaphore_signal(
                    credit.at[color], inc=1, device_id=across(weight_of(color, 0)), device_id_type=MESH
                )

        c = i - LAGS[2]

        @pl.when((c >= 0) & (c < ITEMS))
        def _():
            copy(c, 2).wait_recv()
            r3[c] += r2[lax.rem(c, HELD), 0:2]
            copy(c, 3).start()
            copy(c, 2).wait_send()

            @pl.when(c + HELD < ITEMS)
            def _():
                color = color_of(c + HELD)
                pl.semaphore_signal(
                    credit_two.at[color], inc=1, device_id=across(weight_of(color, 1)), device_id_type=MESH
                )

        e = i - LAGS[3]

        @pl.when((e >= 0) & (e < ITEMS))
        def _():
            copy(e, 3).wait_recv()
            out[e] = r4[e, 0] + r3[e, 0]

        @pl.when(i < ITEMS)
        def _():
            @pl.when(i >= RING)
            def _():
                copy(i - RING, 0).wait_send()

            @pl.when(i >= LAGS[0])
            def _():
                fetched(i, 0)

            s1[lax.rem(i, RING)] = product(i, 1, 0)

            @pl.when(i >= HELD)
            def _():
                pl.semaphore_wait(credit.at[color_of(i)], 1)

            copy(i, 0).start()

            @pl.when((i + 2 < ITEMS) & (i >= LAGS[0]))
            def _():
                fetch(i + 2, 0)

    rows, width = tokens.shape
    pairs = q_in.shape[0]
    length = length_ref[0]
    part = 256
    parts = rows // part
    half, full = jnp.bfloat16, jnp.float32

    def keep_of(at):
        return jnp.where(at + lax.broadcasted_iota(jnp.int32, (part, 1), 0) < length, 1.0, 0.0)

    def core_copy(use, i):
        return pltpu.make_async_remote_copy(
            src_ref=send_p.at[i], dst_ref=recv_p.at[i], send_sem=psem.at[use, i], recv_sem=qsem.at[use, i],
            device_id=core, device_id_type=MESH,
        )

    def core_sent(use):
        for i in range(parts):
            core_copy(use, i).wait_send()
        if use < 2:
            pl.semaphore_signal(core_free, inc=1, device_id=core, device_id_type=MESH)
            pl.semaphore_wait(core_free, 1)

    def norm_parts(values):
        centred = values - jnp.mean(values, axis=1, keepdims=True)
        inverse = lax.rsqrt(jnp.mean(centred * centred, axis=1, keepdims=True) + epsilon)
        return centred * inverse, inverse

    def norm_grad(grad, normed, inverse, scale):
        hat = grad * scale
        middle = jnp.mean(hat, axis=1, keepdims=True)
        return inverse * (hat - middle - normed * jnp.mean(hat * normed, axis=1, keepdims=True))

    def run_ticks(first, last):
        lax.fori_loop(first, last, lambda i, _: (tick(i), 0)[1], 0)

    def mlp(vu, vd, cot, wide, hid, gp, gh, wsem, usem, dsem, tsem, osem):
        mid_load = pltpu.make_async_copy(mid_in, ga, wsem.at[0])
        mid_load.start()
        tiles = wu.shape[1] // TILE

        def columns(k):
            return pl.ds(pl.multiple_of(k * TILE, TILE), TILE)

        def up_load(k):
            return pltpu.make_async_copy(wu.at[:, columns(k)], vu.at[:, columns(k)], usem.at[k])

        for k in range(tiles):
            up_load(k).start()
        down_load = pltpu.make_async_copy(wd, vd, wsem.at[1])
        down_load.start()

        def tile_stores(k, lane):
            slot = lax.rem(k, 2)
            return (
                pltpu.make_async_copy(rb.at[lane, slot], r_down.at[:, columns(k)], dsem.at[0, slot]),
                pltpu.make_async_copy(qkv.at[slot], slope.at[:, columns(k)], dsem.at[1, slot]),
            )

        def up_tile(k, lane):
            slot = lax.rem(k, 2)

            @pl.when(k >= 2)
            def _():
                for x in tile_stores(k - 2, lane):
                    x.wait()

            up_load(k).wait()
            for r in range(0, rows, 512):
                v = mm(ga[r : r + 512, :], vu[:, columns(k)])
                square = v * v
                t = jnp.tanh(0.7978845608028654 * v * (1.0 + 0.044715 * square))
                above = 0.5 * (1.0 + t)
                rb[lane, slot, r : r + 512, :] = (v * above).astype(half)
                qkv[slot, r : r + 512, :] = (
                    above + 0.5 * v * (1.0 - t * t) * (0.7978845608028654 * (1.0 + 0.134145 * square))
                ).astype(half)
            for x in tile_stores(k, lane):
                x.start()

        def tile(source, target, n, i):
            own = pl.ds(pl.multiple_of(i * part, part), part)
            slot = lax.rem(i, 2)
            return pltpu.make_async_copy(source.at[own, :], target.at[slot], tsem.at[n, slot])

        def stream(sources, i, body):
            for n, source, target in sources:
                tile(source, target, n, i).wait()

                @pl.when(i + 1 < parts)
                def _():
                    tile(source, target, n, i + 1).start()

            return body(i, pl.multiple_of(i * part, part), lax.rem(i, 2))

        def begin(sources):
            for n, source, target in sources:
                tile(source, target, n, jnp.int32(0)).start()

        mid_load.wait()
        left_loaded(0)

        def early(k, _):
            up_tile(k, 0)
            tick(k)
            return 0

        lax.fori_loop(0, LAGS[0], early, 0)
        lax.fori_loop(LAGS[0], tiles, lambda k, _: (up_tile(k, 1), 0)[1], 0)
        for k in (tiles - 2, tiles - 1):
            for x in tile_stores(k, 1):
                x.wait()
        for i in range(2):
            fetch(jnp.int32(i), 1)
            fetch(jnp.int32(LAGS[0] + i), 0)
        streams = ((0, cotangent, cot), (1, slope, wide))
        begin(streams)
        down_load.wait()

        def store_pre(i):
            own = pl.ds(pl.multiple_of(i * part, part), part)
            return pltpu.make_async_copy(gp, r_up.at[own, :], osem.at[0])

        def first(i, at, slot):
            x = (cot[slot].astype(full) * keep_of(at)).astype(half)
            g = mm_nt(x, vd[...]) * wide[slot].astype(full)

            @pl.when(i > 0)
            def _():
                store_pre(i - 1).wait()

            gp[...] = g.astype(half)
            store_pre(i).start()
            send_p[i] = mm_nt(gp[...], vu[...])
            core_copy(0, i).start()

            @pl.when(i < 2)
            def _():
                tick(LAGS[0] + i)

            return 0

        lax.fori_loop(0, parts, lambda i, _: stream(streams, i, first), 0)
        store_pre(parts - 1).wait()
        run_ticks(LAGS[0] + 2, LAGS[0] + 4)
        streams_two = ((0, cotangent, cot), (2, hidden, hid))
        begin(streams_two)

        def store_hidden(i):
            own = pl.ds(pl.multiple_of(i * part, part), part)
            return pltpu.make_async_copy(gh, hidden_grad.at[own, :], osem.at[1])

        def second(i, at, slot, total):
            own = pl.ds(at, part)
            normed, inverse = norm_parts(hid[slot])
            turn(normed * scale_two[...], 1, own)
            core_copy(0, i).wait_recv()
            grad = send_p[i] + recv_p[i]

            @pl.when(i > 0)
            def _():
                store_hidden(i - 1).wait()

            gh[...] = cot[slot].astype(full) * keep_of(at) + norm_grad(grad, normed, inverse, scale_two[...])
            store_hidden(i).start()
            ga[own, :] = gh[...].astype(half)
            turn(gh[...], 2, own)
            return total + jnp.sum(grad * normed, axis=0, keepdims=True)

        term = lax.fori_loop(
            0, parts, lambda i, total: stream(streams_two, i, functools.partial(second, total=total)),
            jnp.zeros((1, width), full),
        )
        for j in range(8):
            terms[0, 8 + j : 9 + j, :] = term[:, 128 * j : 128 * j + 128]
        store_hidden(parts - 1).wait()
        core_sent(0)
        streams_three = ((1, r_down, wide),)
        begin(streams_three)

        def third(i, at, slot):
            send_p[i] = mm(wide[slot], vd[...])
            core_copy(1, i).start()
            return 0

        lax.fori_loop(0, parts, lambda i, _: stream(streams_three, i, third), 0)
        streams_four = ((2, hidden, hid),)
        begin(streams_four)
        tick(jnp.int32(LAGS[0] + 4))

        def store_layer(i):
            own = pl.ds(pl.multiple_of(i * part, part), part)
            return pltpu.make_async_copy(cot.at[0], layer_out.at[own, :], osem.at[0])

        def fourth(i, at, slot):
            core_copy(1, i).wait_recv()

            @pl.when(i > 0)
            def _():
                store_layer(i - 1).wait()

            cot[0] = ((hid[slot] + (send_p[i] + recv_p[i])) * keep_of(at)).astype(half)
            store_layer(i).start()
            return 0

        lax.fori_loop(0, parts, lambda i, _: stream(streams_four, i, fourth), 0)
        store_layer(parts - 1).wait()
        core_sent(1)

    pl.run_scoped(
        mlp,
        pltpu.VMEM(wu.shape, half),
        pltpu.VMEM(wd.shape, half),
        pltpu.VMEM((2, part, width), half),
        pltpu.VMEM((2, part, wu.shape[1]), half),
        pltpu.VMEM((2, part, width), full),
        pltpu.VMEM((part, wu.shape[1]), half),
        pltpu.VMEM((part, width), full),
        pltpu.SemaphoreType.DMA((2,)),
        pltpu.SemaphoreType.DMA((wu.shape[1] // TILE,)),
        pltpu.SemaphoreType.DMA((2, 2)),
        pltpu.SemaphoreType.DMA((3, 2)),
        pltpu.SemaphoreType.DMA((2,)),
    )

    def attention(q, k, v, o_t, lse, wm, cos, sin, bias, do, do_t, kh, vh, k_t, dq_t, asem):
        loads = [
            pltpu.make_async_copy(a, b, asem.at[n])
            for n, (a, b) in enumerate(
                ((q_in, q), (k_in, k), (v_in, v), (heads_t, o_t), (lse_in, lse), (merge_in, wm),
                 (cosine, cos), (sine, sin))
            )
        ]
        for x in loads:
            x.start()
        for x in loads:
            x.wait()
        place = lax.broadcasted_iota(jnp.int32, (rows, 128), 0)
        bias[...] = (jnp.where(place < length, 1.0, 0.0) - 1.0) * 1000000000.0
        lane = lax.broadcasted_iota(jnp.int32, (rows, 128), 1) < HEAD
        block = 256

        def unrotate_lanes(y):
            return (y * cos[...] - swap_halves(y) * sin[...]).astype(jnp.bfloat16)

        def pair(p, _):
            weight = wm[pl.ds(pl.multiple_of(128 * p, 128), 128), :]
            do[...] = mm_nt(ga[...], weight).astype(jnp.bfloat16)
            do_t[...] = mm_nt(weight, ga[...]).astype(jnp.bfloat16)
            k_t[...] = (k[p].astype(jnp.float32) * 0.125).T.astype(jnp.bfloat16)
            product_t = do_t[...].astype(jnp.float32) * o_t[p].astype(jnp.float32)
            dks, dvs = [], []
            for h in range(2):
                tick(LAGS[0] + 5 + 2 * p + h)
                delta = jnp.sum(product_t[HEAD * h : HEAD * h + HEAD], axis=0, keepdims=True)
                own = lane == (h == 0)
                kh[...] = jnp.where(own, k[p].astype(jnp.float32) * 0.125, 0.0).astype(jnp.bfloat16)
                vh[...] = jnp.where(own, v[p].astype(jnp.float32), 0.0).astype(jnp.bfloat16)
                dk = jnp.zeros((rows, 128), jnp.float32)
                dv = jnp.zeros((rows, 128), jnp.float32)
                for b in range(0, rows, block):
                    cols = slice(b, b + block)
                    qb = q[p, cols, :]
                    s = mm_nt(kh[...], qb) + bias[:, :1]
                    soft = jnp.exp(s - lse[pl.ds(2 * p + h, 1), cols])
                    ds = soft * (mm(vh[...], do_t[:, cols]) - delta[:, cols])
                    ds = ds.astype(jnp.bfloat16)
                    dv = dv + mm(soft.astype(jnp.bfloat16), do[cols, :])
                    dk = dk + mm(ds, qb)
                    dq_t[HEAD * h : HEAD * h + HEAD, cols] = mm(k_t[HEAD * h : HEAD * h + HEAD, :], ds)
                dks.append(dk)
                dvs.append(dv)
            quad = 3 * lax.div(p, 2)
            at = pl.ds(pl.multiple_of(128 * lax.rem(p, 2), 128), 128)
            qkv[quad, :, at] = unrotate_lanes(dq_t[...].T)
            qkv[quad + 1, :, at] = unrotate_lanes(jnp.where(lane, dks[0], dks[1]) * 0.125)
            qkv[quad + 2, :, at] = jnp.where(lane, dvs[0], dvs[1]).astype(jnp.bfloat16)
            return 0

        lax.fori_loop(0, pairs, pair, 0)

    pl.run_scoped(
        attention,
        pltpu.VMEM((pairs, rows, 128), half),
        pltpu.VMEM((pairs, rows, 128), half),
        pltpu.VMEM((pairs, rows, 128), half),
        pltpu.VMEM((pairs, 128, rows), half),
        pltpu.VMEM((2 * pairs, rows), full),
        pltpu.VMEM(merge_in.shape, half),
        pltpu.VMEM((rows, 128), full),
        pltpu.VMEM((rows, 128), full),
        pltpu.VMEM((rows, 128), full),
        pltpu.VMEM((rows, 128), half),
        pltpu.VMEM((128, rows), half),
        pltpu.VMEM((rows, 128), half),
        pltpu.VMEM((rows, 128), half),
        pltpu.VMEM((128, rows), half),
        pltpu.VMEM((128, rows), full),
        pltpu.SemaphoreType.DMA((10,)),
    )

    def inner(vq, vk, vv, x_in, gh, to, sem, hsem, osem):
        loads = [
            pltpu.make_async_copy(a, b, sem.at[n])
            for n, (a, b) in enumerate(((wq, vq), (wk, vk), (wv, vv), (tokens, x_in)))
        ]
        for x in loads:
            x.start()
        for x in loads:
            x.wait()

        def send(i, _):
            at = pl.multiple_of(i * part, part)
            own = pl.ds(at, part)
            total = None
            for quad in range(2):
                for n, w in enumerate((vq, vk, vv)):
                    term = mm_nt(qkv[3 * quad + n, own, :], w[:, TILE * quad : TILE * quad + TILE])
                    total = term if total is None else total + term
            send_p[i] = total
            core_copy(2, i).start()
            normed, _ = norm_parts(x_in[own, :].astype(full) * keep_of(at))
            turn(normed * scale_one[...], 0, own)

            @pl.when(i == 1)
            def _():
                tick(LAGS[0] + 13)

            return 0

        lax.fori_loop(0, parts, send, 0)

        def store_tokens(i):
            own = pl.ds(pl.multiple_of(i * part, part), part)
            return pltpu.make_async_copy(to, tokens_out.at[own, :], osem)

        def take(i, total):
            at = pl.multiple_of(i * part, part)
            own = pl.ds(at, part)
            hidden_copy = pltpu.make_async_copy(hidden_grad.at[own, :], gh, hsem)
            hidden_copy.start()

            @pl.when(i < 2)
            def _():
                tick(LAGS[0] + 14 + i)

            core_copy(2, i).wait_recv()
            grad = send_p[i] + recv_p[i]
            keep = keep_of(at)
            normed, inverse = norm_parts(x_in[own, :].astype(full) * keep)
            back = norm_grad(grad, normed, inverse, scale_one[...])
            hidden_copy.wait()

            @pl.when(i > 0)
            def _():
                store_tokens(i - 1).wait()

            to[...] = ((gh[...] + back) * keep).astype(half)
            store_tokens(i).start()
            return total + jnp.sum(grad * normed, axis=0, keepdims=True)

        first = lax.fori_loop(0, parts, take, jnp.zeros((1, width), full))
        store_tokens(parts - 1).wait()
        core_sent(2)
        for j in range(8):
            terms[0, j : j + 1, :] = first[:, 128 * j : 128 * j + 128]
        terms[0, 16:24, :] = jnp.broadcast_to(moment[...], (8, 128))

    pl.run_scoped(
        inner,
        pltpu.VMEM(wq.shape, half),
        pltpu.VMEM(wk.shape, half),
        pltpu.VMEM(wv.shape, half),
        pltpu.VMEM((rows, width), half),
        pltpu.VMEM((part, width), full),
        pltpu.VMEM((part, width), half),
        pltpu.SemaphoreType.DMA((4,)),
        pltpu.SemaphoreType.DMA,
        pltpu.SemaphoreType.DMA,
    )
    done = LAGS[0] + 16
    for stage in range(4):
        held = 2**stage
        exchange = pltpu.make_async_remote_copy(
            src_ref=terms.at[pl.ds(0, held)], dst_ref=terms.at[pl.ds(held, held)],
            send_sem=gsem.at[stage], recv_sem=jsem.at[stage], device_id=across(held), device_id_type=MESH,
        )
        exchange.start()
        tick(jnp.int32(done + stage))
        exchange.wait()
    rows_out[...] = terms[...]
    run_ticks(done + 4, ITEMS + LAGS[3])

    def drain(i, _):
        @pl.when(i >= ITEMS - RING)
        def _():
            copy(i, 0).wait_send()

        copy(i, 3).wait_send()
        return 0

    lax.fori_loop(0, ITEMS, drain, 0)


def backward(names, length, moment, scale_one, scale_two, *arrays):
    tokens, up = arrays[-5], arrays[-2]
    rows, width = tokens.shape
    smem = pl.BlockSpec(memory_space=pltpu.SMEM)
    vmem = pl.BlockSpec(memory_space=pltpu.VMEM)
    hbm = pl.BlockSpec(memory_space=pl.ANY)
    half, full = jnp.bfloat16, jnp.float32
    dma = pltpu.SemaphoreType.DMA
    return pl.pallas_call(
        functools.partial(backward_kernel, names),
        out_shape=[
            jax.ShapeDtypeStruct((ITEMS, 64, TILE), full),
            jax.ShapeDtypeStruct((16, 24, 128), full),
            jax.ShapeDtypeStruct((rows, width), half),
            jax.ShapeDtypeStruct((rows, width), half),
            jax.ShapeDtypeStruct((rows, up.shape[1]), half),
            jax.ShapeDtypeStruct((rows, up.shape[1]), half),
            jax.ShapeDtypeStruct((rows, up.shape[1]), half),
            jax.ShapeDtypeStruct((rows, width), full),
        ],
        in_specs=[smem] + [vmem] * 3 + [hbm] * len(arrays),
        out_specs=[vmem] * 2 + [hbm] * 6,
        scratch_shapes=[
            pltpu.VMEM((3, 16, 64, rows), half),
            pltpu.VMEM((RING, 8, 64, TILE), full),
            pltpu.VMEM((HELD, 8, 64, TILE), full),
            pltpu.VMEM((HELD, 4, 64, TILE), full),
            pltpu.VMEM((ITEMS, 2, 64, TILE), full),
            pltpu.VMEM((ITEMS, 1, 64, TILE), full),
            pltpu.VMEM((2, 2, rows, TILE), half),
            pltpu.VMEM((6, rows, TILE), half),
            pltpu.VMEM((rows // 256, 256, width), full),
            pltpu.VMEM((rows // 256, 256, width), full),
            pltpu.VMEM((rows, width), half),
            pltpu.VMEM((16, 24, 128), full),
            dma,
            dma((2, 2)),
            dma((4, ITEMS)),
            dma((4, ITEMS)),
            dma((3, 4)),
            dma((3, 4)),
            dma((4,)),
            dma((4,)),
            pltpu.SemaphoreType.REGULAR((3,)),
            pltpu.SemaphoreType.REGULAR((3,)),
            pltpu.SemaphoreType.REGULAR,
        ],
        compiler_params=pltpu.CompilerParams(
            collective_id=0, has_side_effects=True, vmem_limit_bytes=60 * 2**20
        ),
        name="backward",
    )(length, moment, scale_one, scale_two, *arrays)


def finish_kernel(
    names, pieces, gathered, tokens_in, layer_in,
    layer_out, tokens_out, grad_q, grad_k, grad_v, grad_m, grad_u, grad_d, first, second, held, sem,
):
    parts = held.shape[1]
    step = layer_in.shape[0] // parts

    def move(n, k):
        source, target = ((layer_in, layer_out), (tokens_in, tokens_out))[n]
        own = pl.ds(k * step, step)
        return (
            pltpu.make_async_copy(source.at[own, :], held.at[n, k], sem.at[0, n, k]),
            pltpu.make_async_copy(held.at[n, k], target.at[own, :], sem.at[1, n, k]),
        )

    moves = [move(n, k) for n in range(2) for k in range(parts)]
    for m in moves:
        m[0].start()
    for k in range(8):
        grad_d[:, TILE * k : TILE * k + TILE] = pieces[k]
        grad_u[:, TILE * k : TILE * k + TILE] = pieces[8 + k]
    for k in range(2):
        grad_m[:, TILE * k : TILE * k + TILE] = pieces[16 + k]
        for n, ref in enumerate((grad_q, grad_k, grad_v)):
            ref[:, TILE * k : TILE * k + TILE] = pieces[18 + 3 * k + n]
    for m in moves:
        m[0].wait()
        m[1].start()
    d = lax.axis_index(names[0])
    count, table_rows = first.shape
    upper = lax.rem(d, 2) == 1
    places = lax.broadcasted_iota(jnp.int32, (table_rows, 128), 0).astype(jnp.float32)
    total = jnp.zeros((table_rows, 128), jnp.float32)
    for s in range(gathered.shape[0]):
        row = []
        for base in (0, 8):
            part = gathered[s, pl.ds(base + lax.div(d, 2), 1), :]
            row.append(jnp.where(upper, part[:, count:], part[:, :count]))
        total = total + jnp.where(places == gathered[s, 16:17, :], jnp.concatenate(row, axis=1), 0.0)
    turned = total.T
    first[...] = turned[:count]
    second[...] = turned[count:]
    for m in moves:
        m[1].wait()


def finish(names, table_rows, pieces, gathered, tokens, layer):
    vmem = pl.BlockSpec(memory_space=pltpu.VMEM)
    hbm = pl.BlockSpec(memory_space=pl.ANY)
    full = jnp.float32
    rows, width = layer.shape
    shapes = [(64, 512)] * 4 + [(64, 2048), (64, 2048), (64, table_rows), (64, table_rows)]
    layer, tokens, *grads = pl.pallas_call(
        functools.partial(finish_kernel, names),
        out_shape=[jax.ShapeDtypeStruct(a.shape, a.dtype) for a in (layer, tokens)]
        + [jax.ShapeDtypeStruct(s, full) for s in shapes],
        in_specs=[vmem] * 2 + [hbm] * 2,
        out_specs=[hbm] * 2 + [vmem] * len(shapes),
        scratch_shapes=[
            pltpu.VMEM((2, 4, rows // 4, width), layer.dtype),
            pltpu.SemaphoreType.DMA((2, 2, 4)),
        ],
        name="finish",
    )(pieces, gathered, tokens, layer)
    query, key, value, merge, up, down, first, second = grads
    return layer[None], tokens[None], query, key, value, merge.T, up, down.T, first.T, second.T


def fast_body(
    tokens,
    cotangent,
    lengths,
    noise_times,
    query_weight,
    key_weight,
    value_weight,
    merge_weight,
    up_weight,
    down_weight,
    first_scales,
    second_scales,
):
    tokens, cotangent = tokens[0], cotangent[0]
    rows, width = tokens.shape
    names = ("dp", "tensor")
    moment = noise_times[0]
    scale_one = lax.dynamic_slice_in_dim(first_scales, moment, 1, axis=0)
    scale_two = lax.dynamic_slice_in_dim(second_scales, moment, 1, axis=0)
    cosine, sine = (jnp.asarray(a) for a in rope_lanes(rows))
    query, key, value, heads, heads_t, lse, hidden, normal_mid, mlp_t = forward(
        names, lengths, tokens, scale_one, scale_two, cotangent, cosine, sine,
        query_weight, key_weight, value_weight, merge_weight,
    )
    pieces, gathered, grad_tokens, layer_output, *_ = backward(
        names, lengths, jnp.full((1, 128), 1.0, jnp.float32) * moment.astype(jnp.float32), scale_one, scale_two,
        mlp_t, normal_mid, heads, query, key, value, heads_t, lse, cosine, sine,
        merge_weight, query_weight, key_weight, value_weight, tokens, hidden, cotangent, up_weight, down_weight,
    )
    return finish(names, first_scales.shape[0], pieces, gathered, grad_tokens, layer_output)


def body(
    tokens,
    cotangent,
    lengths,
    noise_times,
    query_weight,
    key_weight,
    value_weight,
    merge_weight,
    up_weight,
    down_weight,
    first_scales,
    second_scales,
):
    seq_count, length, width = tokens.shape
    local_width = query_weight.shape[1]
    local_heads = local_width // HEAD
    table_rows = first_scales.shape[0]
    flat_rows = seq_count * length
    scale_factor = 1.0 / math.sqrt(HEAD)
    block_rows = min(512, length)
    head_shape = (seq_count, length, local_heads, HEAD)
    row_mask = (jnp.arange(length, dtype=jnp.int32)[None, :] < lengths[:, None]).astype(jnp.float32)
    key_bias = (row_mask - 1.0) * 1000000000.0
    one_hot = (noise_times[:, None] == jnp.arange(table_rows, dtype=jnp.int32)[None, :]).astype(
        jnp.float32
    )
    scale_one = jnp.dot(one_hot, first_scales, precision=highest)
    scale_two = jnp.dot(one_hot, second_scales, precision=highest)
    cos_table, sin_table = rope_tables(length, HEAD)
    inputs = tokens.astype(jnp.float32) * row_mask[:, :, None]
    normed_one, inv_one = normalize(inputs)
    normal_in = (normed_one * scale_one[:, None, :]).astype(jnp.bfloat16).reshape(flat_rows, width)
    queries = jnp.dot(normal_in, query_weight, preferred_element_type=jnp.float32).reshape(
        head_shape
    )
    key_proj = jnp.dot(normal_in, key_weight, preferred_element_type=jnp.float32).reshape(
        head_shape
    )
    value_rows = (
        jnp.dot(normal_in, value_weight, preferred_element_type=jnp.float32)
        .astype(jnp.bfloat16)
        .reshape(head_shape)
    )
    query_rot = rotate(queries, cos_table, sin_table).astype(jnp.bfloat16)
    key_rot = rotate(key_proj, cos_table, sin_table).astype(jnp.bfloat16)
    attended = []
    log_sums = []
    for offset in range(0, length, block_rows):
        scores = block_scores(
            query_rot[:, offset : offset + block_rows], key_rot, key_bias, scale_factor
        )
        peak_score = jnp.max(scores, axis=-1, keepdims=True)
        exponent = jnp.exp(scores - peak_score)
        totals = jnp.sum(exponent, axis=-1, keepdims=True)
        soft_weights = (exponent / totals).astype(jnp.bfloat16)
        log_sums.append(peak_score + jnp.log(totals))
        attended.append(
            jnp.einsum(
                "shqk,skhd->sqhd", soft_weights, value_rows, preferred_element_type=jnp.float32
            )
        )
    heads_out = (
        jnp.concatenate(attended, axis=1).astype(jnp.bfloat16).reshape(flat_rows, local_width)
    )
    attn_part = jnp.dot(heads_out, merge_weight, preferred_element_type=jnp.float32)
    attn_total = lax.psum(attn_part, "tensor")
    hidden_one = inputs + attn_total.reshape(seq_count, length, width)
    normed_two, inv_two = normalize(hidden_one)
    normal_mid = (normed_two * scale_two[:, None, :]).astype(jnp.bfloat16).reshape(flat_rows, width)
    pre_act = jnp.dot(normal_mid, up_weight, preferred_element_type=jnp.float32)
    activated = gelu_tanh(pre_act).astype(jnp.bfloat16)
    mlp_part = jnp.dot(activated, down_weight, preferred_element_type=jnp.float32)
    mlp_total = lax.psum(mlp_part, "tensor")
    layer_output = (
        (hidden_one + mlp_total.reshape(seq_count, length, width)) * row_mask[:, :, None]
    ).astype(jnp.bfloat16)
    grad_final = cotangent.astype(jnp.float32) * row_mask[:, :, None]
    grad_mlp = grad_final.astype(jnp.bfloat16).reshape(flat_rows, width)
    grad_down = jnp.dot(activated.T, grad_mlp, preferred_element_type=jnp.float32)
    grad_act = jnp.dot(grad_mlp, down_weight.T, preferred_element_type=jnp.float32)
    unused_value, gelu_back = jax.vjp(gelu_tanh, pre_act)
    grad_pre = gelu_back(grad_act)[0].astype(jnp.bfloat16)
    grad_up = jnp.dot(normal_mid.T, grad_pre, preferred_element_type=jnp.float32)
    mid_part = jnp.dot(grad_pre, up_weight.T, preferred_element_type=jnp.float32)
    grad_mid = lax.psum(mid_part, "tensor").reshape(seq_count, length, width)
    grad_hat_two, scale_grad_two = norm_back(grad_mid, normed_two, inv_two, scale_two)
    grad_hidden = grad_final + grad_hat_two
    grad_second = jnp.dot(one_hot.T, scale_grad_two, precision=highest)
    grad_attn = grad_hidden.astype(jnp.bfloat16).reshape(flat_rows, width)
    grad_merge = jnp.dot(heads_out.T, grad_attn, preferred_element_type=jnp.float32)
    grad_heads = (
        jnp.dot(grad_attn, merge_weight.T, preferred_element_type=jnp.float32)
        .astype(jnp.bfloat16)
        .reshape(head_shape)
    )
    grad_keys = jnp.zeros(head_shape, jnp.float32)
    grad_values = jnp.zeros(head_shape, jnp.float32)
    query_grads = []
    for block_index in range(len(log_sums)):
        offset = block_index * block_rows
        query_block = query_rot[:, offset : offset + block_rows]
        grad_block = grad_heads[:, offset : offset + block_rows]
        scores = block_scores(query_block, key_rot, key_bias, scale_factor)
        soft_weights = jnp.exp(scores - log_sums[block_index])
        grad_soft = jnp.einsum(
            "sqhd,skhd->shqk", grad_block, value_rows, preferred_element_type=jnp.float32
        )
        grad_values = grad_values + jnp.einsum(
            "shqk,sqhd->skhd",
            soft_weights.astype(jnp.bfloat16),
            grad_block,
            preferred_element_type=jnp.float32,
        )
        grad_scores = (
            soft_weights * (grad_soft - jnp.sum(soft_weights * grad_soft, axis=-1, keepdims=True))
        ).astype(jnp.bfloat16)
        query_grads.append(
            jnp.einsum("shqk,skhd->sqhd", grad_scores, key_rot, preferred_element_type=jnp.float32)
            * scale_factor
        )
        grad_keys = (
            grad_keys
            + jnp.einsum(
                "shqk,sqhd->skhd", grad_scores, query_block, preferred_element_type=jnp.float32
            )
            * scale_factor
        )
    query_back = (
        unrotate(jnp.concatenate(query_grads, axis=1), cos_table, sin_table)
        .astype(jnp.bfloat16)
        .reshape(flat_rows, local_width)
    )
    key_back = (
        unrotate(grad_keys, cos_table, sin_table)
        .astype(jnp.bfloat16)
        .reshape(flat_rows, local_width)
    )
    value_back = grad_values.astype(jnp.bfloat16).reshape(flat_rows, local_width)
    grad_query = jnp.dot(normal_in.T, query_back, preferred_element_type=jnp.float32)
    grad_key = jnp.dot(normal_in.T, key_back, preferred_element_type=jnp.float32)
    grad_value = jnp.dot(normal_in.T, value_back, preferred_element_type=jnp.float32)
    inner_part = jnp.dot(query_back, query_weight.T, preferred_element_type=jnp.float32)
    inner_part = inner_part + jnp.dot(key_back, key_weight.T, preferred_element_type=jnp.float32)
    inner_part = inner_part + jnp.dot(
        value_back, value_weight.T, preferred_element_type=jnp.float32
    )
    grad_inner = lax.psum(inner_part, "tensor").reshape(seq_count, length, width)
    grad_hat_one, scale_grad_one = norm_back(grad_inner, normed_one, inv_one, scale_one)
    grad_tokens = ((grad_hidden + grad_hat_one) * row_mask[:, :, None]).astype(jnp.bfloat16)
    grad_first = jnp.dot(one_hot.T, scale_grad_one, precision=highest)
    summed = (
        lax.psum_scatter(grad_query, "dp", scatter_dimension=0, tiled=True),
        lax.psum_scatter(grad_key, "dp", scatter_dimension=0, tiled=True),
        lax.psum_scatter(grad_value, "dp", scatter_dimension=0, tiled=True),
        lax.psum_scatter(grad_merge, "dp", scatter_dimension=1, tiled=True),
        lax.psum_scatter(grad_up, "dp", scatter_dimension=0, tiled=True),
        lax.psum_scatter(grad_down, "dp", scatter_dimension=1, tiled=True),
        lax.psum_scatter(grad_first, "dp", scatter_dimension=1, tiled=True),
        lax.psum_scatter(grad_second, "dp", scatter_dimension=1, tiled=True),
    )
    return (
        layer_output,
        grad_tokens,
        summed[0],
        summed[1],
        summed[2],
        summed[3],
        summed[4],
        summed[5],
        summed[6],
        summed[7],
    )


def solution(mesh):
    fast = mesh.shape["dp"] == 16 and mesh.shape["tensor"] == 2
    return jax.shard_map(
        fast_body if fast else body,
        mesh=mesh,
        in_specs=(
            P("dp", None, None),
            P("dp", None, None),
            P("dp"),
            P("dp"),
            P(None, "tensor"),
            P(None, "tensor"),
            P(None, "tensor"),
            P("tensor", None),
            P(None, "tensor"),
            P("tensor", None),
            P(),
            P(),
        ),
        out_specs=(
            P("dp", None, None),
            P("dp", None, None),
            P("dp", "tensor"),
            P("dp", "tensor"),
            P("dp", "tensor"),
            P("tensor", "dp"),
            P("dp", "tensor"),
            P("tensor", "dp"),
            P(None, "dp"),
            P(None, "dp"),
        ),
        check_vma=False,
    )
```

```python
import functools
import math

import jax
import jax.numpy as jnp
import numpy as np
from jax import lax
from jax.experimental import pallas as pl
from jax.experimental.pallas import tpu as pltpu
from jax.sharding import PartitionSpec as P

HEAD = 64
MESH = pl.DeviceIdType.MESH


epsilon = 1e-05
highest = lax.Precision.HIGHEST


def gelu_tanh(values):
    return (
        0.5
        * values
        * (1.0 + jnp.tanh(0.7978845608028654 * (values + 0.044715 * values * values * values)))
    )


def rope_tables(length, head_size):
    halves = head_size // 2
    places = jnp.arange(length, dtype=jnp.float32)[:, None]
    frequency = jnp.exp(
        jnp.arange(halves, dtype=jnp.float32) * (-2.0 * math.log(10000.0) / head_size)
    )
    angles = places * frequency[None, :]
    return (jnp.cos(angles), jnp.sin(angles))


def rotate(values, cos_table, sin_table):
    halves = values.shape[-1] // 2
    first_half = values[..., :halves]
    second_half = values[..., halves:]
    cosine = cos_table[:, None, :]
    sine_part = sin_table[:, None, :]
    return jnp.concatenate(
        [
            first_half * cosine - second_half * sine_part,
            second_half * cosine + first_half * sine_part,
        ],
        axis=-1,
    )


def unrotate(gradient, cos_table, sin_table):
    halves = gradient.shape[-1] // 2
    first_half = gradient[..., :halves]
    second_half = gradient[..., halves:]
    cosine = cos_table[:, None, :]
    sine_part = sin_table[:, None, :]
    return jnp.concatenate(
        [
            first_half * cosine + second_half * sine_part,
            second_half * cosine - first_half * sine_part,
        ],
        axis=-1,
    )


def normalize(values):
    centred = values - jnp.mean(values, axis=-1, keepdims=True)
    inv_std = lax.rsqrt(jnp.mean(centred * centred, axis=-1, keepdims=True) + epsilon)
    return (centred * inv_std, inv_std)


def norm_back(grad_norm, normed, inv_std, scale_rows):
    grad_hat = grad_norm * scale_rows[:, None, :]
    grad_scale = jnp.sum(grad_norm * normed, axis=1)
    mean_grad = jnp.mean(grad_hat, axis=-1, keepdims=True)
    mean_cross = jnp.mean(grad_hat * normed, axis=-1, keepdims=True)
    return (inv_std * (grad_hat - mean_grad - normed * mean_cross), grad_scale)


def block_scores(query_block, key_rot, key_bias, scale_factor):
    scores = jnp.einsum("sqhd,skhd->shqk", query_block, key_rot, preferred_element_type=jnp.float32)
    return scores * scale_factor + key_bias[:, None, None, :]


def rope_lanes(length):
    halves = HEAD // 2
    places = np.arange(length, dtype=np.float64)[:, None]
    frequency = np.exp(np.arange(halves) * (-2.0 * math.log(10000.0) / HEAD))
    angles = places * frequency[None, :]
    cosine, sine = np.cos(angles), np.sin(angles)
    return (
        np.concatenate([cosine] * 4, axis=1).astype(np.float32),
        np.concatenate([-sine, sine] * 2, axis=1).astype(np.float32),
    )


def swap_halves(values):
    lanes = lax.broadcasted_iota(jnp.int32, values.shape, 1)
    first = lax.rem(lanes, HEAD) < HEAD // 2
    half = HEAD // 2
    return jnp.where(first, pltpu.roll(values, 128 - half, 1), pltpu.roll(values, half, 1))


def centre(values):
    middle = jnp.mean(values, axis=1, keepdims=True)
    centred = values - middle
    inverse = lax.rsqrt(jnp.mean(centred * centred, axis=1, keepdims=True) + epsilon)
    return centred * inverse


NT = (((1,), (1,)), ((), ()))


def mm(a, b):
    return jnp.dot(a, b, preferred_element_type=jnp.float32)


def mm_nt(a, b):
    return lax.dot_general(a, b, NT, preferred_element_type=jnp.float32)


def forward_kernel(
    names, length_ref, tokens, scale_one, scale_two, cotangent_in, cosine_in, sine_in, wq, wk, wv, wm,
    q_hbm, k_hbm, v_hbm, heads_hbm, heads_t_hbm, lse_hbm, hidden_hbm, mid_hbm, mlp_t_hbm,
    q_out, k_out, v_out, heads, heads_t, lse, hidden, mid, mlp_t, cotangent, cosine, sine,
    nin, vq, vk, vv, vm, other_m, v_t, send_m, recv_m, send_o, recv_o, bias, wsem, osem, tsem, ssem, rsem,
):
    rows, width = tokens.shape
    pairs = q_out.shape[0]
    here = {n: lax.axis_index(n) for n in names}
    other = {**here, names[1]: 1 - here[names[1]]}
    other = tuple(other[n] for n in names)
    loads = [
        pltpu.make_async_copy(a, b, wsem.at[i])
        for i, (a, b) in enumerate(
            ((wq, vq), (cosine_in, cosine), (sine_in, sine), (wk, vk), (wv, vv), (wm, vm), (cotangent_in, cotangent))
        )
    ]
    for c in loads[:5]:
        c.start()
    barrier = pltpu.get_barrier_semaphore()
    pl.semaphore_signal(barrier, inc=1, device_id=other, device_id_type=MESH)
    pl.semaphore_wait(barrier, 1)
    length = length_ref[0]

    def place(start, count):
        return start + lax.broadcasted_iota(jnp.int32, (count, 1), 0)

    def mask_of(start, count):
        return jnp.where(place(start, count) < length, 1.0, 0.0)

    bias[...] = jnp.broadcast_to((mask_of(0, rows) - 1.0) * 1000000000.0, (rows, 128))

    def norm_rows(i, _):
        at = pl.multiple_of(i * 128, 128)
        x = tokens[pl.ds(at, 128), :].astype(jnp.float32) * mask_of(at, 128)
        nin[pl.ds(at, 128), :] = (centre(x) * scale_one[...]).astype(jnp.bfloat16)
        return 0

    lax.fori_loop(0, rows // 128, norm_rows, 0)
    for c in loads[5:]:
        c.start()
    for c in loads[:5]:
        c.wait()

    def project(i, _):
        at = pl.multiple_of(i * 256, 256)
        own = pl.ds(at, 256)
        x = nin[own, :]
        c, s = cosine[own, :], sine[own, :]
        for ref, w in ((q_out, vq), (k_out, vk)):
            y = mm(x, w[...])
            for p in range(pairs):
                part = y[:, 128 * p : 128 * p + 128]
                ref[p, own, :] = (part * c + swap_halves(part) * s).astype(jnp.bfloat16)
        y = mm(x, vv[...])
        for p in range(pairs):
            part = y[:, 128 * p : 128 * p + 128]
            v_out[p, own, :] = part.astype(jnp.bfloat16)
            v_t[p, :, own] = part.T.astype(jnp.bfloat16)
        return 0

    lax.fori_loop(0, rows // 256, project, 0)
    stores = [
        pltpu.make_async_copy(a, b, osem.at[i])
        for i, (a, b) in enumerate(
            ((q_out, q_hbm), (k_out, k_hbm), (v_out, v_hbm), (heads, heads_hbm), (heads_t, heads_t_hbm), (lse, lse_hbm),
             (mlp_t, mlp_t_hbm))
        )
    ]
    for c in stores[:3]:
        c.start()
    for c in loads[5:]:
        c.wait()
    send_m[...] = vm[...].astype(jnp.float32)
    merge_copy = pltpu.make_async_remote_copy(
        src_ref=send_m, dst_ref=recv_m, send_sem=ssem.at[0], recv_sem=rsem.at[0],
        device_id=other, device_id_type=MESH,
    )
    merge_copy.start()


    def o_copy(p):
        return pltpu.make_async_remote_copy(
            src_ref=send_o.at[p], dst_ref=recv_o.at[p], send_sem=ssem.at[1 + p], recv_sem=rsem.at[1 + p],
            device_id=other, device_id_type=MESH,
        )

    lane = lax.broadcasted_iota(jnp.int32, (rows, 128), 1)
    block = 1024

    def attend(p, _):
        for h in range(2):
            keys = jnp.where((lane < HEAD) == (h == 0), k_out[p] * 0.125, 0.0).astype(jnp.bfloat16)
            values_t = v_t[p, pl.ds(HEAD * h, HEAD), :]
            for b in range(rows // block):
                cols = pl.ds(b * block, block)
                s = mm_nt(keys, q_out[p, cols, :]) + bias[:, :1]
                peak = jnp.max(s, axis=0, keepdims=True)
                e = jnp.exp(s - peak)
                total = jnp.sum(e, axis=0, keepdims=True)
                o = mm(values_t, e.astype(jnp.bfloat16)) / total
                heads_t[p, pl.ds(HEAD * h, HEAD), cols] = o.astype(jnp.bfloat16)
                lse[pl.ds(2 * p + h, 1), cols] = peak + jnp.log(total)
        o = heads_t[p].astype(jnp.float32).T
        send_o[p] = o
        heads[p] = o.astype(jnp.bfloat16)
        o_copy(p).start()
        count = rows // pairs
        at = pl.multiple_of(p * count, count)
        turned = (cotangent[pl.ds(at, count), :].astype(jnp.float32) * mask_of(at, count)).T
        mlp_t[:, :, pl.ds(at, count)] = turned.astype(jnp.bfloat16).reshape(mlp_t.shape[0], mlp_t.shape[1], count)
        return 0

    lax.fori_loop(0, pairs, attend, 0)
    for c in stores[3:]:
        c.start()
    merge_copy.wait()
    other_m[...] = recv_m[...].astype(jnp.bfloat16)
    for p in range(pairs):
        o_copy(p).wait()

    def tile_stores(i):
        own = pl.ds(pl.multiple_of(i * 256, 256), 256)
        return [
            pltpu.make_async_copy(hidden.at[own, :], hidden_hbm.at[own, :], tsem.at[0, i]),
            pltpu.make_async_copy(mid.at[own, :], mid_hbm.at[own, :], tsem.at[1, i]),
        ]

    def finish(i, _):
        at = pl.multiple_of(i * 256, 256)
        own = pl.ds(at, 256)
        mine = jnp.concatenate([heads[p, own, :] for p in range(pairs)], axis=1)
        theirs = jnp.concatenate([recv_o[p, own, :].astype(jnp.bfloat16) for p in range(pairs)], axis=1)
        attn = mm(mine, vm[...]) + mm(theirs, other_m[...])
        one = tokens[own, :].astype(jnp.float32) * mask_of(at, 256) + attn
        hidden[own, :] = one
        mid[own, :] = (centre(one) * scale_two[...]).astype(jnp.bfloat16)
        for c in tile_stores(i):
            c.start()
        return 0

    lax.fori_loop(0, rows // 256, finish, 0)
    for c in stores:
        c.wait()
    for i in range(rows // 256):
        for c in tile_stores(i):
            c.wait()


def forward(names, length, tokens, scale_one, scale_two, cotangent, cosine, sine, wq, wk, wv, wm):
    rows, width = tokens.shape
    local = wq.shape[1]
    pairs = local // 128
    vmem = pl.BlockSpec(memory_space=pltpu.VMEM)
    hbm = pl.BlockSpec(memory_space=pl.ANY)
    half = jnp.bfloat16
    full = jnp.float32
    shapes = [
        ((pairs, rows, 128), half),
        ((pairs, rows, 128), half),
        ((pairs, rows, 128), half),
        ((pairs, rows, 128), half),
        ((pairs, 128, rows), half),
        ((2 * pairs, rows), full),
        ((rows, width), full),
        ((rows, width), half),
        ((16, width // 16, rows), half),
    ]
    return pl.pallas_call(
        functools.partial(forward_kernel, names),
        out_shape=[jax.ShapeDtypeStruct(*s) for s in shapes],
        in_specs=[pl.BlockSpec(memory_space=pltpu.SMEM)] + [vmem] * 3 + [hbm] * 7,
        out_specs=[hbm] * len(shapes),
        scratch_shapes=[pltpu.VMEM(*s) for s in shapes]
        + [
            pltpu.VMEM((rows, width), half),
            pltpu.VMEM((rows, 128), full),
            pltpu.VMEM((rows, 128), full),
            pltpu.VMEM((rows, width), half),
            pltpu.VMEM(wq.shape, half),
            pltpu.VMEM(wk.shape, half),
            pltpu.VMEM(wv.shape, half),
            pltpu.VMEM(wm.shape, half),
            pltpu.VMEM(wm.shape, half),
            pltpu.VMEM((pairs, 128, rows), half),
            pltpu.VMEM(wm.shape, full),
            pltpu.VMEM(wm.shape, full),
            pltpu.VMEM((pairs, rows, 128), full),
            pltpu.VMEM((pairs, rows, 128), full),
            pltpu.VMEM((rows, 128), full),
            pltpu.SemaphoreType.DMA((7,)),
            pltpu.SemaphoreType.DMA((7,)),
            pltpu.SemaphoreType.DMA((2, 4)),
            pltpu.SemaphoreType.DMA((1 + pairs,)),
            pltpu.SemaphoreType.DMA((1 + pairs,)),
        ],
        compiler_params=pltpu.CompilerParams(collective_id=1, has_side_effects=True, vmem_limit_bytes=58 * 2**20),
        name="forward",
    )(length, tokens, scale_one, scale_two, cotangent, cosine, sine, wq, wk, wv, wm)


ITEMS = 24
TILE = 256
RING = 5
HELD = 12
LAGS = (4, 6, 8, 10)
FIRSTS = (0, 8, 16, 18, 24)


def count_from(i, starts):
    total = 0
    for start in starts:
        total = total + jnp.where(i >= start, 1, 0)
    return total


def flip(index, weight):
    return index + weight * (1 - 2 * lax.rem(lax.div(index, weight), 2))


def weight_of(color, stage):
    k = lax.rem(color + stage, 3)
    return 1 + (k * (k + 1)) // 2


STARTS_Z = (2, 5, 10, 15, 19)


def color_of(i):
    turn = i - count_from(i, [p + 1 for p in STARTS_Z])
    on_z = sum(jnp.where(i == p, 1, 0) for p in STARTS_Z)
    return jnp.where(on_z == 1, 2, lax.rem(turn, 2))


def slot_of(i):
    return count_from(i, (8, 16)) - 2 * count_from(i, (18,))


def backward_kernel(
    names, length_ref, moment_ref, scale_one, scale_two,
    l_down, mid_in, heads, q_in, k_in, v_in, heads_t, lse_in, cosine, sine,
    merge_in, wq, wk, wv, tokens, hidden, cotangent, wu, wd,
    out, rows_out, tokens_out, layer_out, r_down, slope, r_up, hidden_grad,
    left, s1, r1, r2, r3, r4, rb, qkv, send_p, recv_p, ga, terms,
    msem, lsem, fsem, ssem, csem, psem, qsem, gsem, jsem, credit, credit_two, core_free,
):
    here = {n: lax.axis_index(n) for n in names}
    d = here[names[0]]

    def device(**moved):
        at = {**here, **moved}
        return tuple(at[n] for n in names)

    core = device(**{names[1]: 1 - here[names[1]]})

    def across(weight):
        return device(**{names[0]: flip(d, weight)})

    def absolute(r):
        total = 0
        for b in range(4):
            bit = lax.rem(lax.div(d, 2**b), 2)
            total = total + (2**b) * (1 - bit if (r >> b) & 1 else bit)
        return total

    def load_left(source, slot):
        for r in range(16):
            pltpu.make_async_copy(source.at[absolute(r)], left.at[slot, r], lsem).start()

    def left_loaded(slot):
        pltpu.make_async_copy(left.at[slot], left.at[slot], lsem).wait()

    def turn(values, slot, own):
        turned = values.T.astype(jnp.bfloat16)
        for c in range(16):
            left[slot, absolute(c), :, own] = turned[64 * c : 64 * c + 64]

    mid_load = pltpu.make_async_copy(mid_in, ga, msem)
    mid_load.start()
    load_left(l_down, 0)
    barrier = pltpu.get_barrier_semaphore()
    for weight in (1, 2, 4, 8):
        pl.semaphore_signal(barrier, inc=1, device_id=across(weight), device_id_type=MESH)
    pl.semaphore_signal(barrier, inc=1, device_id=core, device_id_type=MESH)
    pl.semaphore_wait(barrier, 5)

    def fetch(i, lane):
        slot = lax.rem(i, 2)
        target, sem = rb.at[lane, slot], fsem.at[lane, slot]
        for g, source in ((0, r_down), (1, r_up)):
            @pl.when((i >= FIRSTS[g]) & (i < FIRSTS[g + 1]))
            def _():
                col = pl.multiple_of((i - FIRSTS[g]) * TILE, TILE)
                pltpu.make_async_copy(source.at[:, pl.ds(col, TILE)], target, sem).start()

        @pl.when((i >= FIRSTS[2]) & (i < FIRSTS[3]))
        def _():
            for k in range(2):
                pltpu.make_async_copy(
                    heads.at[2 * (i - FIRSTS[2]) + k], target.at[:, pl.ds(128 * k, 128)], sem
                ).start()

        @pl.when(i >= FIRSTS[3])
        def _():
            pltpu.make_async_copy(qkv.at[i - FIRSTS[3]], target, sem).start()

    def fetched(i, lane):
        slot = lax.rem(i, 2)
        pltpu.make_async_copy(rb.at[lane, slot], rb.at[lane, slot], fsem.at[lane, slot]).wait()

    def product(i, first, lane):
        color, slot = color_of(i), slot_of(i)
        weights = [weight_of(color, s) for s in range(3)] + [8]
        rows = []
        for bits in range(8):
            r = first * weights[0] + sum(((bits >> (2 - k)) & 1) * weights[1 + k] for k in range(3))
            rows.append(left[slot, r])
        lhs = jnp.concatenate(rows, axis=0)
        return mm(lhs, rb[lane, lax.rem(i, 2)]).reshape(8, 64, TILE)

    def copy(i, s):
        weight = weight_of(color_of(i), s) if s < 3 else 8
        src = (s1.at[lax.rem(i, RING)], r1.at[lax.rem(i, HELD), pl.ds(4, 4)], r2.at[lax.rem(i, HELD), pl.ds(2, 2)], r3.at[i, pl.ds(1, 1)])[s]
        dst = (r1.at[lax.rem(i, HELD)], r2.at[lax.rem(i, HELD)], r3.at[i], r4.at[i])[s]
        return pltpu.make_async_remote_copy(
            src_ref=src, dst_ref=dst, send_sem=ssem.at[s, i], recv_sem=csem.at[s, i],
            device_id=across(weight), device_id_type=MESH,
        )

    def tick(i):
        e = i - LAGS[3]

        @pl.when((e >= 0) & (e < ITEMS))
        def _():
            copy(e, 3).wait_recv()
            out[e] = r4[e, 0] + r3[e, 0]

        c = i - LAGS[2]

        @pl.when((c >= 0) & (c < ITEMS))
        def _():
            copy(c, 2).wait_recv()
            r3[c] += r2[lax.rem(c, HELD), 0:2]
            copy(c, 3).start()
            copy(c, 2).wait_send()

            @pl.when(c + HELD < ITEMS)
            def _():
                color = color_of(c + HELD)
                pl.semaphore_signal(
                    credit_two.at[color], inc=1, device_id=across(weight_of(color, 1)), device_id_type=MESH
                )

        b = i - LAGS[1]

        @pl.when((b >= 0) & (b < ITEMS))
        def _():
            copy(b, 1).wait_recv()
            r2[lax.rem(b, HELD)] += r1[lax.rem(b, HELD), 0:4]
            copy(b, 2).start()
            copy(b, 1).wait_send()

            @pl.when(b + HELD < ITEMS)
            def _():
                color = color_of(b + HELD)
                pl.semaphore_signal(
                    credit.at[color], inc=1, device_id=across(weight_of(color, 0)), device_id_type=MESH
                )

        a = i - LAGS[0]

        @pl.when((a >= 0) & (a < ITEMS))
        def _():
            fetched(a, 1)
            copy(a, 0).wait_recv()
            r1[lax.rem(a, HELD)] += product(a, 0, 1)

            @pl.when(a >= HELD)
            def _():
                pl.semaphore_wait(credit_two.at[color_of(a)], 1)

            copy(a, 1).start()

            @pl.when(a + 2 < ITEMS)
            def _():
                fetch(a + 2, 1)

        @pl.when(i < ITEMS)
        def _():
            @pl.when(i >= RING)
            def _():
                copy(i - RING, 0).wait_send()

            @pl.when(i >= LAGS[0])
            def _():
                fetched(i, 0)

            s1[lax.rem(i, RING)] = product(i, 1, 0)

            @pl.when(i >= HELD)
            def _():
                pl.semaphore_wait(credit.at[color_of(i)], 1)

            copy(i, 0).start()

            @pl.when((i + 2 < ITEMS) & (i >= LAGS[0]))
            def _():
                fetch(i + 2, 0)

    rows, width = tokens.shape
    pairs = q_in.shape[0]
    length = length_ref[0]
    part = 256
    parts = rows // part
    half, full = jnp.bfloat16, jnp.float32

    def keep_of(at):
        return jnp.where(at + lax.broadcasted_iota(jnp.int32, (part, 1), 0) < length, 1.0, 0.0)

    def core_copy(use, i):
        return pltpu.make_async_remote_copy(
            src_ref=send_p.at[i], dst_ref=recv_p.at[i], send_sem=psem.at[use, i], recv_sem=qsem.at[use, i],
            device_id=core, device_id_type=MESH,
        )

    def core_sent(use):
        for i in range(parts):
            core_copy(use, i).wait_send()
        if use < 2:
            pl.semaphore_signal(core_free, inc=1, device_id=core, device_id_type=MESH)
            pl.semaphore_wait(core_free, 1)

    def norm_parts(values):
        centred = values - jnp.mean(values, axis=1, keepdims=True)
        inverse = lax.rsqrt(jnp.mean(centred * centred, axis=1, keepdims=True) + epsilon)
        return centred * inverse, inverse

    def norm_grad(grad, normed, inverse, scale):
        hat = grad * scale
        middle = jnp.mean(hat, axis=1, keepdims=True)
        return inverse * (hat - middle - normed * jnp.mean(hat * normed, axis=1, keepdims=True))

    def run_ticks(first, last):
        lax.fori_loop(first, last, lambda i, _: (tick(i), 0)[1], 0)

    def mlp(vu, vd, cot, wide, hid, gp, gh, wsem, usem, dsem, tsem, osem):
        tiles = wu.shape[1] // TILE

        def columns(k):
            return pl.ds(pl.multiple_of(k * TILE, TILE), TILE)

        def up_load(k):
            return pltpu.make_async_copy(wu.at[:, columns(k)], vu.at[:, columns(k)], usem.at[k])

        for k in range(2):
            up_load(k).start()
        down_load = pltpu.make_async_copy(wd, vd, wsem)

        def tile_stores(k, lane):
            slot = lax.rem(k, 2)
            return (
                pltpu.make_async_copy(rb.at[lane, slot], r_down.at[:, columns(k)], dsem.at[0, slot]),
                pltpu.make_async_copy(qkv.at[slot], slope.at[:, columns(k)], dsem.at[1, slot]),
            )

        def up_tile(k, lane):
            slot = lax.rem(k, 2)

            @pl.when(k >= 2)
            def _():
                for x in tile_stores(k - 2, lane):
                    x.wait()

            up_load(k).wait()

            @pl.when(k + 2 < tiles)
            def _():
                up_load(k + 2).start()

            for r in range(0, rows, 512):
                v = mm(ga[r : r + 512, :], vu[:, columns(k)])
                square = v * v
                t = jnp.tanh(0.7978845608028654 * v * (1.0 + 0.044715 * square))
                above = 0.5 * (1.0 + t)
                rb[lane, slot, r : r + 512, :] = (v * above).astype(half)
                qkv[slot, r : r + 512, :] = (
                    above + 0.5 * v * (1.0 - t * t) * (0.7978845608028654 * (1.0 + 0.134145 * square))
                ).astype(half)
            for x in tile_stores(k, lane):
                x.start()

        def tile(source, target, n, i):
            own = pl.ds(pl.multiple_of(i * part, part), part)
            slot = lax.rem(i, 2)
            return pltpu.make_async_copy(source.at[own, :], target.at[slot], tsem.at[n, slot])

        def stream(sources, i, body):
            for n, source, target in sources:
                tile(source, target, n, i).wait()

                @pl.when(i + 1 < parts)
                def _():
                    tile(source, target, n, i + 1).start()

            return body(i, pl.multiple_of(i * part, part), lax.rem(i, 2))

        def begin(sources):
            for n, source, target in sources:
                tile(source, target, n, jnp.int32(0)).start()

        mid_load.wait()
        left_loaded(0)

        def early(k, _):
            up_tile(k, 0)
            tick(k)
            return 0

        lax.fori_loop(0, LAGS[0], early, 0)
        down_load.start()
        lax.fori_loop(LAGS[0], tiles, lambda k, _: (up_tile(k, 1), 0)[1], 0)
        for k in (tiles - 2, tiles - 1):
            for x in tile_stores(k, 1):
                x.wait()
        for i in range(2):
            fetch(jnp.int32(i), 1)
            fetch(jnp.int32(LAGS[0] + i), 0)
        streams = ((0, cotangent, cot), (1, slope, wide))
        begin(streams)
        down_load.wait()

        def store_pre(i):
            own = pl.ds(pl.multiple_of(i * part, part), part)
            return pltpu.make_async_copy(gp, r_up.at[own, :], osem.at[0])

        def first(i, at, slot):
            x = (cot[slot].astype(full) * keep_of(at)).astype(half)
            g = mm_nt(x, vd[...]) * wide[slot].astype(full)

            @pl.when(i > 0)
            def _():
                store_pre(i - 1).wait()

            gp[...] = g.astype(half)
            store_pre(i).start()
            send_p[i] = mm_nt(gp[...], vu[...])
            core_copy(0, i).start()

            @pl.when(i < 2)
            def _():
                tick(LAGS[0] + i)

            return 0

        lax.fori_loop(0, parts, lambda i, _: stream(streams, i, first), 0)
        store_pre(parts - 1).wait()
        run_ticks(LAGS[0] + 2, LAGS[0] + 4)
        streams_two = ((0, cotangent, cot), (2, hidden, hid))
        begin(streams_two)

        def store_hidden(i):
            own = pl.ds(pl.multiple_of(i * part, part), part)
            return pltpu.make_async_copy(gh, hidden_grad.at[own, :], osem.at[1])

        def second(i, at, slot, total):
            own = pl.ds(at, part)
            normed, inverse = norm_parts(hid[slot])
            turn(normed * scale_two[...], 1, own)
            core_copy(0, i).wait_recv()
            grad = send_p[i] + recv_p[i]

            @pl.when(i > 0)
            def _():
                store_hidden(i - 1).wait()

            gh[...] = cot[slot].astype(full) * keep_of(at) + norm_grad(grad, normed, inverse, scale_two[...])
            store_hidden(i).start()
            ga[own, :] = gh[...].astype(half)
            turn(gh[...], 2, own)
            return total + jnp.sum(grad * normed, axis=0, keepdims=True)

        term = lax.fori_loop(
            0, parts, lambda i, total: stream(streams_two, i, functools.partial(second, total=total)),
            jnp.zeros((1, width), full),
        )
        for j in range(8):
            terms[0, 8 + j : 9 + j, :] = term[:, 128 * j : 128 * j + 128]
        store_hidden(parts - 1).wait()
        core_sent(0)
        streams_three = ((1, r_down, wide),)
        begin(streams_three)

        def third(i, at, slot):
            send_p[i] = mm(wide[slot], vd[...])
            core_copy(1, i).start()
            return 0

        lax.fori_loop(0, parts, lambda i, _: stream(streams_three, i, third), 0)
        streams_four = ((2, hidden, hid),)
        begin(streams_four)
        tick(jnp.int32(LAGS[0] + 4))

        def store_layer(i):
            own = pl.ds(pl.multiple_of(i * part, part), part)
            return pltpu.make_async_copy(cot.at[0], layer_out.at[own, :], osem.at[0])

        def fourth(i, at, slot):
            core_copy(1, i).wait_recv()

            @pl.when(i > 0)
            def _():
                store_layer(i - 1).wait()

            cot[0] = ((hid[slot] + (send_p[i] + recv_p[i])) * keep_of(at)).astype(half)
            store_layer(i).start()
            return 0

        lax.fori_loop(0, parts, lambda i, _: stream(streams_four, i, fourth), 0)
        store_layer(parts - 1).wait()
        core_sent(1)

    pl.run_scoped(
        mlp,
        pltpu.VMEM(wu.shape, half),
        pltpu.VMEM(wd.shape, half),
        pltpu.VMEM((2, part, width), half),
        pltpu.VMEM((2, part, wu.shape[1]), half),
        pltpu.VMEM((2, part, width), full),
        pltpu.VMEM((part, wu.shape[1]), half),
        pltpu.VMEM((part, width), full),
        pltpu.SemaphoreType.DMA,
        pltpu.SemaphoreType.DMA((wu.shape[1] // TILE,)),
        pltpu.SemaphoreType.DMA((2, 2)),
        pltpu.SemaphoreType.DMA((3, 2)),
        pltpu.SemaphoreType.DMA((2,)),
    )

    def attention(q, k, v, o_t, lse, wm, cos, sin, bias, do, do_t, kh, vh, k_t, dq_t, asem):
        loads = [
            pltpu.make_async_copy(a, b, asem.at[n])
            for n, (a, b) in enumerate(
                ((q_in, q), (k_in, k), (v_in, v), (heads_t, o_t), (lse_in, lse), (merge_in, wm),
                 (cosine, cos), (sine, sin))
            )
        ]
        for x in loads:
            x.start()
        for x in loads:
            x.wait()
        place = lax.broadcasted_iota(jnp.int32, (rows, 128), 0)
        bias[...] = (jnp.where(place < length, 1.0, 0.0) - 1.0) * 1000000000.0
        lane = lax.broadcasted_iota(jnp.int32, (rows, 128), 1) < HEAD
        block = 256

        def unrotate_lanes(y):
            return (y * cos[...] - swap_halves(y) * sin[...]).astype(jnp.bfloat16)

        def pair(p, _):
            weight = wm[pl.ds(pl.multiple_of(128 * p, 128), 128), :]
            do[...] = mm_nt(ga[...], weight).astype(jnp.bfloat16)
            do_t[...] = mm_nt(weight, ga[...]).astype(jnp.bfloat16)
            k_t[...] = (k[p].astype(jnp.float32) * 0.125).T.astype(jnp.bfloat16)
            product_t = do_t[...].astype(jnp.float32) * o_t[p].astype(jnp.float32)
            dks, dvs = [], []
            for h in range(2):
                tick(LAGS[0] + 5 + 2 * p + h)
                delta = jnp.sum(product_t[HEAD * h : HEAD * h + HEAD], axis=0, keepdims=True)
                own = lane == (h == 0)
                kh[...] = jnp.where(own, k[p].astype(jnp.float32) * 0.125, 0.0).astype(jnp.bfloat16)
                vh[...] = jnp.where(own, v[p].astype(jnp.float32), 0.0).astype(jnp.bfloat16)
                dk = jnp.zeros((rows, 128), jnp.float32)
                dv = jnp.zeros((rows, 128), jnp.float32)
                for b in range(0, rows, block):
                    cols = slice(b, b + block)
                    qb = q[p, cols, :]
                    s = mm_nt(kh[...], qb) + bias[:, :1]
                    soft = jnp.exp(s - lse[pl.ds(2 * p + h, 1), cols])
                    ds = soft * (mm(vh[...], do_t[:, cols]) - delta[:, cols])
                    ds = ds.astype(jnp.bfloat16)
                    dv = dv + mm(soft.astype(jnp.bfloat16), do[cols, :])
                    dk = dk + mm(ds, qb)
                    dq_t[HEAD * h : HEAD * h + HEAD, cols] = mm(k_t[HEAD * h : HEAD * h + HEAD, :], ds)
                dks.append(dk)
                dvs.append(dv)
            quad = 3 * lax.div(p, 2)
            at = pl.ds(pl.multiple_of(128 * lax.rem(p, 2), 128), 128)
            qkv[quad, :, at] = unrotate_lanes(dq_t[...].T)
            qkv[quad + 1, :, at] = unrotate_lanes(jnp.where(lane, dks[0], dks[1]) * 0.125)
            qkv[quad + 2, :, at] = jnp.where(lane, dvs[0], dvs[1]).astype(jnp.bfloat16)
            return 0

        lax.fori_loop(0, pairs, pair, 0)

    pl.run_scoped(
        attention,
        pltpu.VMEM((pairs, rows, 128), half),
        pltpu.VMEM((pairs, rows, 128), half),
        pltpu.VMEM((pairs, rows, 128), half),
        pltpu.VMEM((pairs, 128, rows), half),
        pltpu.VMEM((2 * pairs, rows), full),
        pltpu.VMEM(merge_in.shape, half),
        pltpu.VMEM((rows, 128), full),
        pltpu.VMEM((rows, 128), full),
        pltpu.VMEM((rows, 128), full),
        pltpu.VMEM((rows, 128), half),
        pltpu.VMEM((128, rows), half),
        pltpu.VMEM((rows, 128), half),
        pltpu.VMEM((rows, 128), half),
        pltpu.VMEM((128, rows), half),
        pltpu.VMEM((128, rows), full),
        pltpu.SemaphoreType.DMA((10,)),
    )

    def inner(vq, vk, vv, x_in, gh, to, sem, hsem, osem):
        loads = [
            pltpu.make_async_copy(a, b, sem.at[n])
            for n, (a, b) in enumerate(((wq, vq), (wk, vk), (wv, vv), (tokens, x_in)))
        ]
        for x in loads:
            x.start()
        for x in loads:
            x.wait()

        def send(i, _):
            at = pl.multiple_of(i * part, part)
            own = pl.ds(at, part)
            total = None
            for quad in range(2):
                for n, w in enumerate((vq, vk, vv)):
                    term = mm_nt(qkv[3 * quad + n, own, :], w[:, TILE * quad : TILE * quad + TILE])
                    total = term if total is None else total + term
            send_p[i] = total
            core_copy(2, i).start()
            normed, _ = norm_parts(x_in[own, :].astype(full) * keep_of(at))
            turn(normed * scale_one[...], 0, own)

            @pl.when(i == 1)
            def _():
                tick(LAGS[0] + 13)

            return 0

        lax.fori_loop(0, parts, send, 0)

        def store_tokens(i):
            own = pl.ds(pl.multiple_of(i * part, part), part)
            return pltpu.make_async_copy(to, tokens_out.at[own, :], osem)

        def take(i, total):
            at = pl.multiple_of(i * part, part)
            own = pl.ds(at, part)
            hidden_copy = pltpu.make_async_copy(hidden_grad.at[own, :], gh, hsem)
            hidden_copy.start()

            @pl.when(i < 2)
            def _():
                tick(LAGS[0] + 14 + i)

            core_copy(2, i).wait_recv()
            grad = send_p[i] + recv_p[i]
            keep = keep_of(at)
            normed, inverse = norm_parts(x_in[own, :].astype(full) * keep)
            back = norm_grad(grad, normed, inverse, scale_one[...])
            hidden_copy.wait()

            @pl.when(i > 0)
            def _():
                store_tokens(i - 1).wait()

            to[...] = ((gh[...] + back) * keep).astype(half)
            store_tokens(i).start()
            return total + jnp.sum(grad * normed, axis=0, keepdims=True)

        first = lax.fori_loop(0, parts, take, jnp.zeros((1, width), full))
        store_tokens(parts - 1).wait()
        core_sent(2)
        for j in range(8):
            terms[0, j : j + 1, :] = first[:, 128 * j : 128 * j + 128]
        terms[0, 16:24, :] = jnp.full((8, 128), moment_ref[0].astype(full), full)

    pl.run_scoped(
        inner,
        pltpu.VMEM(wq.shape, half),
        pltpu.VMEM(wk.shape, half),
        pltpu.VMEM(wv.shape, half),
        pltpu.VMEM((rows, width), half),
        pltpu.VMEM((part, width), full),
        pltpu.VMEM((part, width), half),
        pltpu.SemaphoreType.DMA((4,)),
        pltpu.SemaphoreType.DMA,
        pltpu.SemaphoreType.DMA,
    )
    done = LAGS[0] + 16
    for stage in range(4):
        held = 2**stage
        exchange = pltpu.make_async_remote_copy(
            src_ref=terms.at[pl.ds(0, held)], dst_ref=terms.at[pl.ds(held, held)],
            send_sem=gsem.at[stage], recv_sem=jsem.at[stage], device_id=across(held), device_id_type=MESH,
        )
        exchange.start()
        tick(jnp.int32(done + stage))
        exchange.wait()
    table_rows = rows_out.shape[1]
    upper = lax.rem(d, 2) == 1
    places = lax.broadcasted_iota(jnp.int32, (table_rows, 128), 0).astype(full)
    total = jnp.zeros((table_rows, 128), full)
    for n in range(16):
        row = []
        for base in (0, 8):
            piece = terms[n, pl.ds(base + lax.div(d, 2), 1), :]
            row.append(jnp.where(upper, piece[:, 64:], piece[:, :64]))
        total = total + jnp.where(places == terms[n, 16:17, :], jnp.concatenate(row, axis=1), 0.0)
    rows_out[...] = total.T
    run_ticks(done + 4, ITEMS + LAGS[3])

    def drain(i, _):
        @pl.when(i >= ITEMS - RING)
        def _():
            copy(i, 0).wait_send()

        copy(i, 3).wait_send()
        return 0

    lax.fori_loop(0, ITEMS, drain, 0)


def backward(names, table_rows, length, moment, scale_one, scale_two, *arrays):
    tokens, up = arrays[-5], arrays[-2]
    rows, width = tokens.shape
    smem = pl.BlockSpec(memory_space=pltpu.SMEM)
    vmem = pl.BlockSpec(memory_space=pltpu.VMEM)
    hbm = pl.BlockSpec(memory_space=pl.ANY)
    half, full = jnp.bfloat16, jnp.float32
    dma = pltpu.SemaphoreType.DMA
    return pl.pallas_call(
        functools.partial(backward_kernel, names),
        out_shape=[
            jax.ShapeDtypeStruct((ITEMS, 64, TILE), full),
            jax.ShapeDtypeStruct((128, table_rows), full),
            jax.ShapeDtypeStruct((rows, width), half),
            jax.ShapeDtypeStruct((rows, width), half),
            jax.ShapeDtypeStruct((rows, up.shape[1]), half),
            jax.ShapeDtypeStruct((rows, up.shape[1]), half),
            jax.ShapeDtypeStruct((rows, up.shape[1]), half),
            jax.ShapeDtypeStruct((rows, width), full),
        ],
        in_specs=[smem] * 2 + [vmem] * 2 + [hbm] * len(arrays),
        out_specs=[vmem] * 2 + [hbm] * 6,
        scratch_shapes=[
            pltpu.VMEM((3, 16, 64, rows), half),
            pltpu.VMEM((RING, 8, 64, TILE), full),
            pltpu.VMEM((HELD, 8, 64, TILE), full),
            pltpu.VMEM((HELD, 4, 64, TILE), full),
            pltpu.VMEM((ITEMS, 2, 64, TILE), full),
            pltpu.VMEM((ITEMS, 1, 64, TILE), full),
            pltpu.VMEM((2, 2, rows, TILE), half),
            pltpu.VMEM((6, rows, TILE), half),
            pltpu.VMEM((rows // 256, 256, width), full),
            pltpu.VMEM((rows // 256, 256, width), full),
            pltpu.VMEM((rows, width), half),
            pltpu.VMEM((16, 24, 128), full),
            dma,
            dma,
            dma((2, 2)),
            dma((4, ITEMS)),
            dma((4, ITEMS)),
            dma((3, 4)),
            dma((3, 4)),
            dma((4,)),
            dma((4,)),
            pltpu.SemaphoreType.REGULAR((3,)),
            pltpu.SemaphoreType.REGULAR((3,)),
            pltpu.SemaphoreType.REGULAR,
        ],
        compiler_params=pltpu.CompilerParams(
            collective_id=0, has_side_effects=True, vmem_limit_bytes=60 * 2**20
        ),
        name="backward",
    )(length, moment, scale_one, scale_two, *arrays)


def finish_kernel(
    pieces_in, tables_in, tokens_in, layer_in,
    layer_out, tokens_out, grad_q, grad_k, grad_v, grad_m, grad_u, grad_d, first, second,
    pieces, tables, held, isem, osem,
):
    parts = held.shape[1]
    step = layer_in.shape[0] // parts
    incoming, outgoing = [], []

    def move(source, keep, target):
        n = len(incoming)
        incoming.append(pltpu.make_async_copy(source, keep, isem.at[n]))
        outgoing.append(pltpu.make_async_copy(keep, target, osem.at[n]))

    for n, (source, target) in enumerate(((layer_in, layer_out), (tokens_in, tokens_out))):
        for k in range(parts):
            own = pl.ds(k * step, step)
            move(source.at[own, :], held.at[n, k], target.at[own, :])
    targets = [(grad_d, k) for k in range(8)] + [(grad_u, k) for k in range(8)] + [(grad_m, k) for k in range(2)]
    targets += [(ref, k) for k in range(2) for ref in (grad_q, grad_k, grad_v)]
    for n, (ref, k) in enumerate(targets):
        move(pieces_in.at[n], pieces.at[n], ref.at[:, pl.ds(TILE * k, TILE)])
    count = first.shape[0]
    for k, ref in enumerate((first, second)):
        own = pl.ds(k * count, count)
        move(tables_in.at[own, :], tables.at[own, :], ref)
    for c in incoming:
        c.start()
    for a, b in zip(incoming, outgoing):
        a.wait()
        b.start()
    for c in outgoing:
        c.wait()


def finish(pieces, tables, tokens, layer):
    hbm = pl.BlockSpec(memory_space=pl.ANY)
    full = jnp.float32
    rows, width = layer.shape
    table_rows = tables.shape[1]
    shapes = [(64, 512)] * 4 + [(64, 2048), (64, 2048), (64, table_rows), (64, table_rows)]
    layer, tokens, *grads = pl.pallas_call(
        finish_kernel,
        out_shape=[jax.ShapeDtypeStruct(a.shape, a.dtype) for a in (layer, tokens)]
        + [jax.ShapeDtypeStruct(s, full) for s in shapes],
        in_specs=[hbm] * 4,
        out_specs=[hbm] * (2 + len(shapes)),
        scratch_shapes=[
            pltpu.VMEM(pieces.shape, full),
            pltpu.VMEM(tables.shape, full),
            pltpu.VMEM((2, 4, rows // 4, width), layer.dtype),
            pltpu.SemaphoreType.DMA((34,)),
            pltpu.SemaphoreType.DMA((34,)),
        ],
        name="finish",
    )(pieces, tables, tokens, layer)
    query, key, value, merge, up, down, first, second = grads
    return layer[None], tokens[None], query, key, value, merge.T, up, down.T, first.T, second.T


def fast_body(
    tokens,
    cotangent,
    lengths,
    noise_times,
    query_weight,
    key_weight,
    value_weight,
    merge_weight,
    up_weight,
    down_weight,
    first_scales,
    second_scales,
):
    tokens, cotangent = tokens[0], cotangent[0]
    rows, width = tokens.shape
    names = ("dp", "tensor")
    moment = noise_times[0]
    scale_one = lax.dynamic_slice_in_dim(first_scales, moment, 1, axis=0)
    scale_two = lax.dynamic_slice_in_dim(second_scales, moment, 1, axis=0)
    cosine, sine = (jnp.asarray(a) for a in rope_lanes(rows))
    query, key, value, heads, heads_t, lse, hidden, normal_mid, mlp_t = forward(
        names, lengths, tokens, scale_one, scale_two, cotangent, cosine, sine,
        query_weight, key_weight, value_weight, merge_weight,
    )
    pieces, tables, grad_tokens, layer_output, *_ = backward(
        names, first_scales.shape[0], lengths, noise_times, scale_one, scale_two,
        mlp_t, normal_mid, heads, query, key, value, heads_t, lse, cosine, sine,
        merge_weight, query_weight, key_weight, value_weight, tokens, hidden, cotangent, up_weight, down_weight,
    )
    return finish(pieces, tables, grad_tokens, layer_output)


def body(
    tokens,
    cotangent,
    lengths,
    noise_times,
    query_weight,
    key_weight,
    value_weight,
    merge_weight,
    up_weight,
    down_weight,
    first_scales,
    second_scales,
):
    seq_count, length, width = tokens.shape
    local_width = query_weight.shape[1]
    local_heads = local_width // HEAD
    table_rows = first_scales.shape[0]
    flat_rows = seq_count * length
    scale_factor = 1.0 / math.sqrt(HEAD)
    block_rows = min(512, length)
    head_shape = (seq_count, length, local_heads, HEAD)
    row_mask = (jnp.arange(length, dtype=jnp.int32)[None, :] < lengths[:, None]).astype(jnp.float32)
    key_bias = (row_mask - 1.0) * 1000000000.0
    one_hot = (noise_times[:, None] == jnp.arange(table_rows, dtype=jnp.int32)[None, :]).astype(
        jnp.float32
    )
    scale_one = jnp.dot(one_hot, first_scales, precision=highest)
    scale_two = jnp.dot(one_hot, second_scales, precision=highest)
    cos_table, sin_table = rope_tables(length, HEAD)
    inputs = tokens.astype(jnp.float32) * row_mask[:, :, None]
    normed_one, inv_one = normalize(inputs)
    normal_in = (normed_one * scale_one[:, None, :]).astype(jnp.bfloat16).reshape(flat_rows, width)
    queries = jnp.dot(normal_in, query_weight, preferred_element_type=jnp.float32).reshape(
        head_shape
    )
    key_proj = jnp.dot(normal_in, key_weight, preferred_element_type=jnp.float32).reshape(
        head_shape
    )
    value_rows = (
        jnp.dot(normal_in, value_weight, preferred_element_type=jnp.float32)
        .astype(jnp.bfloat16)
        .reshape(head_shape)
    )
    query_rot = rotate(queries, cos_table, sin_table).astype(jnp.bfloat16)
    key_rot = rotate(key_proj, cos_table, sin_table).astype(jnp.bfloat16)
    attended = []
    log_sums = []
    for offset in range(0, length, block_rows):
        scores = block_scores(
            query_rot[:, offset : offset + block_rows], key_rot, key_bias, scale_factor
        )
        peak_score = jnp.max(scores, axis=-1, keepdims=True)
        exponent = jnp.exp(scores - peak_score)
        totals = jnp.sum(exponent, axis=-1, keepdims=True)
        soft_weights = (exponent / totals).astype(jnp.bfloat16)
        log_sums.append(peak_score + jnp.log(totals))
        attended.append(
            jnp.einsum(
                "shqk,skhd->sqhd", soft_weights, value_rows, preferred_element_type=jnp.float32
            )
        )
    heads_out = (
        jnp.concatenate(attended, axis=1).astype(jnp.bfloat16).reshape(flat_rows, local_width)
    )
    attn_part = jnp.dot(heads_out, merge_weight, preferred_element_type=jnp.float32)
    attn_total = lax.psum(attn_part, "tensor")
    hidden_one = inputs + attn_total.reshape(seq_count, length, width)
    normed_two, inv_two = normalize(hidden_one)
    normal_mid = (normed_two * scale_two[:, None, :]).astype(jnp.bfloat16).reshape(flat_rows, width)
    pre_act = jnp.dot(normal_mid, up_weight, preferred_element_type=jnp.float32)
    activated = gelu_tanh(pre_act).astype(jnp.bfloat16)
    mlp_part = jnp.dot(activated, down_weight, preferred_element_type=jnp.float32)
    mlp_total = lax.psum(mlp_part, "tensor")
    layer_output = (
        (hidden_one + mlp_total.reshape(seq_count, length, width)) * row_mask[:, :, None]
    ).astype(jnp.bfloat16)
    grad_final = cotangent.astype(jnp.float32) * row_mask[:, :, None]
    grad_mlp = grad_final.astype(jnp.bfloat16).reshape(flat_rows, width)
    grad_down = jnp.dot(activated.T, grad_mlp, preferred_element_type=jnp.float32)
    grad_act = jnp.dot(grad_mlp, down_weight.T, preferred_element_type=jnp.float32)
    unused_value, gelu_back = jax.vjp(gelu_tanh, pre_act)
    grad_pre = gelu_back(grad_act)[0].astype(jnp.bfloat16)
    grad_up = jnp.dot(normal_mid.T, grad_pre, preferred_element_type=jnp.float32)
    mid_part = jnp.dot(grad_pre, up_weight.T, preferred_element_type=jnp.float32)
    grad_mid = lax.psum(mid_part, "tensor").reshape(seq_count, length, width)
    grad_hat_two, scale_grad_two = norm_back(grad_mid, normed_two, inv_two, scale_two)
    grad_hidden = grad_final + grad_hat_two
    grad_second = jnp.dot(one_hot.T, scale_grad_two, precision=highest)
    grad_attn = grad_hidden.astype(jnp.bfloat16).reshape(flat_rows, width)
    grad_merge = jnp.dot(heads_out.T, grad_attn, preferred_element_type=jnp.float32)
    grad_heads = (
        jnp.dot(grad_attn, merge_weight.T, preferred_element_type=jnp.float32)
        .astype(jnp.bfloat16)
        .reshape(head_shape)
    )
    grad_keys = jnp.zeros(head_shape, jnp.float32)
    grad_values = jnp.zeros(head_shape, jnp.float32)
    query_grads = []
    for block_index in range(len(log_sums)):
        offset = block_index * block_rows
        query_block = query_rot[:, offset : offset + block_rows]
        grad_block = grad_heads[:, offset : offset + block_rows]
        scores = block_scores(query_block, key_rot, key_bias, scale_factor)
        soft_weights = jnp.exp(scores - log_sums[block_index])
        grad_soft = jnp.einsum(
            "sqhd,skhd->shqk", grad_block, value_rows, preferred_element_type=jnp.float32
        )
        grad_values = grad_values + jnp.einsum(
            "shqk,sqhd->skhd",
            soft_weights.astype(jnp.bfloat16),
            grad_block,
            preferred_element_type=jnp.float32,
        )
        grad_scores = (
            soft_weights * (grad_soft - jnp.sum(soft_weights * grad_soft, axis=-1, keepdims=True))
        ).astype(jnp.bfloat16)
        query_grads.append(
            jnp.einsum("shqk,skhd->sqhd", grad_scores, key_rot, preferred_element_type=jnp.float32)
            * scale_factor
        )
        grad_keys = (
            grad_keys
            + jnp.einsum(
                "shqk,sqhd->skhd", grad_scores, query_block, preferred_element_type=jnp.float32
            )
            * scale_factor
        )
    query_back = (
        unrotate(jnp.concatenate(query_grads, axis=1), cos_table, sin_table)
        .astype(jnp.bfloat16)
        .reshape(flat_rows, local_width)
    )
    key_back = (
        unrotate(grad_keys, cos_table, sin_table)
        .astype(jnp.bfloat16)
        .reshape(flat_rows, local_width)
    )
    value_back = grad_values.astype(jnp.bfloat16).reshape(flat_rows, local_width)
    grad_query = jnp.dot(normal_in.T, query_back, preferred_element_type=jnp.float32)
    grad_key = jnp.dot(normal_in.T, key_back, preferred_element_type=jnp.float32)
    grad_value = jnp.dot(normal_in.T, value_back, preferred_element_type=jnp.float32)
    inner_part = jnp.dot(query_back, query_weight.T, preferred_element_type=jnp.float32)
    inner_part = inner_part + jnp.dot(key_back, key_weight.T, preferred_element_type=jnp.float32)
    inner_part = inner_part + jnp.dot(
        value_back, value_weight.T, preferred_element_type=jnp.float32
    )
    grad_inner = lax.psum(inner_part, "tensor").reshape(seq_count, length, width)
    grad_hat_one, scale_grad_one = norm_back(grad_inner, normed_one, inv_one, scale_one)
    grad_tokens = ((grad_hidden + grad_hat_one) * row_mask[:, :, None]).astype(jnp.bfloat16)
    grad_first = jnp.dot(one_hot.T, scale_grad_one, precision=highest)
    summed = (
        lax.psum_scatter(grad_query, "dp", scatter_dimension=0, tiled=True),
        lax.psum_scatter(grad_key, "dp", scatter_dimension=0, tiled=True),
        lax.psum_scatter(grad_value, "dp", scatter_dimension=0, tiled=True),
        lax.psum_scatter(grad_merge, "dp", scatter_dimension=1, tiled=True),
        lax.psum_scatter(grad_up, "dp", scatter_dimension=0, tiled=True),
        lax.psum_scatter(grad_down, "dp", scatter_dimension=1, tiled=True),
        lax.psum_scatter(grad_first, "dp", scatter_dimension=1, tiled=True),
        lax.psum_scatter(grad_second, "dp", scatter_dimension=1, tiled=True),
    )
    return (
        layer_output,
        grad_tokens,
        summed[0],
        summed[1],
        summed[2],
        summed[3],
        summed[4],
        summed[5],
        summed[6],
        summed[7],
    )


def solution(mesh):
    fast = mesh.shape["dp"] == 16 and mesh.shape["tensor"] == 2
    return jax.shard_map(
        fast_body if fast else body,
        mesh=mesh,
        in_specs=(
            P("dp", None, None),
            P("dp", None, None),
            P("dp"),
            P("dp"),
            P(None, "tensor"),
            P(None, "tensor"),
            P(None, "tensor"),
            P("tensor", None),
            P(None, "tensor"),
            P("tensor", None),
            P(),
            P(),
        ),
        out_specs=(
            P("dp", None, None),
            P("dp", None, None),
            P("dp", "tensor"),
            P("dp", "tensor"),
            P("dp", "tensor"),
            P("tensor", "dp"),
            P("dp", "tensor"),
            P("tensor", "dp"),
            P(None, "dp"),
            P(None, "dp"),
        ),
        check_vma=False,
    )
```

```python
import functools
import math

import jax
import jax.numpy as jnp
import numpy as np
from jax import lax
from jax.experimental import pallas as pl
from jax.experimental.pallas import tpu as pltpu
from jax.sharding import PartitionSpec as P

HEAD = 64
MESH = pl.DeviceIdType.MESH


epsilon = 1e-05
highest = lax.Precision.HIGHEST


def gelu_tanh(values):
    return (
        0.5
        * values
        * (1.0 + jnp.tanh(0.7978845608028654 * (values + 0.044715 * values * values * values)))
    )


def rope_tables(length, head_size):
    halves = head_size // 2
    places = jnp.arange(length, dtype=jnp.float32)[:, None]
    frequency = jnp.exp(
        jnp.arange(halves, dtype=jnp.float32) * (-2.0 * math.log(10000.0) / head_size)
    )
    angles = places * frequency[None, :]
    return (jnp.cos(angles), jnp.sin(angles))


def rotate(values, cos_table, sin_table):
    halves = values.shape[-1] // 2
    first_half = values[..., :halves]
    second_half = values[..., halves:]
    cosine = cos_table[:, None, :]
    sine_part = sin_table[:, None, :]
    return jnp.concatenate(
        [
            first_half * cosine - second_half * sine_part,
            second_half * cosine + first_half * sine_part,
        ],
        axis=-1,
    )


def unrotate(gradient, cos_table, sin_table):
    halves = gradient.shape[-1] // 2
    first_half = gradient[..., :halves]
    second_half = gradient[..., halves:]
    cosine = cos_table[:, None, :]
    sine_part = sin_table[:, None, :]
    return jnp.concatenate(
        [
            first_half * cosine + second_half * sine_part,
            second_half * cosine - first_half * sine_part,
        ],
        axis=-1,
    )


def normalize(values):
    centred = values - jnp.mean(values, axis=-1, keepdims=True)
    inv_std = lax.rsqrt(jnp.mean(centred * centred, axis=-1, keepdims=True) + epsilon)
    return (centred * inv_std, inv_std)


def norm_back(grad_norm, normed, inv_std, scale_rows):
    grad_hat = grad_norm * scale_rows[:, None, :]
    grad_scale = jnp.sum(grad_norm * normed, axis=1)
    mean_grad = jnp.mean(grad_hat, axis=-1, keepdims=True)
    mean_cross = jnp.mean(grad_hat * normed, axis=-1, keepdims=True)
    return (inv_std * (grad_hat - mean_grad - normed * mean_cross), grad_scale)


def block_scores(query_block, key_rot, key_bias, scale_factor):
    scores = jnp.einsum("sqhd,skhd->shqk", query_block, key_rot, preferred_element_type=jnp.float32)
    return scores * scale_factor + key_bias[:, None, None, :]


def rope_lanes(length):
    halves = HEAD // 2
    places = np.arange(length, dtype=np.float64)[:, None]
    frequency = np.exp(np.arange(halves) * (-2.0 * math.log(10000.0) / HEAD))
    angles = places * frequency[None, :]
    cosine, sine = np.cos(angles), np.sin(angles)
    return (
        np.concatenate([cosine] * 4, axis=1).astype(np.float32),
        np.concatenate([-sine, sine] * 2, axis=1).astype(np.float32),
    )


def swap_halves(values):
    lanes = lax.broadcasted_iota(jnp.int32, values.shape, 1)
    first = lax.rem(lanes, HEAD) < HEAD // 2
    half = HEAD // 2
    return jnp.where(first, pltpu.roll(values, 128 - half, 1), pltpu.roll(values, half, 1))


def centre(values):
    middle = jnp.mean(values, axis=1, keepdims=True)
    centred = values - middle
    inverse = lax.rsqrt(jnp.mean(centred * centred, axis=1, keepdims=True) + epsilon)
    return centred * inverse


NT = (((1,), (1,)), ((), ()))


def mm(a, b):
    return jnp.dot(a, b, preferred_element_type=jnp.float32)


def mm_nt(a, b):
    return lax.dot_general(a, b, NT, preferred_element_type=jnp.float32)


def forward_kernel(
    names, length_ref, moment_ref, tokens, first_in, second_in, cotangent_in, cosine_in, sine_in, wq, wk, wv, wm,
    q_hbm, k_hbm, v_hbm, heads_hbm, heads_t_hbm, lse_hbm, hidden_hbm, mid_hbm, mlp_t_hbm, one_hbm, two_hbm,
    q_out, k_out, v_out, heads, heads_t, lse, hidden, mid, mlp_t, scale_one, scale_two, cotangent, cosine, sine,
    first_scales, second_scales, nin, vq, vk, vv, vm, other_m, v_t, send_m, recv_m, send_o, recv_o, bias, wsem, osem, tsem, ssem, rsem,
):
    rows, width = tokens.shape
    pairs = q_out.shape[0]
    here = {n: lax.axis_index(n) for n in names}
    other = {**here, names[1]: 1 - here[names[1]]}
    other = tuple(other[n] for n in names)
    loads = [
        pltpu.make_async_copy(a, b, wsem.at[i])
        for i, (a, b) in enumerate(
            ((first_in, first_scales), (wq, vq), (cosine_in, cosine), (sine_in, sine), (wk, vk), (wv, vv), (wm, vm),
             (cotangent_in, cotangent), (second_in, second_scales))
        )
    ]
    for c in loads[:6]:
        c.start()
    barrier = pltpu.get_barrier_semaphore()
    pl.semaphore_signal(barrier, inc=1, device_id=other, device_id_type=MESH)
    pl.semaphore_wait(barrier, 1)
    length = length_ref[0]

    def place(start, count):
        return start + lax.broadcasted_iota(jnp.int32, (count, 1), 0)

    def mask_of(start, count):
        return jnp.where(place(start, count) < length, 1.0, 0.0)

    bias[...] = jnp.broadcast_to((mask_of(0, rows) - 1.0) * 1000000000.0, (rows, 128))

    loads[0].wait()
    scale_one[...] = first_scales[pl.ds(moment_ref[0], 1), :]

    def norm_rows(i, _):
        at = pl.multiple_of(i * 128, 128)
        x = tokens[pl.ds(at, 128), :].astype(jnp.float32) * mask_of(at, 128)
        nin[pl.ds(at, 128), :] = (centre(x) * scale_one[...]).astype(jnp.bfloat16)
        return 0

    lax.fori_loop(0, rows // 128, norm_rows, 0)
    for c in loads[6:]:
        c.start()
    for c in loads[1:6]:
        c.wait()

    def project(i, _):
        at = pl.multiple_of(i * 256, 256)
        own = pl.ds(at, 256)
        x = nin[own, :]
        c, s = cosine[own, :], sine[own, :]
        for ref, w in ((q_out, vq), (k_out, vk)):
            y = mm(x, w[...])
            for p in range(pairs):
                part = y[:, 128 * p : 128 * p + 128]
                ref[p, own, :] = (part * c + swap_halves(part) * s).astype(jnp.bfloat16)
        y = mm(x, vv[...])
        for p in range(pairs):
            part = y[:, 128 * p : 128 * p + 128]
            v_out[p, own, :] = part.astype(jnp.bfloat16)
            v_t[p, :, own] = part.T.astype(jnp.bfloat16)
        return 0

    lax.fori_loop(0, rows // 256, project, 0)
    stores = [
        pltpu.make_async_copy(a, b, osem.at[i])
        for i, (a, b) in enumerate(
            ((q_out, q_hbm), (k_out, k_hbm), (v_out, v_hbm), (heads, heads_hbm), (heads_t, heads_t_hbm), (lse, lse_hbm),
             (mlp_t, mlp_t_hbm), (scale_one, one_hbm), (scale_two, two_hbm))
        )
    ]
    for c in stores[:3]:
        c.start()
    for c in loads[6:]:
        c.wait()
    scale_two[...] = second_scales[pl.ds(moment_ref[0], 1), :]
    send_m[...] = vm[...].astype(jnp.float32)
    merge_copy = pltpu.make_async_remote_copy(
        src_ref=send_m, dst_ref=recv_m, send_sem=ssem.at[0], recv_sem=rsem.at[0],
        device_id=other, device_id_type=MESH,
    )
    merge_copy.start()


    def o_copy(p):
        return pltpu.make_async_remote_copy(
            src_ref=send_o.at[p], dst_ref=recv_o.at[p], send_sem=ssem.at[1 + p], recv_sem=rsem.at[1 + p],
            device_id=other, device_id_type=MESH,
        )

    lane = lax.broadcasted_iota(jnp.int32, (rows, 128), 1)
    block = 1024

    def attend(p, _):
        for h in range(2):
            keys = jnp.where((lane < HEAD) == (h == 0), k_out[p] * 0.125, 0.0).astype(jnp.bfloat16)
            values_t = v_t[p, pl.ds(HEAD * h, HEAD), :]
            for b in range(rows // block):
                cols = pl.ds(b * block, block)
                s = mm_nt(keys, q_out[p, cols, :]) + bias[:, :1]
                peak = jnp.max(s, axis=0, keepdims=True)
                e = jnp.exp(s - peak)
                total = jnp.sum(e, axis=0, keepdims=True)
                o = mm(values_t, e.astype(jnp.bfloat16)) / total
                heads_t[p, pl.ds(HEAD * h, HEAD), cols] = o.astype(jnp.bfloat16)
                lse[pl.ds(2 * p + h, 1), cols] = peak + jnp.log(total)
        o = heads_t[p].astype(jnp.float32).T
        send_o[p] = o
        heads[p] = o.astype(jnp.bfloat16)
        o_copy(p).start()
        count = rows // pairs
        at = pl.multiple_of(p * count, count)
        turned = (cotangent[pl.ds(at, count), :].astype(jnp.float32) * mask_of(at, count)).T
        mlp_t[:, :, pl.ds(at, count)] = turned.astype(jnp.bfloat16).reshape(mlp_t.shape[0], mlp_t.shape[1], count)
        return 0

    lax.fori_loop(0, pairs, attend, 0)
    for c in stores[3:]:
        c.start()

    def merge_own(i, _):
        own = pl.ds(pl.multiple_of(i * 256, 256), 256)
        hidden[own, :] = mm(jnp.concatenate([heads[p, own, :] for p in range(pairs)], axis=1), vm[...])
        return 0

    lax.fori_loop(0, rows // 256, merge_own, 0)
    merge_copy.wait()
    other_m[...] = recv_m[...].astype(jnp.bfloat16)
    for p in range(pairs):
        o_copy(p).wait()

    def tile_stores(i):
        own = pl.ds(pl.multiple_of(i * 256, 256), 256)
        return [
            pltpu.make_async_copy(hidden.at[own, :], hidden_hbm.at[own, :], tsem.at[0, i]),
            pltpu.make_async_copy(mid.at[own, :], mid_hbm.at[own, :], tsem.at[1, i]),
        ]

    def finish(i, _):
        at = pl.multiple_of(i * 256, 256)
        own = pl.ds(at, 256)
        theirs = jnp.concatenate([recv_o[p, own, :].astype(jnp.bfloat16) for p in range(pairs)], axis=1)
        attn = hidden[own, :] + mm(theirs, other_m[...])
        one = tokens[own, :].astype(jnp.float32) * mask_of(at, 256) + attn
        hidden[own, :] = one
        mid[own, :] = (centre(one) * scale_two[...]).astype(jnp.bfloat16)
        for c in tile_stores(i):
            c.start()
        return 0

    lax.fori_loop(0, rows // 256, finish, 0)
    for c in stores:
        c.wait()
    for i in range(rows // 256):
        for c in tile_stores(i):
            c.wait()


def forward(names, length, moment, tokens, first_scales, second_scales, cotangent, cosine, sine, wq, wk, wv, wm):
    rows, width = tokens.shape
    local = wq.shape[1]
    pairs = local // 128
    vmem = pl.BlockSpec(memory_space=pltpu.VMEM)
    hbm = pl.BlockSpec(memory_space=pl.ANY)
    half = jnp.bfloat16
    full = jnp.float32
    shapes = [
        ((pairs, rows, 128), half),
        ((pairs, rows, 128), half),
        ((pairs, rows, 128), half),
        ((pairs, rows, 128), half),
        ((pairs, 128, rows), half),
        ((2 * pairs, rows), full),
        ((rows, width), full),
        ((rows, width), half),
        ((16, width // 16, rows), half),
        ((1, width), full),
        ((1, width), full),
    ]
    return pl.pallas_call(
        functools.partial(forward_kernel, names),
        out_shape=[jax.ShapeDtypeStruct(*s) for s in shapes],
        in_specs=[pl.BlockSpec(memory_space=pltpu.SMEM)] * 2 + [vmem] + [hbm] * 9,
        out_specs=[hbm] * len(shapes),
        scratch_shapes=[pltpu.VMEM(*s) for s in shapes]
        + [
            pltpu.VMEM((rows, width), half),
            pltpu.VMEM((rows, 128), full),
            pltpu.VMEM((rows, 128), full),
            pltpu.VMEM(first_scales.shape, full),
            pltpu.VMEM(second_scales.shape, full),
            pltpu.VMEM((rows, width), half),
            pltpu.VMEM(wq.shape, half),
            pltpu.VMEM(wk.shape, half),
            pltpu.VMEM(wv.shape, half),
            pltpu.VMEM(wm.shape, half),
            pltpu.VMEM(wm.shape, half),
            pltpu.VMEM((pairs, 128, rows), half),
            pltpu.VMEM(wm.shape, full),
            pltpu.VMEM(wm.shape, full),
            pltpu.VMEM((pairs, rows, 128), full),
            pltpu.VMEM((pairs, rows, 128), full),
            pltpu.VMEM((rows, 128), full),
            pltpu.SemaphoreType.DMA((9,)),
            pltpu.SemaphoreType.DMA((9,)),
            pltpu.SemaphoreType.DMA((2, 4)),
            pltpu.SemaphoreType.DMA((1 + pairs,)),
            pltpu.SemaphoreType.DMA((1 + pairs,)),
        ],
        compiler_params=pltpu.CompilerParams(collective_id=1, has_side_effects=True, vmem_limit_bytes=58 * 2**20),
        name="forward",
    )(length, moment, tokens, first_scales, second_scales, cotangent, cosine, sine, wq, wk, wv, wm)


ITEMS = 24
TILE = 256
RING = 5
HELD = 12
LAGS = (4, 6, 8, 10)
FIRSTS = (0, 8, 16, 18, 24)


def count_from(i, starts):
    total = 0
    for start in starts:
        total = total + jnp.where(i >= start, 1, 0)
    return total


def flip(index, weight):
    return index + weight * (1 - 2 * lax.rem(lax.div(index, weight), 2))


def weight_of(color, stage):
    k = lax.rem(color + stage, 3)
    return 1 + (k * (k + 1)) // 2


STARTS_Z = (2, 5, 10, 15, 19)


def color_of(i):
    turn = i - count_from(i, [p + 1 for p in STARTS_Z])
    on_z = sum(jnp.where(i == p, 1, 0) for p in STARTS_Z)
    return jnp.where(on_z == 1, 2, lax.rem(turn, 2))


def slot_of(i):
    return count_from(i, (8, 16)) - 2 * count_from(i, (18,))


def backward_kernel(
    names, length_ref, moment_ref, scale_one, scale_two,
    l_down, mid_in, heads, q_in, k_in, v_in, heads_t, lse_in, cosine, sine,
    merge_in, wq, wk, wv, tokens, hidden, cotangent, wu, wd,
    out, rows_out, tokens_out, layer_out, r_down, slope, r_up, hidden_grad,
    left, s1, r1, r2, r3, r4, rb, qkv, send_p, recv_p, ga, terms,
    msem, lsem, rsem, fsem, ssem, csem, psem, qsem, gsem, jsem, credit, credit_two, core_free,
):
    here = {n: lax.axis_index(n) for n in names}
    d = here[names[0]]

    def device(**moved):
        at = {**here, **moved}
        return tuple(at[n] for n in names)

    core = device(**{names[1]: 1 - here[names[1]]})

    def across(weight):
        return device(**{names[0]: flip(d, weight)})

    def absolute(r):
        total = 0
        for b in range(4):
            bit = lax.rem(lax.div(d, 2**b), 2)
            total = total + (2**b) * (1 - bit if (r >> b) & 1 else bit)
        return total

    def load_left(source, slot):
        for r in range(16):
            pltpu.make_async_copy(source.at[absolute(r)], left.at[slot, r], lsem).start()

    def left_loaded(slot):
        pltpu.make_async_copy(left.at[slot], left.at[slot], lsem).wait()

    def turn(values, slot, own):
        turned = values.T.astype(jnp.bfloat16)
        for c in range(16):
            left[slot, absolute(c), :, own] = turned[64 * c : 64 * c + 64]

    mid_load = pltpu.make_async_copy(mid_in, ga, msem)
    mid_load.start()
    load_left(l_down, 0)
    barrier = pltpu.get_barrier_semaphore()
    for weight in (1, 2, 4, 8):
        pl.semaphore_signal(barrier, inc=1, device_id=across(weight), device_id_type=MESH)
    pl.semaphore_signal(barrier, inc=1, device_id=core, device_id_type=MESH)
    pl.semaphore_wait(barrier, 5)

    def fetch(i, lane):
        slot = lax.rem(i, 2)
        target, sem = rb.at[lane, slot], fsem.at[lane, slot]
        for g, source in ((0, r_down), (1, r_up)):
            @pl.when((i >= FIRSTS[g]) & (i < FIRSTS[g + 1]))
            def _():
                col = pl.multiple_of((i - FIRSTS[g]) * TILE, TILE)
                pltpu.make_async_copy(source.at[:, pl.ds(col, TILE)], target, sem).start()

        @pl.when((i >= FIRSTS[2]) & (i < FIRSTS[3]))
        def _():
            for k in range(2):
                pltpu.make_async_copy(
                    heads.at[2 * (i - FIRSTS[2]) + k], target.at[:, pl.ds(128 * k, 128)], sem
                ).start()

        @pl.when(i >= FIRSTS[3])
        def _():
            pltpu.make_async_copy(qkv.at[i - FIRSTS[3]], target, sem).start()

    def fetched(i, lane):
        slot = lax.rem(i, 2)
        pltpu.make_async_copy(rb.at[lane, slot], rb.at[lane, slot], fsem.at[lane, slot]).wait()

    def product(i, first, lane):
        color, slot = color_of(i), slot_of(i)
        weights = [weight_of(color, s) for s in range(3)] + [8]
        rows = []
        for bits in range(8):
            r = first * weights[0] + sum(((bits >> (2 - k)) & 1) * weights[1 + k] for k in range(3))
            rows.append(left[slot, r])
        lhs = jnp.concatenate(rows, axis=0)
        return mm(lhs, rb[lane, lax.rem(i, 2)]).reshape(8, 64, TILE)

    def copy(i, s):
        weight = weight_of(color_of(i), s) if s < 3 else 8
        src = (s1.at[lax.rem(i, RING)], r1.at[lax.rem(i, HELD), pl.ds(4, 4)], r2.at[lax.rem(i, HELD), pl.ds(2, 2)], r3.at[i, pl.ds(1, 1)])[s]
        dst = (r1.at[lax.rem(i, HELD)], r2.at[lax.rem(i, HELD)], r3.at[i], r4.at[i])[s]
        return pltpu.make_async_remote_copy(
            src_ref=src, dst_ref=dst, send_sem=ssem.at[s, i], recv_sem=csem.at[s, i],
            device_id=across(weight), device_id_type=MESH,
        )

    def result(i):
        return pltpu.make_async_copy(r4.at[i, 0], out.at[i], rsem.at[i])

    def tick(i):
        e = i - LAGS[3]

        @pl.when((e >= 0) & (e < ITEMS))
        def _():
            copy(e, 3).wait_recv()
            r4[e, 0] = r4[e, 0] + r3[e, 0]
            result(e).start()

        c = i - LAGS[2]

        @pl.when((c >= 0) & (c < ITEMS))
        def _():
            copy(c, 2).wait_recv()
            r3[c] += r2[lax.rem(c, HELD), 0:2]
            copy(c, 3).start()
            copy(c, 2).wait_send()

            @pl.when(c + HELD < ITEMS)
            def _():
                color = color_of(c + HELD)
                pl.semaphore_signal(
                    credit_two.at[color], inc=1, device_id=across(weight_of(color, 1)), device_id_type=MESH
                )

        b = i - LAGS[1]

        @pl.when((b >= 0) & (b < ITEMS))
        def _():
            copy(b, 1).wait_recv()
            r2[lax.rem(b, HELD)] += r1[lax.rem(b, HELD), 0:4]
            copy(b, 2).start()
            copy(b, 1).wait_send()

            @pl.when(b + HELD < ITEMS)
            def _():
                color = color_of(b + HELD)
                pl.semaphore_signal(
                    credit.at[color], inc=1, device_id=across(weight_of(color, 0)), device_id_type=MESH
                )

        a = i - LAGS[0]

        @pl.when((a >= 0) & (a < ITEMS))
        def _():
            fetched(a, 1)
            copy(a, 0).wait_recv()
            r1[lax.rem(a, HELD)] += product(a, 0, 1)

            @pl.when(a >= HELD)
            def _():
                pl.semaphore_wait(credit_two.at[color_of(a)], 1)

            copy(a, 1).start()

            @pl.when(a + 2 < ITEMS)
            def _():
                fetch(a + 2, 1)

        @pl.when(i < ITEMS)
        def _():
            @pl.when(i >= RING)
            def _():
                copy(i - RING, 0).wait_send()

            @pl.when(i >= LAGS[0])
            def _():
                fetched(i, 0)

            s1[lax.rem(i, RING)] = product(i, 1, 0)

            @pl.when(i >= HELD)
            def _():
                pl.semaphore_wait(credit.at[color_of(i)], 1)

            copy(i, 0).start()

            @pl.when((i + 2 < ITEMS) & (i >= LAGS[0]))
            def _():
                fetch(i + 2, 0)

    rows, width = tokens.shape
    pairs = q_in.shape[0]
    length = length_ref[0]
    part = 256
    parts = rows // part
    half, full = jnp.bfloat16, jnp.float32

    def keep_of(at):
        return jnp.where(at + lax.broadcasted_iota(jnp.int32, (part, 1), 0) < length, 1.0, 0.0)

    def core_copy(use, i):
        return pltpu.make_async_remote_copy(
            src_ref=send_p.at[i], dst_ref=recv_p.at[i], send_sem=psem.at[use, i], recv_sem=qsem.at[use, i],
            device_id=core, device_id_type=MESH,
        )

    def core_sent(use):
        for i in range(parts):
            core_copy(use, i).wait_send()
        if use < 2:
            pl.semaphore_signal(core_free, inc=1, device_id=core, device_id_type=MESH)
            pl.semaphore_wait(core_free, 1)

    def norm_parts(values):
        centred = values - jnp.mean(values, axis=1, keepdims=True)
        inverse = lax.rsqrt(jnp.mean(centred * centred, axis=1, keepdims=True) + epsilon)
        return centred * inverse, inverse

    def norm_grad(grad, normed, inverse, scale):
        hat = grad * scale
        middle = jnp.mean(hat, axis=1, keepdims=True)
        return inverse * (hat - middle - normed * jnp.mean(hat * normed, axis=1, keepdims=True))

    def run_ticks(first, last):
        lax.fori_loop(first, last, lambda i, _: (tick(i), 0)[1], 0)

    def mlp(vu, vd, cot, wide, hid, gp, gh, wsem, usem, dsem, tsem, osem):
        tiles = wu.shape[1] // TILE

        def columns(k):
            return pl.ds(pl.multiple_of(k * TILE, TILE), TILE)

        def up_load(k):
            return pltpu.make_async_copy(wu.at[:, columns(k)], vu.at[:, columns(k)], usem.at[k])

        for k in range(2):
            up_load(k).start()
        down_load = pltpu.make_async_copy(wd, vd, wsem)

        def tile_stores(k, lane):
            slot = lax.rem(k, 2)
            return (
                pltpu.make_async_copy(rb.at[lane, slot], r_down.at[:, columns(k)], dsem.at[0, slot]),
                pltpu.make_async_copy(qkv.at[slot], slope.at[:, columns(k)], dsem.at[1, slot]),
            )

        def up_tile(k, lane):
            slot = lax.rem(k, 2)

            @pl.when(k >= 2)
            def _():
                for x in tile_stores(k - 2, lane):
                    x.wait()

            up_load(k).wait()

            @pl.when(k + 2 < tiles)
            def _():
                up_load(k + 2).start()

            for r in range(0, rows, 512):
                v = mm(ga[r : r + 512, :], vu[:, columns(k)])
                square = v * v
                t = jnp.tanh(0.7978845608028654 * v * (1.0 + 0.044715 * square))
                above = 0.5 * (1.0 + t)
                rb[lane, slot, r : r + 512, :] = (v * above).astype(half)
                qkv[slot, r : r + 512, :] = (
                    above + 0.5 * v * (1.0 - t * t) * (0.7978845608028654 * (1.0 + 0.134145 * square))
                ).astype(half)
            for x in tile_stores(k, lane):
                x.start()

        def tile(source, target, n, i):
            own = pl.ds(pl.multiple_of(i * part, part), part)
            slot = lax.rem(i, 2)
            return pltpu.make_async_copy(source.at[own, :], target.at[slot], tsem.at[n, slot])

        def stream(sources, i, body):
            for n, source, target in sources:
                tile(source, target, n, i).wait()

                @pl.when(i + 1 < parts)
                def _():
                    tile(source, target, n, i + 1).start()

            return body(i, pl.multiple_of(i * part, part), lax.rem(i, 2))

        def begin(sources):
            for n, source, target in sources:
                tile(source, target, n, jnp.int32(0)).start()

        mid_load.wait()
        left_loaded(0)

        def early(k, _):
            up_tile(k, 0)
            tick(k)
            return 0

        lax.fori_loop(0, LAGS[0], early, 0)
        down_load.start()
        lax.fori_loop(LAGS[0], tiles, lambda k, _: (up_tile(k, 1), 0)[1], 0)
        for k in (tiles - 2, tiles - 1):
            for x in tile_stores(k, 1):
                x.wait()
        for i in range(2):
            fetch(jnp.int32(i), 1)
            fetch(jnp.int32(LAGS[0] + i), 0)
        streams = ((0, cotangent, cot), (1, slope, wide))
        begin(streams)
        down_load.wait()

        def store_pre(i):
            own = pl.ds(pl.multiple_of(i * part, part), part)
            return pltpu.make_async_copy(gp, r_up.at[own, :], osem.at[0])

        def first(i, at, slot):
            x = (cot[slot].astype(full) * keep_of(at)).astype(half)
            g = mm_nt(x, vd[...]) * wide[slot].astype(full)

            @pl.when(i > 0)
            def _():
                store_pre(i - 1).wait()

            gp[...] = g.astype(half)
            store_pre(i).start()
            send_p[i] = mm_nt(gp[...], vu[...])
            core_copy(0, i).start()

            @pl.when(i < 2)
            def _():
                tick(LAGS[0] + i)

            return 0

        lax.fori_loop(0, parts, lambda i, _: stream(streams, i, first), 0)
        store_pre(parts - 1).wait()
        run_ticks(LAGS[0] + 2, LAGS[0] + 4)
        streams_two = ((0, cotangent, cot), (2, hidden, hid))
        begin(streams_two)

        def store_hidden(i):
            own = pl.ds(pl.multiple_of(i * part, part), part)
            return pltpu.make_async_copy(gh, hidden_grad.at[own, :], osem.at[1])

        def second(i, at, slot, total):
            own = pl.ds(at, part)
            normed, inverse = norm_parts(hid[slot])
            turn(normed * scale_two[...], 1, own)
            core_copy(0, i).wait_recv()
            grad = send_p[i] + recv_p[i]

            @pl.when(i > 0)
            def _():
                store_hidden(i - 1).wait()

            gh[...] = cot[slot].astype(full) * keep_of(at) + norm_grad(grad, normed, inverse, scale_two[...])
            store_hidden(i).start()
            ga[own, :] = gh[...].astype(half)
            turn(gh[...], 2, own)
            return total + jnp.sum(grad * normed, axis=0, keepdims=True)

        term = lax.fori_loop(
            0, parts, lambda i, total: stream(streams_two, i, functools.partial(second, total=total)),
            jnp.zeros((1, width), full),
        )
        for j in range(8):
            terms[0, 8 + j : 9 + j, :] = term[:, 128 * j : 128 * j + 128]
        store_hidden(parts - 1).wait()
        core_sent(0)
        streams_three = ((1, r_down, wide),)
        begin(streams_three)

        def third(i, at, slot):
            send_p[i] = mm(wide[slot], vd[...])
            core_copy(1, i).start()
            return 0

        lax.fori_loop(0, parts, lambda i, _: stream(streams_three, i, third), 0)
        streams_four = ((2, hidden, hid),)
        begin(streams_four)
        tick(jnp.int32(LAGS[0] + 4))

        def store_layer(i):
            own = pl.ds(pl.multiple_of(i * part, part), part)
            return pltpu.make_async_copy(cot.at[0], layer_out.at[own, :], osem.at[0])

        def fourth(i, at, slot):
            core_copy(1, i).wait_recv()

            @pl.when(i > 0)
            def _():
                store_layer(i - 1).wait()

            cot[0] = ((hid[slot] + (send_p[i] + recv_p[i])) * keep_of(at)).astype(half)
            store_layer(i).start()
            return 0

        lax.fori_loop(0, parts, lambda i, _: stream(streams_four, i, fourth), 0)
        store_layer(parts - 1).wait()
        core_sent(1)

    pl.run_scoped(
        mlp,
        pltpu.VMEM(wu.shape, half),
        pltpu.VMEM(wd.shape, half),
        pltpu.VMEM((2, part, width), half),
        pltpu.VMEM((2, part, wu.shape[1]), half),
        pltpu.VMEM((2, part, width), full),
        pltpu.VMEM((part, wu.shape[1]), half),
        pltpu.VMEM((part, width), full),
        pltpu.SemaphoreType.DMA,
        pltpu.SemaphoreType.DMA((wu.shape[1] // TILE,)),
        pltpu.SemaphoreType.DMA((2, 2)),
        pltpu.SemaphoreType.DMA((3, 2)),
        pltpu.SemaphoreType.DMA((2,)),
    )

    def attention(q, k, v, o_t, lse, wm, cos, sin, bias, do, do_t, kh, vh, k_t, dq_t, asem):
        loads = [
            pltpu.make_async_copy(a, b, asem.at[n])
            for n, (a, b) in enumerate(
                ((q_in, q), (k_in, k), (v_in, v), (heads_t, o_t), (lse_in, lse), (merge_in, wm),
                 (cosine, cos), (sine, sin))
            )
        ]
        for x in loads:
            x.start()
        for x in loads:
            x.wait()
        place = lax.broadcasted_iota(jnp.int32, (rows, 128), 0)
        bias[...] = (jnp.where(place < length, 1.0, 0.0) - 1.0) * 1000000000.0
        lane = lax.broadcasted_iota(jnp.int32, (rows, 128), 1) < HEAD
        block = 256

        def unrotate_lanes(y):
            return (y * cos[...] - swap_halves(y) * sin[...]).astype(jnp.bfloat16)

        def pair(p, _):
            weight = wm[pl.ds(pl.multiple_of(128 * p, 128), 128), :]
            do[...] = mm_nt(ga[...], weight).astype(jnp.bfloat16)
            do_t[...] = mm_nt(weight, ga[...]).astype(jnp.bfloat16)
            k_t[...] = (k[p].astype(jnp.float32) * 0.125).T.astype(jnp.bfloat16)
            product_t = do_t[...].astype(jnp.float32) * o_t[p].astype(jnp.float32)
            dks, dvs = [], []
            for h in range(2):
                tick(LAGS[0] + 5 + 2 * p + h)
                delta = jnp.sum(product_t[HEAD * h : HEAD * h + HEAD], axis=0, keepdims=True)
                own = lane == (h == 0)
                kh[...] = jnp.where(own, k[p].astype(jnp.float32) * 0.125, 0.0).astype(jnp.bfloat16)
                vh[...] = jnp.where(own, v[p].astype(jnp.float32), 0.0).astype(jnp.bfloat16)
                dk = jnp.zeros((rows, 128), jnp.float32)
                dv = jnp.zeros((rows, 128), jnp.float32)
                for b in range(0, rows, block):
                    cols = slice(b, b + block)
                    qb = q[p, cols, :]
                    s = mm_nt(kh[...], qb) + bias[:, :1]
                    soft = jnp.exp(s - lse[pl.ds(2 * p + h, 1), cols])
                    ds = soft * (mm(vh[...], do_t[:, cols]) - delta[:, cols])
                    ds = ds.astype(jnp.bfloat16)
                    dv = dv + mm(soft.astype(jnp.bfloat16), do[cols, :])
                    dk = dk + mm(ds, qb)
                    dq_t[HEAD * h : HEAD * h + HEAD, cols] = mm(k_t[HEAD * h : HEAD * h + HEAD, :], ds)
                dks.append(dk)
                dvs.append(dv)
            quad = 3 * lax.div(p, 2)
            at = pl.ds(pl.multiple_of(128 * lax.rem(p, 2), 128), 128)
            qkv[quad, :, at] = unrotate_lanes(dq_t[...].T)
            qkv[quad + 1, :, at] = unrotate_lanes(jnp.where(lane, dks[0], dks[1]) * 0.125)
            qkv[quad + 2, :, at] = jnp.where(lane, dvs[0], dvs[1]).astype(jnp.bfloat16)
            return 0

        lax.fori_loop(0, pairs, pair, 0)

    pl.run_scoped(
        attention,
        pltpu.VMEM((pairs, rows, 128), half),
        pltpu.VMEM((pairs, rows, 128), half),
        pltpu.VMEM((pairs, rows, 128), half),
        pltpu.VMEM((pairs, 128, rows), half),
        pltpu.VMEM((2 * pairs, rows), full),
        pltpu.VMEM(merge_in.shape, half),
        pltpu.VMEM((rows, 128), full),
        pltpu.VMEM((rows, 128), full),
        pltpu.VMEM((rows, 128), full),
        pltpu.VMEM((rows, 128), half),
        pltpu.VMEM((128, rows), half),
        pltpu.VMEM((rows, 128), half),
        pltpu.VMEM((rows, 128), half),
        pltpu.VMEM((128, rows), half),
        pltpu.VMEM((128, rows), full),
        pltpu.SemaphoreType.DMA((10,)),
    )

    def inner(vq, vk, vv, x_in, gh, to, sem, hsem, osem):
        loads = [
            pltpu.make_async_copy(a, b, sem.at[n])
            for n, (a, b) in enumerate(((wq, vq), (wk, vk), (wv, vv), (tokens, x_in)))
        ]
        for x in loads:
            x.start()
        for x in loads:
            x.wait()

        def send(i, _):
            at = pl.multiple_of(i * part, part)
            own = pl.ds(at, part)
            total = None
            for quad in range(2):
                for n, w in enumerate((vq, vk, vv)):
                    term = mm_nt(qkv[3 * quad + n, own, :], w[:, TILE * quad : TILE * quad + TILE])
                    total = term if total is None else total + term
            send_p[i] = total
            core_copy(2, i).start()
            normed, _ = norm_parts(x_in[own, :].astype(full) * keep_of(at))
            turn(normed * scale_one[...], 0, own)

            @pl.when(i == 1)
            def _():
                tick(LAGS[0] + 13)

            return 0

        lax.fori_loop(0, parts, send, 0)

        def store_tokens(i):
            own = pl.ds(pl.multiple_of(i * part, part), part)
            return pltpu.make_async_copy(to, tokens_out.at[own, :], osem)

        def take(i, total):
            at = pl.multiple_of(i * part, part)
            own = pl.ds(at, part)
            hidden_copy = pltpu.make_async_copy(hidden_grad.at[own, :], gh, hsem)
            hidden_copy.start()

            @pl.when(i < 2)
            def _():
                tick(LAGS[0] + 14 + i)

            core_copy(2, i).wait_recv()
            grad = send_p[i] + recv_p[i]
            keep = keep_of(at)
            normed, inverse = norm_parts(x_in[own, :].astype(full) * keep)
            back = norm_grad(grad, normed, inverse, scale_one[...])
            hidden_copy.wait()

            @pl.when(i > 0)
            def _():
                store_tokens(i - 1).wait()

            to[...] = ((gh[...] + back) * keep).astype(half)
            store_tokens(i).start()
            return total + jnp.sum(grad * normed, axis=0, keepdims=True)

        first = lax.fori_loop(0, parts, take, jnp.zeros((1, width), full))
        store_tokens(parts - 1).wait()
        core_sent(2)
        for j in range(8):
            terms[0, j : j + 1, :] = first[:, 128 * j : 128 * j + 128]
        terms[0, 16:24, :] = jnp.full((8, 128), moment_ref[0].astype(full), full)

    pl.run_scoped(
        inner,
        pltpu.VMEM(wq.shape, half),
        pltpu.VMEM(wk.shape, half),
        pltpu.VMEM(wv.shape, half),
        pltpu.VMEM((rows, width), half),
        pltpu.VMEM((part, width), full),
        pltpu.VMEM((part, width), half),
        pltpu.SemaphoreType.DMA((4,)),
        pltpu.SemaphoreType.DMA,
        pltpu.SemaphoreType.DMA,
    )
    done = LAGS[0] + 16
    for stage in range(4):
        held = 2**stage
        exchange = pltpu.make_async_remote_copy(
            src_ref=terms.at[pl.ds(0, held)], dst_ref=terms.at[pl.ds(held, held)],
            send_sem=gsem.at[stage], recv_sem=jsem.at[stage], device_id=across(held), device_id_type=MESH,
        )
        exchange.start()
        tick(jnp.int32(done + stage))
        exchange.wait()
    table_rows = rows_out.shape[1]
    upper = lax.rem(d, 2) == 1
    places = lax.broadcasted_iota(jnp.int32, (table_rows, 128), 0).astype(full)
    total = jnp.zeros((table_rows, 128), full)
    for n in range(16):
        row = []
        for base in (0, 8):
            piece = terms[n, pl.ds(base + lax.div(d, 2), 1), :]
            row.append(jnp.where(upper, piece[:, 64:], piece[:, :64]))
        total = total + jnp.where(places == terms[n, 16:17, :], jnp.concatenate(row, axis=1), 0.0)
    rows_out[...] = total.T
    run_ticks(done + 4, ITEMS + LAGS[3])

    def drain(i, _):
        @pl.when(i >= ITEMS - RING)
        def _():
            copy(i, 0).wait_send()

        copy(i, 3).wait_send()
        result(i).wait()
        return 0

    lax.fori_loop(0, ITEMS, drain, 0)


def backward(names, table_rows, length, moment, scale_one, scale_two, *arrays):
    tokens, up = arrays[-5], arrays[-2]
    rows, width = tokens.shape
    smem = pl.BlockSpec(memory_space=pltpu.SMEM)
    vmem = pl.BlockSpec(memory_space=pltpu.VMEM)
    hbm = pl.BlockSpec(memory_space=pl.ANY)
    half, full = jnp.bfloat16, jnp.float32
    dma = pltpu.SemaphoreType.DMA
    return pl.pallas_call(
        functools.partial(backward_kernel, names),
        out_shape=[
            jax.ShapeDtypeStruct((ITEMS, 64, TILE), full),
            jax.ShapeDtypeStruct((128, table_rows), full),
            jax.ShapeDtypeStruct((rows, width), half),
            jax.ShapeDtypeStruct((rows, width), half),
            jax.ShapeDtypeStruct((rows, up.shape[1]), half),
            jax.ShapeDtypeStruct((rows, up.shape[1]), half),
            jax.ShapeDtypeStruct((rows, up.shape[1]), half),
            jax.ShapeDtypeStruct((rows, width), full),
        ],
        in_specs=[smem] * 2 + [vmem] * 2 + [hbm] * len(arrays),
        out_specs=[hbm, vmem] + [hbm] * 6,
        scratch_shapes=[
            pltpu.VMEM((3, 16, 64, rows), half),
            pltpu.VMEM((RING, 8, 64, TILE), full),
            pltpu.VMEM((HELD, 8, 64, TILE), full),
            pltpu.VMEM((HELD, 4, 64, TILE), full),
            pltpu.VMEM((ITEMS, 2, 64, TILE), full),
            pltpu.VMEM((ITEMS, 1, 64, TILE), full),
            pltpu.VMEM((2, 2, rows, TILE), half),
            pltpu.VMEM((6, rows, TILE), half),
            pltpu.VMEM((rows // 256, 256, width), full),
            pltpu.VMEM((rows // 256, 256, width), full),
            pltpu.VMEM((rows, width), half),
            pltpu.VMEM((16, 24, 128), full),
            dma,
            dma,
            dma((ITEMS,)),
            dma((2, 2)),
            dma((4, ITEMS)),
            dma((4, ITEMS)),
            dma((3, 4)),
            dma((3, 4)),
            dma((4,)),
            dma((4,)),
            pltpu.SemaphoreType.REGULAR((3,)),
            pltpu.SemaphoreType.REGULAR((3,)),
            pltpu.SemaphoreType.REGULAR,
        ],
        compiler_params=pltpu.CompilerParams(
            collective_id=0, has_side_effects=True, vmem_limit_bytes=60 * 2**20
        ),
        name="backward",
    )(length, moment, scale_one, scale_two, *arrays)


def finish_kernel(
    pieces_in, tables_in, tokens_in, layer_in,
    layer_out, tokens_out, grad_q, grad_k, grad_v, grad_m, grad_u, grad_d, first, second,
    pieces, tables, held, isem, osem,
):
    parts = held.shape[1]
    step = layer_in.shape[0] // parts
    incoming, outgoing = [], []

    def move(source, keep, target):
        n = len(incoming)
        incoming.append(pltpu.make_async_copy(source, keep, isem.at[n]))
        outgoing.append(pltpu.make_async_copy(keep, target, osem.at[n]))

    for n, (source, target) in enumerate(((layer_in, layer_out), (tokens_in, tokens_out))):
        for k in range(parts):
            own = pl.ds(k * step, step)
            move(source.at[own, :], held.at[n, k], target.at[own, :])
    targets = [(grad_d, k) for k in range(8)] + [(grad_u, k) for k in range(8)] + [(grad_m, k) for k in range(2)]
    targets += [(ref, k) for k in range(2) for ref in (grad_q, grad_k, grad_v)]
    for n, (ref, k) in enumerate(targets):
        move(pieces_in.at[n], pieces.at[n], ref.at[:, pl.ds(TILE * k, TILE)])
    count = first.shape[0]
    for k, ref in enumerate((first, second)):
        own = pl.ds(k * count, count)
        move(tables_in.at[own, :], tables.at[own, :], ref)
    for c in incoming:
        c.start()
    for a, b in zip(incoming, outgoing):
        a.wait()
        b.start()
    for c in outgoing:
        c.wait()


def finish(pieces, tables, tokens, layer):
    hbm = pl.BlockSpec(memory_space=pl.ANY)
    full = jnp.float32
    rows, width = layer.shape
    table_rows = tables.shape[1]
    shapes = [(64, 512)] * 4 + [(64, 2048), (64, 2048), (64, table_rows), (64, table_rows)]
    layer, tokens, *grads = pl.pallas_call(
        finish_kernel,
        out_shape=[jax.ShapeDtypeStruct(a.shape, a.dtype) for a in (layer, tokens)]
        + [jax.ShapeDtypeStruct(s, full) for s in shapes],
        in_specs=[hbm] * 4,
        out_specs=[hbm] * (2 + len(shapes)),
        scratch_shapes=[
            pltpu.VMEM(pieces.shape, full),
            pltpu.VMEM(tables.shape, full),
            pltpu.VMEM((2, 1, rows // 1, width), layer.dtype),
            pltpu.SemaphoreType.DMA((28,)),
            pltpu.SemaphoreType.DMA((28,)),
        ],
        name="finish",
    )(pieces, tables, tokens, layer)
    query, key, value, merge, up, down, first, second = grads
    return layer[None], tokens[None], query, key, value, merge.T, up, down.T, first.T, second.T


def fast_body(
    tokens,
    cotangent,
    lengths,
    noise_times,
    query_weight,
    key_weight,
    value_weight,
    merge_weight,
    up_weight,
    down_weight,
    first_scales,
    second_scales,
):
    tokens, cotangent = tokens[0], cotangent[0]
    rows, width = tokens.shape
    names = ("dp", "tensor")
    cosine, sine = (jnp.asarray(a) for a in rope_lanes(rows))
    query, key, value, heads, heads_t, lse, hidden, normal_mid, mlp_t, scale_one, scale_two = forward(
        names, lengths, noise_times, tokens, first_scales, second_scales, cotangent, cosine, sine,
        query_weight, key_weight, value_weight, merge_weight,
    )
    pieces, tables, grad_tokens, layer_output, *_ = backward(
        names, first_scales.shape[0], lengths, noise_times, scale_one, scale_two,
        mlp_t, normal_mid, heads, query, key, value, heads_t, lse, cosine, sine,
        merge_weight, query_weight, key_weight, value_weight, tokens, hidden, cotangent, up_weight, down_weight,
    )
    return finish(pieces, tables, grad_tokens, layer_output)


def body(
    tokens,
    cotangent,
    lengths,
    noise_times,
    query_weight,
    key_weight,
    value_weight,
    merge_weight,
    up_weight,
    down_weight,
    first_scales,
    second_scales,
):
    seq_count, length, width = tokens.shape
    local_width = query_weight.shape[1]
    local_heads = local_width // HEAD
    table_rows = first_scales.shape[0]
    flat_rows = seq_count * length
    scale_factor = 1.0 / math.sqrt(HEAD)
    block_rows = min(512, length)
    head_shape = (seq_count, length, local_heads, HEAD)
    row_mask = (jnp.arange(length, dtype=jnp.int32)[None, :] < lengths[:, None]).astype(jnp.float32)
    key_bias = (row_mask - 1.0) * 1000000000.0
    one_hot = (noise_times[:, None] == jnp.arange(table_rows, dtype=jnp.int32)[None, :]).astype(
        jnp.float32
    )
    scale_one = jnp.dot(one_hot, first_scales, precision=highest)
    scale_two = jnp.dot(one_hot, second_scales, precision=highest)
    cos_table, sin_table = rope_tables(length, HEAD)
    inputs = tokens.astype(jnp.float32) * row_mask[:, :, None]
    normed_one, inv_one = normalize(inputs)
    normal_in = (normed_one * scale_one[:, None, :]).astype(jnp.bfloat16).reshape(flat_rows, width)
    queries = jnp.dot(normal_in, query_weight, preferred_element_type=jnp.float32).reshape(
        head_shape
    )
    key_proj = jnp.dot(normal_in, key_weight, preferred_element_type=jnp.float32).reshape(
        head_shape
    )
    value_rows = (
        jnp.dot(normal_in, value_weight, preferred_element_type=jnp.float32)
        .astype(jnp.bfloat16)
        .reshape(head_shape)
    )
    query_rot = rotate(queries, cos_table, sin_table).astype(jnp.bfloat16)
    key_rot = rotate(key_proj, cos_table, sin_table).astype(jnp.bfloat16)
    attended = []
    log_sums = []
    for offset in range(0, length, block_rows):
        scores = block_scores(
            query_rot[:, offset : offset + block_rows], key_rot, key_bias, scale_factor
        )
        peak_score = jnp.max(scores, axis=-1, keepdims=True)
        exponent = jnp.exp(scores - peak_score)
        totals = jnp.sum(exponent, axis=-1, keepdims=True)
        soft_weights = (exponent / totals).astype(jnp.bfloat16)
        log_sums.append(peak_score + jnp.log(totals))
        attended.append(
            jnp.einsum(
                "shqk,skhd->sqhd", soft_weights, value_rows, preferred_element_type=jnp.float32
            )
        )
    heads_out = (
        jnp.concatenate(attended, axis=1).astype(jnp.bfloat16).reshape(flat_rows, local_width)
    )
    attn_part = jnp.dot(heads_out, merge_weight, preferred_element_type=jnp.float32)
    attn_total = lax.psum(attn_part, "tensor")
    hidden_one = inputs + attn_total.reshape(seq_count, length, width)
    normed_two, inv_two = normalize(hidden_one)
    normal_mid = (normed_two * scale_two[:, None, :]).astype(jnp.bfloat16).reshape(flat_rows, width)
    pre_act = jnp.dot(normal_mid, up_weight, preferred_element_type=jnp.float32)
    activated = gelu_tanh(pre_act).astype(jnp.bfloat16)
    mlp_part = jnp.dot(activated, down_weight, preferred_element_type=jnp.float32)
    mlp_total = lax.psum(mlp_part, "tensor")
    layer_output = (
        (hidden_one + mlp_total.reshape(seq_count, length, width)) * row_mask[:, :, None]
    ).astype(jnp.bfloat16)
    grad_final = cotangent.astype(jnp.float32) * row_mask[:, :, None]
    grad_mlp = grad_final.astype(jnp.bfloat16).reshape(flat_rows, width)
    grad_down = jnp.dot(activated.T, grad_mlp, preferred_element_type=jnp.float32)
    grad_act = jnp.dot(grad_mlp, down_weight.T, preferred_element_type=jnp.float32)
    unused_value, gelu_back = jax.vjp(gelu_tanh, pre_act)
    grad_pre = gelu_back(grad_act)[0].astype(jnp.bfloat16)
    grad_up = jnp.dot(normal_mid.T, grad_pre, preferred_element_type=jnp.float32)
    mid_part = jnp.dot(grad_pre, up_weight.T, preferred_element_type=jnp.float32)
    grad_mid = lax.psum(mid_part, "tensor").reshape(seq_count, length, width)
    grad_hat_two, scale_grad_two = norm_back(grad_mid, normed_two, inv_two, scale_two)
    grad_hidden = grad_final + grad_hat_two
    grad_second = jnp.dot(one_hot.T, scale_grad_two, precision=highest)
    grad_attn = grad_hidden.astype(jnp.bfloat16).reshape(flat_rows, width)
    grad_merge = jnp.dot(heads_out.T, grad_attn, preferred_element_type=jnp.float32)
    grad_heads = (
        jnp.dot(grad_attn, merge_weight.T, preferred_element_type=jnp.float32)
        .astype(jnp.bfloat16)
        .reshape(head_shape)
    )
    grad_keys = jnp.zeros(head_shape, jnp.float32)
    grad_values = jnp.zeros(head_shape, jnp.float32)
    query_grads = []
    for block_index in range(len(log_sums)):
        offset = block_index * block_rows
        query_block = query_rot[:, offset : offset + block_rows]
        grad_block = grad_heads[:, offset : offset + block_rows]
        scores = block_scores(query_block, key_rot, key_bias, scale_factor)
        soft_weights = jnp.exp(scores - log_sums[block_index])
        grad_soft = jnp.einsum(
            "sqhd,skhd->shqk", grad_block, value_rows, preferred_element_type=jnp.float32
        )
        grad_values = grad_values + jnp.einsum(
            "shqk,sqhd->skhd",
            soft_weights.astype(jnp.bfloat16),
            grad_block,
            preferred_element_type=jnp.float32,
        )
        grad_scores = (
            soft_weights * (grad_soft - jnp.sum(soft_weights * grad_soft, axis=-1, keepdims=True))
        ).astype(jnp.bfloat16)
        query_grads.append(
            jnp.einsum("shqk,skhd->sqhd", grad_scores, key_rot, preferred_element_type=jnp.float32)
            * scale_factor
        )
        grad_keys = (
            grad_keys
            + jnp.einsum(
                "shqk,sqhd->skhd", grad_scores, query_block, preferred_element_type=jnp.float32
            )
            * scale_factor
        )
    query_back = (
        unrotate(jnp.concatenate(query_grads, axis=1), cos_table, sin_table)
        .astype(jnp.bfloat16)
        .reshape(flat_rows, local_width)
    )
    key_back = (
        unrotate(grad_keys, cos_table, sin_table)
        .astype(jnp.bfloat16)
        .reshape(flat_rows, local_width)
    )
    value_back = grad_values.astype(jnp.bfloat16).reshape(flat_rows, local_width)
    grad_query = jnp.dot(normal_in.T, query_back, preferred_element_type=jnp.float32)
    grad_key = jnp.dot(normal_in.T, key_back, preferred_element_type=jnp.float32)
    grad_value = jnp.dot(normal_in.T, value_back, preferred_element_type=jnp.float32)
    inner_part = jnp.dot(query_back, query_weight.T, preferred_element_type=jnp.float32)
    inner_part = inner_part + jnp.dot(key_back, key_weight.T, preferred_element_type=jnp.float32)
    inner_part = inner_part + jnp.dot(
        value_back, value_weight.T, preferred_element_type=jnp.float32
    )
    grad_inner = lax.psum(inner_part, "tensor").reshape(seq_count, length, width)
    grad_hat_one, scale_grad_one = norm_back(grad_inner, normed_one, inv_one, scale_one)
    grad_tokens = ((grad_hidden + grad_hat_one) * row_mask[:, :, None]).astype(jnp.bfloat16)
    grad_first = jnp.dot(one_hot.T, scale_grad_one, precision=highest)
    summed = (
        lax.psum_scatter(grad_query, "dp", scatter_dimension=0, tiled=True),
        lax.psum_scatter(grad_key, "dp", scatter_dimension=0, tiled=True),
        lax.psum_scatter(grad_value, "dp", scatter_dimension=0, tiled=True),
        lax.psum_scatter(grad_merge, "dp", scatter_dimension=1, tiled=True),
        lax.psum_scatter(grad_up, "dp", scatter_dimension=0, tiled=True),
        lax.psum_scatter(grad_down, "dp", scatter_dimension=1, tiled=True),
        lax.psum_scatter(grad_first, "dp", scatter_dimension=1, tiled=True),
        lax.psum_scatter(grad_second, "dp", scatter_dimension=1, tiled=True),
    )
    return (
        layer_output,
        grad_tokens,
        summed[0],
        summed[1],
        summed[2],
        summed[3],
        summed[4],
        summed[5],
        summed[6],
        summed[7],
    )


def solution(mesh):
    fast = mesh.shape["dp"] == 16 and mesh.shape["tensor"] == 2
    return jax.shard_map(
        fast_body if fast else body,
        mesh=mesh,
        in_specs=(
            P("dp", None, None),
            P("dp", None, None),
            P("dp"),
            P("dp"),
            P(None, "tensor"),
            P(None, "tensor"),
            P(None, "tensor"),
            P("tensor", None),
            P(None, "tensor"),
            P("tensor", None),
            P(),
            P(),
        ),
        out_specs=(
            P("dp", None, None),
            P("dp", None, None),
            P("dp", "tensor"),
            P("dp", "tensor"),
            P("dp", "tensor"),
            P("tensor", "dp"),
            P("dp", "tensor"),
            P("tensor", "dp"),
            P(None, "dp"),
            P(None, "dp"),
        ),
        check_vma=False,
    )
```

```python
import functools
import math

import jax
import jax.numpy as jnp
import numpy as np
from jax import lax
from jax.experimental import pallas as pl
from jax.experimental.pallas import tpu as pltpu
from jax.sharding import PartitionSpec as P

HEAD = 64
MESH = pl.DeviceIdType.MESH


epsilon = 1e-05
highest = lax.Precision.HIGHEST


def gelu_tanh(values):
    return (
        0.5
        * values
        * (1.0 + jnp.tanh(0.7978845608028654 * (values + 0.044715 * values * values * values)))
    )


def rope_tables(length, head_size):
    halves = head_size // 2
    places = jnp.arange(length, dtype=jnp.float32)[:, None]
    frequency = jnp.exp(
        jnp.arange(halves, dtype=jnp.float32) * (-2.0 * math.log(10000.0) / head_size)
    )
    angles = places * frequency[None, :]
    return (jnp.cos(angles), jnp.sin(angles))


def rotate(values, cos_table, sin_table):
    halves = values.shape[-1] // 2
    first_half = values[..., :halves]
    second_half = values[..., halves:]
    cosine = cos_table[:, None, :]
    sine_part = sin_table[:, None, :]
    return jnp.concatenate(
        [
            first_half * cosine - second_half * sine_part,
            second_half * cosine + first_half * sine_part,
        ],
        axis=-1,
    )


def unrotate(gradient, cos_table, sin_table):
    halves = gradient.shape[-1] // 2
    first_half = gradient[..., :halves]
    second_half = gradient[..., halves:]
    cosine = cos_table[:, None, :]
    sine_part = sin_table[:, None, :]
    return jnp.concatenate(
        [
            first_half * cosine + second_half * sine_part,
            second_half * cosine - first_half * sine_part,
        ],
        axis=-1,
    )


def normalize(values):
    centred = values - jnp.mean(values, axis=-1, keepdims=True)
    inv_std = lax.rsqrt(jnp.mean(centred * centred, axis=-1, keepdims=True) + epsilon)
    return (centred * inv_std, inv_std)


def norm_back(grad_norm, normed, inv_std, scale_rows):
    grad_hat = grad_norm * scale_rows[:, None, :]
    grad_scale = jnp.sum(grad_norm * normed, axis=1)
    mean_grad = jnp.mean(grad_hat, axis=-1, keepdims=True)
    mean_cross = jnp.mean(grad_hat * normed, axis=-1, keepdims=True)
    return (inv_std * (grad_hat - mean_grad - normed * mean_cross), grad_scale)


def block_scores(query_block, key_rot, key_bias, scale_factor):
    scores = jnp.einsum("sqhd,skhd->shqk", query_block, key_rot, preferred_element_type=jnp.float32)
    return scores * scale_factor + key_bias[:, None, None, :]


def rope_lanes(length):
    halves = HEAD // 2
    places = np.arange(length, dtype=np.float64)[:, None]
    frequency = np.exp(np.arange(halves) * (-2.0 * math.log(10000.0) / HEAD))
    angles = places * frequency[None, :]
    cosine, sine = np.cos(angles), np.sin(angles)
    return (
        np.concatenate([cosine] * 4, axis=1).astype(np.float32),
        np.concatenate([-sine, sine] * 2, axis=1).astype(np.float32),
    )


def swap_halves(values):
    lanes = lax.broadcasted_iota(jnp.int32, values.shape, 1)
    first = lax.rem(lanes, HEAD) < HEAD // 2
    half = HEAD // 2
    return jnp.where(first, pltpu.roll(values, 128 - half, 1), pltpu.roll(values, half, 1))


def centre(values):
    middle = jnp.mean(values, axis=1, keepdims=True)
    centred = values - middle
    inverse = lax.rsqrt(jnp.mean(centred * centred, axis=1, keepdims=True) + epsilon)
    return centred * inverse


NT = (((1,), (1,)), ((), ()))


def mm(a, b):
    return jnp.dot(a, b, preferred_element_type=jnp.float32)


def mm_nt(a, b):
    return lax.dot_general(a, b, NT, preferred_element_type=jnp.float32)


def forward_kernel(
    names, length_ref, moment_ref, tokens, first_in, second_in, cotangent_in, cosine_in, sine_in, wq, wk, wv, wm,
    q_hbm, k_hbm, v_hbm, heads_hbm, heads_t_hbm, lse_hbm, hidden_hbm, mid_hbm, mlp_t_hbm, one_hbm, two_hbm,
    q_out, k_out, v_out, heads, heads_t, lse, hidden, mid, mlp_t, scale_one, scale_two, cotangent, cosine, sine,
    first_scales, second_scales, nin, vq, vk, vv, vm, other_m, v_t, send_m, recv_m, send_o, recv_o, bias, wsem, osem, tsem, ssem, rsem,
):
    rows, width = tokens.shape
    pairs = q_out.shape[0]
    here = {n: lax.axis_index(n) for n in names}
    other = {**here, names[1]: 1 - here[names[1]]}
    other = tuple(other[n] for n in names)
    loads = [
        pltpu.make_async_copy(a, b, wsem.at[i])
        for i, (a, b) in enumerate(
            ((first_in, first_scales), (wq, vq), (cosine_in, cosine), (sine_in, sine), (wk, vk), (wv, vv), (wm, vm),
             (cotangent_in, cotangent), (second_in, second_scales))
        )
    ]
    for c in loads[:6]:
        c.start()
    barrier = pltpu.get_barrier_semaphore()
    pl.semaphore_signal(barrier, inc=1, device_id=other, device_id_type=MESH)
    pl.semaphore_wait(barrier, 1)
    length = length_ref[0]

    def place(start, count):
        return start + lax.broadcasted_iota(jnp.int32, (count, 1), 0)

    def mask_of(start, count):
        return jnp.where(place(start, count) < length, 1.0, 0.0)

    bias[...] = jnp.broadcast_to((mask_of(0, rows) - 1.0) * 1000000000.0, (rows, 128))

    loads[0].wait()
    scale_one[...] = first_scales[pl.ds(moment_ref[0], 1), :]

    def norm_rows(i, _):
        at = pl.multiple_of(i * 128, 128)
        x = tokens[pl.ds(at, 128), :].astype(jnp.float32) * mask_of(at, 128)
        nin[pl.ds(at, 128), :] = (centre(x) * scale_one[...]).astype(jnp.bfloat16)
        return 0

    lax.fori_loop(0, rows // 128, norm_rows, 0)
    for c in loads[6:]:
        c.start()
    for c in loads[1:6]:
        c.wait()

    def project(i, _):
        at = pl.multiple_of(i * 256, 256)
        own = pl.ds(at, 256)
        x = nin[own, :]
        c, s = cosine[own, :], sine[own, :]
        for ref, w in ((q_out, vq), (k_out, vk)):
            y = mm(x, w[...])
            for p in range(pairs):
                part = y[:, 128 * p : 128 * p + 128]
                ref[p, own, :] = (part * c + swap_halves(part) * s).astype(jnp.bfloat16)
        y = mm(x, vv[...])
        for p in range(pairs):
            part = y[:, 128 * p : 128 * p + 128]
            v_out[p, own, :] = part.astype(jnp.bfloat16)
            v_t[p, :, own] = part.T.astype(jnp.bfloat16)
        return 0

    lax.fori_loop(0, rows // 256, project, 0)
    stores = [
        pltpu.make_async_copy(a, b, osem.at[i])
        for i, (a, b) in enumerate(
            ((q_out, q_hbm), (k_out, k_hbm), (v_out, v_hbm), (heads, heads_hbm), (heads_t, heads_t_hbm), (lse, lse_hbm),
             (mlp_t, mlp_t_hbm), (scale_one, one_hbm), (scale_two, two_hbm))
        )
    ]
    for c in stores[:3]:
        c.start()
    for c in loads[6:]:
        c.wait()
    scale_two[...] = second_scales[pl.ds(moment_ref[0], 1), :]
    send_m[...] = vm[...].astype(jnp.float32)
    merge_copy = pltpu.make_async_remote_copy(
        src_ref=send_m, dst_ref=recv_m, send_sem=ssem.at[0], recv_sem=rsem.at[0],
        device_id=other, device_id_type=MESH,
    )
    merge_copy.start()


    def o_copy(p):
        return pltpu.make_async_remote_copy(
            src_ref=send_o.at[p], dst_ref=recv_o.at[p], send_sem=ssem.at[1 + p], recv_sem=rsem.at[1 + p],
            device_id=other, device_id_type=MESH,
        )

    lane = lax.broadcasted_iota(jnp.int32, (rows, 128), 1)
    block = 1024

    def attend(p, _):
        for h in range(2):
            keys = jnp.where((lane < HEAD) == (h == 0), k_out[p] * 0.125, 0.0).astype(jnp.bfloat16)
            values_t = v_t[p, pl.ds(HEAD * h, HEAD), :]
            for b in range(rows // block):
                cols = pl.ds(b * block, block)
                s = mm_nt(keys, q_out[p, cols, :]) + bias[:, :1]
                peak = jnp.max(s, axis=0, keepdims=True)
                e = jnp.exp(s - peak)
                total = jnp.sum(e, axis=0, keepdims=True)
                o = mm(values_t, e.astype(jnp.bfloat16)) / total
                heads_t[p, pl.ds(HEAD * h, HEAD), cols] = o.astype(jnp.bfloat16)
                lse[pl.ds(2 * p + h, 1), cols] = peak + jnp.log(total)
        o = heads_t[p].astype(jnp.float32).T
        send_o[p] = o
        heads[p] = o.astype(jnp.bfloat16)
        o_copy(p).start()
        count = rows // pairs
        at = pl.multiple_of(p * count, count)
        turned = (cotangent[pl.ds(at, count), :].astype(jnp.float32) * mask_of(at, count)).T
        mlp_t[:, :, pl.ds(at, count)] = turned.astype(jnp.bfloat16).reshape(mlp_t.shape[0], mlp_t.shape[1], count)
        return 0

    lax.fori_loop(0, pairs, attend, 0)
    for c in stores[3:]:
        c.start()

    def merge_own(i, _):
        own = pl.ds(pl.multiple_of(i * 256, 256), 256)
        hidden[own, :] = mm(jnp.concatenate([heads[p, own, :] for p in range(pairs)], axis=1), vm[...])
        return 0

    lax.fori_loop(0, rows // 256, merge_own, 0)
    merge_copy.wait()
    other_m[...] = recv_m[...].astype(jnp.bfloat16)
    for p in range(pairs):
        o_copy(p).wait()

    def tile_stores(i):
        own = pl.ds(pl.multiple_of(i * 256, 256), 256)
        return [
            pltpu.make_async_copy(hidden.at[own, :], hidden_hbm.at[own, :], tsem.at[0, i]),
            pltpu.make_async_copy(mid.at[own, :], mid_hbm.at[own, :], tsem.at[1, i]),
        ]

    def finish(i, _):
        at = pl.multiple_of(i * 256, 256)
        own = pl.ds(at, 256)
        theirs = jnp.concatenate([recv_o[p, own, :].astype(jnp.bfloat16) for p in range(pairs)], axis=1)
        attn = hidden[own, :] + mm(theirs, other_m[...])
        one = tokens[own, :].astype(jnp.float32) * mask_of(at, 256) + attn
        hidden[own, :] = one
        mid[own, :] = (centre(one) * scale_two[...]).astype(jnp.bfloat16)
        for c in tile_stores(i):
            c.start()
        return 0

    lax.fori_loop(0, rows // 256, finish, 0)
    for c in stores:
        c.wait()
    for i in range(rows // 256):
        for c in tile_stores(i):
            c.wait()


def forward(names, length, moment, tokens, first_scales, second_scales, cotangent, cosine, sine, wq, wk, wv, wm):
    rows, width = tokens.shape
    local = wq.shape[1]
    pairs = local // 128
    vmem = pl.BlockSpec(memory_space=pltpu.VMEM)
    hbm = pl.BlockSpec(memory_space=pl.ANY)
    half = jnp.bfloat16
    full = jnp.float32
    shapes = [
        ((pairs, rows, 128), half),
        ((pairs, rows, 128), half),
        ((pairs, rows, 128), half),
        ((pairs, rows, 128), half),
        ((pairs, 128, rows), half),
        ((2 * pairs, rows), full),
        ((rows, width), full),
        ((rows, width), half),
        ((16, width // 16, rows), half),
        ((1, width), full),
        ((1, width), full),
    ]
    return pl.pallas_call(
        functools.partial(forward_kernel, names),
        out_shape=[jax.ShapeDtypeStruct(*s) for s in shapes],
        in_specs=[pl.BlockSpec(memory_space=pltpu.SMEM)] * 2 + [vmem] + [hbm] * 9,
        out_specs=[hbm] * len(shapes),
        scratch_shapes=[pltpu.VMEM(*s) for s in shapes]
        + [
            pltpu.VMEM((rows, width), half),
            pltpu.VMEM((rows, 128), full),
            pltpu.VMEM((rows, 128), full),
            pltpu.VMEM(first_scales.shape, full),
            pltpu.VMEM(second_scales.shape, full),
            pltpu.VMEM((rows, width), half),
            pltpu.VMEM(wq.shape, half),
            pltpu.VMEM(wk.shape, half),
            pltpu.VMEM(wv.shape, half),
            pltpu.VMEM(wm.shape, half),
            pltpu.VMEM(wm.shape, half),
            pltpu.VMEM((pairs, 128, rows), half),
            pltpu.VMEM(wm.shape, full),
            pltpu.VMEM(wm.shape, full),
            pltpu.VMEM((pairs, rows, 128), full),
            pltpu.VMEM((pairs, rows, 128), full),
            pltpu.VMEM((rows, 128), full),
            pltpu.SemaphoreType.DMA((9,)),
            pltpu.SemaphoreType.DMA((9,)),
            pltpu.SemaphoreType.DMA((2, 4)),
            pltpu.SemaphoreType.DMA((1 + pairs,)),
            pltpu.SemaphoreType.DMA((1 + pairs,)),
        ],
        compiler_params=pltpu.CompilerParams(collective_id=1, has_side_effects=True, vmem_limit_bytes=58 * 2**20),
        name="forward",
    )(length, moment, tokens, first_scales, second_scales, cotangent, cosine, sine, wq, wk, wv, wm)


ITEMS = 24
TILE = 256
RING = 5
HELD = 12
LAGS = (4, 6, 8, 10)
FIRSTS = (0, 8, 16, 18, 24)


def count_from(i, starts):
    total = 0
    for start in starts:
        total = total + jnp.where(i >= start, 1, 0)
    return total


def flip(index, weight):
    return index + weight * (1 - 2 * lax.rem(lax.div(index, weight), 2))


def weight_of(color, stage):
    k = lax.rem(color + stage, 3)
    return 1 + (k * (k + 1)) // 2


STARTS_Z = (2, 5, 10, 15, 19)


def color_of(i):
    turn = i - count_from(i, [p + 1 for p in STARTS_Z])
    on_z = sum(jnp.where(i == p, 1, 0) for p in STARTS_Z)
    return jnp.where(on_z == 1, 2, lax.rem(turn, 2))


def slot_of(i):
    return count_from(i, (8, 16)) - 2 * count_from(i, (18,))


def backward_kernel(
    names, length_ref, moment_ref, scale_one, scale_two,
    l_down, mid_in, heads, q_in, k_in, v_in, heads_t, lse_in, cosine, sine,
    merge_in, wq, wk, wv, tokens, hidden, cotangent, wu, wd,
    out, rows_out, tokens_out, layer_out, r_down, slope, r_up, hidden_grad,
    left, s1, r1, r2, r3, r4, rb, qkv, send_p, recv_p, ga, terms,
    msem, lsem, rsem, fsem, ssem, csem, psem, qsem, gsem, jsem, credit, credit_two, core_free,
):
    here = {n: lax.axis_index(n) for n in names}
    d = here[names[0]]

    def device(**moved):
        at = {**here, **moved}
        return tuple(at[n] for n in names)

    core = device(**{names[1]: 1 - here[names[1]]})

    def across(weight):
        return device(**{names[0]: flip(d, weight)})

    def absolute(r):
        total = 0
        for b in range(4):
            bit = lax.rem(lax.div(d, 2**b), 2)
            total = total + (2**b) * (1 - bit if (r >> b) & 1 else bit)
        return total

    def load_left(source, slot):
        for r in range(16):
            pltpu.make_async_copy(source.at[absolute(r)], left.at[slot, r], lsem).start()

    def left_loaded(slot):
        pltpu.make_async_copy(left.at[slot], left.at[slot], lsem).wait()

    def turn(values, slot, own):
        turned = values.T.astype(jnp.bfloat16)
        for c in range(16):
            left[slot, absolute(c), :, own] = turned[64 * c : 64 * c + 64]

    mid_load = pltpu.make_async_copy(mid_in, ga, msem)
    mid_load.start()
    load_left(l_down, 0)
    barrier = pltpu.get_barrier_semaphore()
    for weight in (1, 2, 4, 8):
        pl.semaphore_signal(barrier, inc=1, device_id=across(weight), device_id_type=MESH)
    pl.semaphore_signal(barrier, inc=1, device_id=core, device_id_type=MESH)
    pl.semaphore_wait(barrier, 5)

    def fetch(i, lane):
        slot = lax.rem(i, 2)
        target, sem = rb.at[lane, slot], fsem.at[lane, slot]
        for g, source in ((0, r_down), (1, r_up)):
            @pl.when((i >= FIRSTS[g]) & (i < FIRSTS[g + 1]))
            def _():
                col = pl.multiple_of((i - FIRSTS[g]) * TILE, TILE)
                pltpu.make_async_copy(source.at[:, pl.ds(col, TILE)], target, sem).start()

        @pl.when((i >= FIRSTS[2]) & (i < FIRSTS[3]))
        def _():
            for k in range(2):
                pltpu.make_async_copy(
                    heads.at[2 * (i - FIRSTS[2]) + k], target.at[:, pl.ds(128 * k, 128)], sem
                ).start()

        @pl.when(i >= FIRSTS[3])
        def _():
            pltpu.make_async_copy(qkv.at[i - FIRSTS[3]], target, sem).start()

    def fetched(i, lane):
        slot = lax.rem(i, 2)
        pltpu.make_async_copy(rb.at[lane, slot], rb.at[lane, slot], fsem.at[lane, slot]).wait()

    def product(i, first, lane):
        color, slot = color_of(i), slot_of(i)
        weights = [weight_of(color, s) for s in range(3)] + [8]
        rows = []
        for bits in range(8):
            r = first * weights[0] + sum(((bits >> (2 - k)) & 1) * weights[1 + k] for k in range(3))
            rows.append(left[slot, r])
        lhs = jnp.concatenate(rows, axis=0)
        return mm(lhs, rb[lane, lax.rem(i, 2)]).reshape(8, 64, TILE)

    def copy(i, s):
        weight = weight_of(color_of(i), s) if s < 3 else 8
        src = (s1.at[lax.rem(i, RING)], r1.at[lax.rem(i, HELD), pl.ds(4, 4)], r2.at[lax.rem(i, HELD), pl.ds(2, 2)], r3.at[i, pl.ds(1, 1)])[s]
        dst = (r1.at[lax.rem(i, HELD)], r2.at[lax.rem(i, HELD)], r3.at[i], r4.at[i])[s]
        return pltpu.make_async_remote_copy(
            src_ref=src, dst_ref=dst, send_sem=ssem.at[s, i], recv_sem=csem.at[s, i],
            device_id=across(weight), device_id_type=MESH,
        )

    def result(i):
        return pltpu.make_async_copy(r4.at[i, 0], out.at[i], rsem.at[i])

    def tick(i):
        e = i - LAGS[3]

        @pl.when((e >= 0) & (e < ITEMS))
        def _():
            copy(e, 3).wait_recv()
            r4[e, 0] = r4[e, 0] + r3[e, 0]
            result(e).start()

        c = i - LAGS[2]

        @pl.when((c >= 0) & (c < ITEMS))
        def _():
            copy(c, 2).wait_recv()
            r3[c] += r2[lax.rem(c, HELD), 0:2]
            copy(c, 3).start()
            copy(c, 2).wait_send()

            @pl.when(c + HELD < ITEMS)
            def _():
                color = color_of(c + HELD)
                pl.semaphore_signal(
                    credit_two.at[color], inc=1, device_id=across(weight_of(color, 1)), device_id_type=MESH
                )

        b = i - LAGS[1]

        @pl.when((b >= 0) & (b < ITEMS))
        def _():
            copy(b, 1).wait_recv()
            r2[lax.rem(b, HELD)] += r1[lax.rem(b, HELD), 0:4]
            copy(b, 2).start()
            copy(b, 1).wait_send()

            @pl.when(b + HELD < ITEMS)
            def _():
                color = color_of(b + HELD)
                pl.semaphore_signal(
                    credit.at[color], inc=1, device_id=across(weight_of(color, 0)), device_id_type=MESH
                )

        a = i - LAGS[0]

        @pl.when((a >= 0) & (a < ITEMS))
        def _():
            fetched(a, 1)
            copy(a, 0).wait_recv()
            r1[lax.rem(a, HELD)] += product(a, 0, 1)

            @pl.when(a >= HELD)
            def _():
                pl.semaphore_wait(credit_two.at[color_of(a)], 1)

            copy(a, 1).start()

            @pl.when(a + 2 < ITEMS)
            def _():
                fetch(a + 2, 1)

        @pl.when(i < ITEMS)
        def _():
            @pl.when(i >= RING)
            def _():
                copy(i - RING, 0).wait_send()

            @pl.when(i >= LAGS[0])
            def _():
                fetched(i, 0)

            s1[lax.rem(i, RING)] = product(i, 1, 0)

            @pl.when(i >= HELD)
            def _():
                pl.semaphore_wait(credit.at[color_of(i)], 1)

            copy(i, 0).start()

            @pl.when((i + 2 < ITEMS) & (i >= LAGS[0]))
            def _():
                fetch(i + 2, 0)

    rows, width = tokens.shape
    pairs = q_in.shape[0]
    length = length_ref[0]
    part = 256
    parts = rows // part
    half, full = jnp.bfloat16, jnp.float32

    def keep_of(at):
        return jnp.where(at + lax.broadcasted_iota(jnp.int32, (part, 1), 0) < length, 1.0, 0.0)

    def core_copy(use, i):
        return pltpu.make_async_remote_copy(
            src_ref=send_p.at[i], dst_ref=recv_p.at[i], send_sem=psem.at[use, i], recv_sem=qsem.at[use, i],
            device_id=core, device_id_type=MESH,
        )

    def core_sent(use):
        for i in range(parts):
            core_copy(use, i).wait_send()
        if use < 2:
            pl.semaphore_signal(core_free, inc=1, device_id=core, device_id_type=MESH)
            pl.semaphore_wait(core_free, 1)

    def norm_parts(values):
        centred = values - jnp.mean(values, axis=1, keepdims=True)
        inverse = lax.rsqrt(jnp.mean(centred * centred, axis=1, keepdims=True) + epsilon)
        return centred * inverse, inverse

    def norm_grad(grad, normed, inverse, scale):
        hat = grad * scale
        middle = jnp.mean(hat, axis=1, keepdims=True)
        return inverse * (hat - middle - normed * jnp.mean(hat * normed, axis=1, keepdims=True))

    def run_ticks(first, last):
        lax.fori_loop(first, last, lambda i, _: (tick(i), 0)[1], 0)

    def mlp(vu, vd, cot, wide, hid, gp, gh, wsem, usem, dsem, tsem, osem):
        tiles = wu.shape[1] // TILE

        def columns(k):
            return pl.ds(pl.multiple_of(k * TILE, TILE), TILE)

        def up_load(k):
            return pltpu.make_async_copy(wu.at[:, columns(k)], vu.at[:, columns(k)], usem.at[k])

        for k in range(2):
            up_load(k).start()
        down_load = pltpu.make_async_copy(wd, vd, wsem)

        def tile_stores(k, lane):
            slot = lax.rem(k, 2)
            return (
                pltpu.make_async_copy(rb.at[lane, slot], r_down.at[:, columns(k)], dsem.at[0, slot]),
                pltpu.make_async_copy(qkv.at[slot], slope.at[:, columns(k)], dsem.at[1, slot]),
            )

        def up_tile(k, lane):
            slot = lax.rem(k, 2)

            @pl.when(k >= 2)
            def _():
                for x in tile_stores(k - 2, lane):
                    x.wait()

            up_load(k).wait()

            @pl.when(k + 2 < tiles)
            def _():
                up_load(k + 2).start()

            for r in range(0, rows, 512):
                v = mm(ga[r : r + 512, :], vu[:, columns(k)])
                square = v * v
                t = jnp.tanh(0.7978845608028654 * v * (1.0 + 0.044715 * square))
                above = 0.5 * (1.0 + t)
                rb[lane, slot, r : r + 512, :] = (v * above).astype(half)
                qkv[slot, r : r + 512, :] = (
                    above + 0.5 * v * (1.0 - t * t) * (0.7978845608028654 * (1.0 + 0.134145 * square))
                ).astype(half)
            for x in tile_stores(k, lane):
                x.start()

        def tile(source, target, n, i):
            own = pl.ds(pl.multiple_of(i * part, part), part)
            slot = lax.rem(i, 2)
            return pltpu.make_async_copy(source.at[own, :], target.at[slot], tsem.at[n, slot])

        def stream(sources, i, body):
            for n, source, target in sources:
                tile(source, target, n, i).wait()

                @pl.when(i + 1 < parts)
                def _():
                    tile(source, target, n, i + 1).start()

            return body(i, pl.multiple_of(i * part, part), lax.rem(i, 2))

        def begin(sources):
            for n, source, target in sources:
                tile(source, target, n, jnp.int32(0)).start()

        mid_load.wait()
        left_loaded(0)

        def early(k, _):
            up_tile(k, 0)
            tick(k)
            return 0

        lax.fori_loop(0, LAGS[0], early, 0)
        down_load.start()
        lax.fori_loop(LAGS[0], tiles, lambda k, _: (up_tile(k, 1), 0)[1], 0)
        for k in (tiles - 2, tiles - 1):
            for x in tile_stores(k, 1):
                x.wait()
        for i in range(2):
            fetch(jnp.int32(i), 1)
            fetch(jnp.int32(LAGS[0] + i), 0)
        streams = ((0, cotangent, cot), (1, slope, wide))
        begin(streams)
        down_load.wait()

        def store_pre(i):
            own = pl.ds(pl.multiple_of(i * part, part), part)
            return pltpu.make_async_copy(gp, r_up.at[own, :], osem.at[0])

        def first(i, at, slot):
            x = (cot[slot].astype(full) * keep_of(at)).astype(half)
            g = mm_nt(x, vd[...]) * wide[slot].astype(full)

            @pl.when(i > 0)
            def _():
                store_pre(i - 1).wait()

            gp[...] = g.astype(half)
            store_pre(i).start()
            send_p[i] = mm_nt(gp[...], vu[...])
            core_copy(0, i).start()

            @pl.when(i < 2)
            def _():
                tick(LAGS[0] + i)

            return 0

        lax.fori_loop(0, parts, lambda i, _: stream(streams, i, first), 0)
        store_pre(parts - 1).wait()
        run_ticks(LAGS[0] + 2, LAGS[0] + 4)
        streams_two = ((0, cotangent, cot), (2, hidden, hid))
        begin(streams_two)

        def store_hidden(i):
            own = pl.ds(pl.multiple_of(i * part, part), part)
            return pltpu.make_async_copy(gh, hidden_grad.at[own, :], osem.at[1])

        def second(i, at, slot, total):
            own = pl.ds(at, part)
            normed, inverse = norm_parts(hid[slot])
            turn(normed * scale_two[...], 1, own)
            core_copy(0, i).wait_recv()
            grad = send_p[i] + recv_p[i]

            @pl.when(i > 0)
            def _():
                store_hidden(i - 1).wait()

            gh[...] = cot[slot].astype(full) * keep_of(at) + norm_grad(grad, normed, inverse, scale_two[...])
            store_hidden(i).start()
            ga[own, :] = gh[...].astype(half)
            turn(gh[...], 2, own)
            return total + jnp.sum(grad * normed, axis=0, keepdims=True)

        term = lax.fori_loop(
            0, parts, lambda i, total: stream(streams_two, i, functools.partial(second, total=total)),
            jnp.zeros((1, width), full),
        )
        for j in range(8):
            terms[0, 8 + j : 9 + j, :] = term[:, 128 * j : 128 * j + 128]
        store_hidden(parts - 1).wait()
        core_sent(0)
        streams_three = ((1, r_down, wide),)
        begin(streams_three)

        def third(i, at, slot):
            send_p[i] = mm(wide[slot], vd[...])
            core_copy(1, i).start()
            return 0

        lax.fori_loop(0, parts, lambda i, _: stream(streams_three, i, third), 0)
        streams_four = ((2, hidden, hid),)
        begin(streams_four)
        tick(jnp.int32(LAGS[0] + 4))

        def store_layer(i):
            own = pl.ds(pl.multiple_of(i * part, part), part)
            return pltpu.make_async_copy(cot.at[0], layer_out.at[own, :], osem.at[0])

        def fourth(i, at, slot):
            core_copy(1, i).wait_recv()

            @pl.when(i > 0)
            def _():
                store_layer(i - 1).wait()

            cot[0] = ((hid[slot] + (send_p[i] + recv_p[i])) * keep_of(at)).astype(half)
            store_layer(i).start()
            return 0

        lax.fori_loop(0, parts, lambda i, _: stream(streams_four, i, fourth), 0)
        store_layer(parts - 1).wait()
        core_sent(1)

    pl.run_scoped(
        mlp,
        pltpu.VMEM(wu.shape, half),
        pltpu.VMEM(wd.shape, half),
        pltpu.VMEM((2, part, width), half),
        pltpu.VMEM((2, part, wu.shape[1]), half),
        pltpu.VMEM((2, part, width), full),
        pltpu.VMEM((part, wu.shape[1]), half),
        pltpu.VMEM((part, width), full),
        pltpu.SemaphoreType.DMA,
        pltpu.SemaphoreType.DMA((wu.shape[1] // TILE,)),
        pltpu.SemaphoreType.DMA((2, 2)),
        pltpu.SemaphoreType.DMA((3, 2)),
        pltpu.SemaphoreType.DMA((2,)),
    )

    def attention(q, k, v, o_t, lse, wm, cos, sin, bias, do, do_t, kh, vh, k_t, dq_t, asem):
        loads = [
            pltpu.make_async_copy(a, b, asem.at[n])
            for n, (a, b) in enumerate(
                ((q_in, q), (k_in, k), (v_in, v), (heads_t, o_t), (lse_in, lse), (merge_in, wm),
                 (cosine, cos), (sine, sin))
            )
        ]
        for x in loads:
            x.start()
        for x in loads:
            x.wait()
        place = lax.broadcasted_iota(jnp.int32, (rows, 128), 0)
        bias[...] = (jnp.where(place < length, 1.0, 0.0) - 1.0) * 1000000000.0
        lane = lax.broadcasted_iota(jnp.int32, (rows, 128), 1) < HEAD
        block = 256

        def unrotate_lanes(y):
            return (y * cos[...] - swap_halves(y) * sin[...]).astype(jnp.bfloat16)

        def pair(p, _):
            weight = wm[pl.ds(pl.multiple_of(128 * p, 128), 128), :]
            do[...] = mm_nt(ga[...], weight).astype(jnp.bfloat16)
            do_t[...] = mm_nt(weight, ga[...]).astype(jnp.bfloat16)
            k_t[...] = (k[p].astype(jnp.float32) * 0.125).T.astype(jnp.bfloat16)
            product_t = do_t[...].astype(jnp.float32) * o_t[p].astype(jnp.float32)
            dks, dvs = [], []
            for h in range(2):
                tick(LAGS[0] + 5 + 2 * p + h)
                delta = jnp.sum(product_t[HEAD * h : HEAD * h + HEAD], axis=0, keepdims=True)
                own = lane == (h == 0)
                kh[...] = jnp.where(own, k[p].astype(jnp.float32) * 0.125, 0.0).astype(jnp.bfloat16)
                vh[...] = jnp.where(own, v[p].astype(jnp.float32), 0.0).astype(jnp.bfloat16)
                dk = jnp.zeros((rows, 128), jnp.float32)
                dv = jnp.zeros((rows, 128), jnp.float32)
                for b in range(0, rows, block):
                    cols = slice(b, b + block)
                    qb = q[p, cols, :]
                    s = mm_nt(kh[...], qb) + bias[:, :1]
                    soft = jnp.exp(s - lse[pl.ds(2 * p + h, 1), cols])
                    ds = soft * (mm(vh[...], do_t[:, cols]) - delta[:, cols])
                    ds = ds.astype(jnp.bfloat16)
                    dv = dv + mm(soft.astype(jnp.bfloat16), do[cols, :])
                    dk = dk + mm(ds, qb)
                    dq_t[HEAD * h : HEAD * h + HEAD, cols] = mm(k_t[HEAD * h : HEAD * h + HEAD, :], ds)
                dks.append(dk)
                dvs.append(dv)
            quad = 3 * lax.div(p, 2)
            at = pl.ds(pl.multiple_of(128 * lax.rem(p, 2), 128), 128)
            qkv[quad, :, at] = unrotate_lanes(dq_t[...].T)
            qkv[quad + 1, :, at] = unrotate_lanes(jnp.where(lane, dks[0], dks[1]) * 0.125)
            qkv[quad + 2, :, at] = jnp.where(lane, dvs[0], dvs[1]).astype(jnp.bfloat16)
            return 0

        lax.fori_loop(0, pairs, pair, 0)

    pl.run_scoped(
        attention,
        pltpu.VMEM((pairs, rows, 128), half),
        pltpu.VMEM((pairs, rows, 128), half),
        pltpu.VMEM((pairs, rows, 128), half),
        pltpu.VMEM((pairs, 128, rows), half),
        pltpu.VMEM((2 * pairs, rows), full),
        pltpu.VMEM(merge_in.shape, half),
        pltpu.VMEM((rows, 128), full),
        pltpu.VMEM((rows, 128), full),
        pltpu.VMEM((rows, 128), full),
        pltpu.VMEM((rows, 128), half),
        pltpu.VMEM((128, rows), half),
        pltpu.VMEM((rows, 128), half),
        pltpu.VMEM((rows, 128), half),
        pltpu.VMEM((128, rows), half),
        pltpu.VMEM((128, rows), full),
        pltpu.SemaphoreType.DMA((10,)),
    )

    def inner(vq, vk, vv, x_in, gh, to, sem, hsem, osem):
        loads = [
            pltpu.make_async_copy(a, b, sem.at[n])
            for n, (a, b) in enumerate(((wq, vq), (wk, vk), (wv, vv), (tokens, x_in)))
        ]
        for x in loads:
            x.start()
        for x in loads:
            x.wait()

        def send(i, _):
            at = pl.multiple_of(i * part, part)
            own = pl.ds(at, part)
            total = None
            for quad in range(2):
                for n, w in enumerate((vq, vk, vv)):
                    term = mm_nt(qkv[3 * quad + n, own, :], w[:, TILE * quad : TILE * quad + TILE])
                    total = term if total is None else total + term
            send_p[i] = total
            core_copy(2, i).start()
            normed, _ = norm_parts(x_in[own, :].astype(full) * keep_of(at))
            turn(normed * scale_one[...], 0, own)

            @pl.when(i == 1)
            def _():
                tick(LAGS[0] + 13)

            return 0

        lax.fori_loop(0, parts, send, 0)

        def store_tokens(i):
            own = pl.ds(pl.multiple_of(i * part, part), part)
            return pltpu.make_async_copy(to, tokens_out.at[own, :], osem)

        def take(i, total):
            at = pl.multiple_of(i * part, part)
            own = pl.ds(at, part)
            hidden_copy = pltpu.make_async_copy(hidden_grad.at[own, :], gh, hsem)
            hidden_copy.start()

            @pl.when(i < 2)
            def _():
                tick(LAGS[0] + 14 + i)

            core_copy(2, i).wait_recv()
            grad = send_p[i] + recv_p[i]
            keep = keep_of(at)
            normed, inverse = norm_parts(x_in[own, :].astype(full) * keep)
            back = norm_grad(grad, normed, inverse, scale_one[...])
            hidden_copy.wait()

            @pl.when(i > 0)
            def _():
                store_tokens(i - 1).wait()

            to[...] = ((gh[...] + back) * keep).astype(half)
            store_tokens(i).start()
            return total + jnp.sum(grad * normed, axis=0, keepdims=True)

        first = lax.fori_loop(0, parts, take, jnp.zeros((1, width), full))
        store_tokens(parts - 1).wait()
        core_sent(2)
        for j in range(8):
            terms[0, j : j + 1, :] = first[:, 128 * j : 128 * j + 128]
        terms[0, 16:24, :] = jnp.full((8, 128), moment_ref[0].astype(full), full)

    pl.run_scoped(
        inner,
        pltpu.VMEM(wq.shape, half),
        pltpu.VMEM(wk.shape, half),
        pltpu.VMEM(wv.shape, half),
        pltpu.VMEM((rows, width), half),
        pltpu.VMEM((part, width), full),
        pltpu.VMEM((part, width), half),
        pltpu.SemaphoreType.DMA((4,)),
        pltpu.SemaphoreType.DMA,
        pltpu.SemaphoreType.DMA,
    )
    done = LAGS[0] + 16
    for stage in range(4):
        held = 2**stage
        exchange = pltpu.make_async_remote_copy(
            src_ref=terms.at[pl.ds(0, held)], dst_ref=terms.at[pl.ds(held, held)],
            send_sem=gsem.at[stage], recv_sem=jsem.at[stage], device_id=across(held), device_id_type=MESH,
        )
        exchange.start()
        tick(jnp.int32(done + stage))
        exchange.wait()
    table_rows = rows_out.shape[1]
    upper = lax.rem(d, 2) == 1
    places = lax.broadcasted_iota(jnp.int32, (table_rows, 128), 0).astype(full)
    total = jnp.zeros((table_rows, 128), full)
    for n in range(16):
        row = []
        for base in (0, 8):
            piece = terms[n, pl.ds(base + lax.div(d, 2), 1), :]
            row.append(jnp.where(upper, piece[:, 64:], piece[:, :64]))
        total = total + jnp.where(places == terms[n, 16:17, :], jnp.concatenate(row, axis=1), 0.0)
    rows_out[...] = total.T
    run_ticks(done + 4, ITEMS + LAGS[3])

    def drain(i, _):
        @pl.when(i >= ITEMS - RING)
        def _():
            copy(i, 0).wait_send()

        copy(i, 3).wait_send()
        result(i).wait()
        return 0

    lax.fori_loop(0, ITEMS, drain, 0)


def backward(names, table_rows, length, moment, scale_one, scale_two, *arrays):
    tokens, up = arrays[-5], arrays[-2]
    rows, width = tokens.shape
    smem = pl.BlockSpec(memory_space=pltpu.SMEM)
    vmem = pl.BlockSpec(memory_space=pltpu.VMEM)
    hbm = pl.BlockSpec(memory_space=pl.ANY)
    half, full = jnp.bfloat16, jnp.float32
    dma = pltpu.SemaphoreType.DMA
    return pl.pallas_call(
        functools.partial(backward_kernel, names),
        out_shape=[
            jax.ShapeDtypeStruct((ITEMS, 64, TILE), full),
            jax.ShapeDtypeStruct((128, table_rows), full),
            jax.ShapeDtypeStruct((rows, width), half),
            jax.ShapeDtypeStruct((rows, width), half),
            jax.ShapeDtypeStruct((rows, up.shape[1]), half),
            jax.ShapeDtypeStruct((rows, up.shape[1]), half),
            jax.ShapeDtypeStruct((rows, up.shape[1]), half),
            jax.ShapeDtypeStruct((rows, width), full),
        ],
        in_specs=[smem] * 2 + [vmem] * 2 + [hbm] * len(arrays),
        out_specs=[hbm, vmem] + [hbm] * 6,
        scratch_shapes=[
            pltpu.VMEM((3, 16, 64, rows), half),
            pltpu.VMEM((RING, 8, 64, TILE), full),
            pltpu.VMEM((HELD, 8, 64, TILE), full),
            pltpu.VMEM((HELD, 4, 64, TILE), full),
            pltpu.VMEM((ITEMS, 2, 64, TILE), full),
            pltpu.VMEM((ITEMS, 1, 64, TILE), full),
            pltpu.VMEM((2, 2, rows, TILE), half),
            pltpu.VMEM((6, rows, TILE), half),
            pltpu.VMEM((rows // 256, 256, width), full),
            pltpu.VMEM((rows // 256, 256, width), full),
            pltpu.VMEM((rows, width), half),
            pltpu.VMEM((16, 24, 128), full),
            dma,
            dma,
            dma((ITEMS,)),
            dma((2, 2)),
            dma((4, ITEMS)),
            dma((4, ITEMS)),
            dma((3, 4)),
            dma((3, 4)),
            dma((4,)),
            dma((4,)),
            pltpu.SemaphoreType.REGULAR((3,)),
            pltpu.SemaphoreType.REGULAR((3,)),
            pltpu.SemaphoreType.REGULAR,
        ],
        compiler_params=pltpu.CompilerParams(
            collective_id=0, has_side_effects=True, vmem_limit_bytes=60 * 2**20
        ),
        name="backward",
    )(length, moment, scale_one, scale_two, *arrays)


def finish_kernel(
    pieces_in, tables_in, tokens_in, layer_in,
    layer_out, tokens_out, grad_q, grad_k, grad_v, grad_m, grad_u, grad_d, first, second,
    pieces, tables, held, isem, osem,
):
    parts = held.shape[1]
    step = layer_in.shape[0] // parts
    incoming, outgoing = [], []

    def move(source, keep, target):
        n = len(incoming)
        incoming.append(pltpu.make_async_copy(source, keep, isem.at[n]))
        outgoing.append(pltpu.make_async_copy(keep, target, osem.at[n]))

    for n, (source, target) in enumerate(((layer_in, layer_out), (tokens_in, tokens_out))):
        for k in range(parts):
            own = pl.ds(k * step, step)
            move(source.at[own, :], held.at[n, k], target.at[own, :])
    targets = [(grad_d, k) for k in range(8)] + [(grad_u, k) for k in range(8)] + [(grad_m, k) for k in range(2)]
    targets += [(ref, k) for k in range(2) for ref in (grad_q, grad_k, grad_v)]
    count = first.shape[0]
    for k, ref in enumerate((first, second)):
        own = pl.ds(k * count, count)
        move(tables_in.at[own, :], tables.at[own, :], ref)
    results = []
    for n, (ref, k) in enumerate(targets):
        results.append(
            pltpu.make_async_copy(pieces.at[n], ref.at[:, pl.ds(TILE * k, TILE)], osem.at[len(incoming) + n])
        )
    whole = pltpu.make_async_copy(pieces_in, pieces, isem.at[len(incoming)])
    whole.start()
    for c in incoming:
        c.start()
    whole.wait()
    for c in results:
        c.start()
    for a, b in zip(incoming, outgoing):
        a.wait()
        b.start()
    for c in results + outgoing:
        c.wait()


def finish(pieces, tables, tokens, layer):
    hbm = pl.BlockSpec(memory_space=pl.ANY)
    full = jnp.float32
    rows, width = layer.shape
    table_rows = tables.shape[1]
    shapes = [(64, 512)] * 4 + [(64, 2048), (64, 2048), (64, table_rows), (64, table_rows)]
    layer, tokens, *grads = pl.pallas_call(
        finish_kernel,
        out_shape=[jax.ShapeDtypeStruct(a.shape, a.dtype) for a in (layer, tokens)]
        + [jax.ShapeDtypeStruct(s, full) for s in shapes],
        in_specs=[hbm] * 4,
        out_specs=[hbm] * (2 + len(shapes)),
        scratch_shapes=[
            pltpu.VMEM(pieces.shape, full),
            pltpu.VMEM(tables.shape, full),
            pltpu.VMEM((2, 1, rows // 1, width), layer.dtype),
            pltpu.SemaphoreType.DMA((28,)),
            pltpu.SemaphoreType.DMA((28,)),
        ],
        name="finish",
    )(pieces, tables, tokens, layer)
    query, key, value, merge, up, down, first, second = grads
    return layer[None], tokens[None], query, key, value, merge.T, up, down.T, first.T, second.T


def fast_body(
    tokens,
    cotangent,
    lengths,
    noise_times,
    query_weight,
    key_weight,
    value_weight,
    merge_weight,
    up_weight,
    down_weight,
    first_scales,
    second_scales,
):
    tokens, cotangent = tokens[0], cotangent[0]
    rows, width = tokens.shape
    names = ("dp", "tensor")
    cosine, sine = (jnp.asarray(a) for a in rope_lanes(rows))
    query, key, value, heads, heads_t, lse, hidden, normal_mid, mlp_t, scale_one, scale_two = forward(
        names, lengths, noise_times, tokens, first_scales, second_scales, cotangent, cosine, sine,
        query_weight, key_weight, value_weight, merge_weight,
    )
    pieces, tables, grad_tokens, layer_output, *_ = backward(
        names, first_scales.shape[0], lengths, noise_times, scale_one, scale_two,
        mlp_t, normal_mid, heads, query, key, value, heads_t, lse, cosine, sine,
        merge_weight, query_weight, key_weight, value_weight, tokens, hidden, cotangent, up_weight, down_weight,
    )
    return finish(pieces, tables, grad_tokens, layer_output)


def body(
    tokens,
    cotangent,
    lengths,
    noise_times,
    query_weight,
    key_weight,
    value_weight,
    merge_weight,
    up_weight,
    down_weight,
    first_scales,
    second_scales,
):
    seq_count, length, width = tokens.shape
    local_width = query_weight.shape[1]
    local_heads = local_width // HEAD
    table_rows = first_scales.shape[0]
    flat_rows = seq_count * length
    scale_factor = 1.0 / math.sqrt(HEAD)
    block_rows = min(512, length)
    head_shape = (seq_count, length, local_heads, HEAD)
    row_mask = (jnp.arange(length, dtype=jnp.int32)[None, :] < lengths[:, None]).astype(jnp.float32)
    key_bias = (row_mask - 1.0) * 1000000000.0
    one_hot = (noise_times[:, None] == jnp.arange(table_rows, dtype=jnp.int32)[None, :]).astype(
        jnp.float32
    )
    scale_one = jnp.dot(one_hot, first_scales, precision=highest)
    scale_two = jnp.dot(one_hot, second_scales, precision=highest)
    cos_table, sin_table = rope_tables(length, HEAD)
    inputs = tokens.astype(jnp.float32) * row_mask[:, :, None]
    normed_one, inv_one = normalize(inputs)
    normal_in = (normed_one * scale_one[:, None, :]).astype(jnp.bfloat16).reshape(flat_rows, width)
    queries = jnp.dot(normal_in, query_weight, preferred_element_type=jnp.float32).reshape(
        head_shape
    )
    key_proj = jnp.dot(normal_in, key_weight, preferred_element_type=jnp.float32).reshape(
        head_shape
    )
    value_rows = (
        jnp.dot(normal_in, value_weight, preferred_element_type=jnp.float32)
        .astype(jnp.bfloat16)
        .reshape(head_shape)
    )
    query_rot = rotate(queries, cos_table, sin_table).astype(jnp.bfloat16)
    key_rot = rotate(key_proj, cos_table, sin_table).astype(jnp.bfloat16)
    attended = []
    log_sums = []
    for offset in range(0, length, block_rows):
        scores = block_scores(
            query_rot[:, offset : offset + block_rows], key_rot, key_bias, scale_factor
        )
        peak_score = jnp.max(scores, axis=-1, keepdims=True)
        exponent = jnp.exp(scores - peak_score)
        totals = jnp.sum(exponent, axis=-1, keepdims=True)
        soft_weights = (exponent / totals).astype(jnp.bfloat16)
        log_sums.append(peak_score + jnp.log(totals))
        attended.append(
            jnp.einsum(
                "shqk,skhd->sqhd", soft_weights, value_rows, preferred_element_type=jnp.float32
            )
        )
    heads_out = (
        jnp.concatenate(attended, axis=1).astype(jnp.bfloat16).reshape(flat_rows, local_width)
    )
    attn_part = jnp.dot(heads_out, merge_weight, preferred_element_type=jnp.float32)
    attn_total = lax.psum(attn_part, "tensor")
    hidden_one = inputs + attn_total.reshape(seq_count, length, width)
    normed_two, inv_two = normalize(hidden_one)
    normal_mid = (normed_two * scale_two[:, None, :]).astype(jnp.bfloat16).reshape(flat_rows, width)
    pre_act = jnp.dot(normal_mid, up_weight, preferred_element_type=jnp.float32)
    activated = gelu_tanh(pre_act).astype(jnp.bfloat16)
    mlp_part = jnp.dot(activated, down_weight, preferred_element_type=jnp.float32)
    mlp_total = lax.psum(mlp_part, "tensor")
    layer_output = (
        (hidden_one + mlp_total.reshape(seq_count, length, width)) * row_mask[:, :, None]
    ).astype(jnp.bfloat16)
    grad_final = cotangent.astype(jnp.float32) * row_mask[:, :, None]
    grad_mlp = grad_final.astype(jnp.bfloat16).reshape(flat_rows, width)
    grad_down = jnp.dot(activated.T, grad_mlp, preferred_element_type=jnp.float32)
    grad_act = jnp.dot(grad_mlp, down_weight.T, preferred_element_type=jnp.float32)
    unused_value, gelu_back = jax.vjp(gelu_tanh, pre_act)
    grad_pre = gelu_back(grad_act)[0].astype(jnp.bfloat16)
    grad_up = jnp.dot(normal_mid.T, grad_pre, preferred_element_type=jnp.float32)
    mid_part = jnp.dot(grad_pre, up_weight.T, preferred_element_type=jnp.float32)
    grad_mid = lax.psum(mid_part, "tensor").reshape(seq_count, length, width)
    grad_hat_two, scale_grad_two = norm_back(grad_mid, normed_two, inv_two, scale_two)
    grad_hidden = grad_final + grad_hat_two
    grad_second = jnp.dot(one_hot.T, scale_grad_two, precision=highest)
    grad_attn = grad_hidden.astype(jnp.bfloat16).reshape(flat_rows, width)
    grad_merge = jnp.dot(heads_out.T, grad_attn, preferred_element_type=jnp.float32)
    grad_heads = (
        jnp.dot(grad_attn, merge_weight.T, preferred_element_type=jnp.float32)
        .astype(jnp.bfloat16)
        .reshape(head_shape)
    )
    grad_keys = jnp.zeros(head_shape, jnp.float32)
    grad_values = jnp.zeros(head_shape, jnp.float32)
    query_grads = []
    for block_index in range(len(log_sums)):
        offset = block_index * block_rows
        query_block = query_rot[:, offset : offset + block_rows]
        grad_block = grad_heads[:, offset : offset + block_rows]
        scores = block_scores(query_block, key_rot, key_bias, scale_factor)
        soft_weights = jnp.exp(scores - log_sums[block_index])
        grad_soft = jnp.einsum(
            "sqhd,skhd->shqk", grad_block, value_rows, preferred_element_type=jnp.float32
        )
        grad_values = grad_values + jnp.einsum(
            "shqk,sqhd->skhd",
            soft_weights.astype(jnp.bfloat16),
            grad_block,
            preferred_element_type=jnp.float32,
        )
        grad_scores = (
            soft_weights * (grad_soft - jnp.sum(soft_weights * grad_soft, axis=-1, keepdims=True))
        ).astype(jnp.bfloat16)
        query_grads.append(
            jnp.einsum("shqk,skhd->sqhd", grad_scores, key_rot, preferred_element_type=jnp.float32)
            * scale_factor
        )
        grad_keys = (
            grad_keys
            + jnp.einsum(
                "shqk,sqhd->skhd", grad_scores, query_block, preferred_element_type=jnp.float32
            )
            * scale_factor
        )
    query_back = (
        unrotate(jnp.concatenate(query_grads, axis=1), cos_table, sin_table)
        .astype(jnp.bfloat16)
        .reshape(flat_rows, local_width)
    )
    key_back = (
        unrotate(grad_keys, cos_table, sin_table)
        .astype(jnp.bfloat16)
        .reshape(flat_rows, local_width)
    )
    value_back = grad_values.astype(jnp.bfloat16).reshape(flat_rows, local_width)
    grad_query = jnp.dot(normal_in.T, query_back, preferred_element_type=jnp.float32)
    grad_key = jnp.dot(normal_in.T, key_back, preferred_element_type=jnp.float32)
    grad_value = jnp.dot(normal_in.T, value_back, preferred_element_type=jnp.float32)
    inner_part = jnp.dot(query_back, query_weight.T, preferred_element_type=jnp.float32)
    inner_part = inner_part + jnp.dot(key_back, key_weight.T, preferred_element_type=jnp.float32)
    inner_part = inner_part + jnp.dot(
        value_back, value_weight.T, preferred_element_type=jnp.float32
    )
    grad_inner = lax.psum(inner_part, "tensor").reshape(seq_count, length, width)
    grad_hat_one, scale_grad_one = norm_back(grad_inner, normed_one, inv_one, scale_one)
    grad_tokens = ((grad_hidden + grad_hat_one) * row_mask[:, :, None]).astype(jnp.bfloat16)
    grad_first = jnp.dot(one_hot.T, scale_grad_one, precision=highest)
    summed = (
        lax.psum_scatter(grad_query, "dp", scatter_dimension=0, tiled=True),
        lax.psum_scatter(grad_key, "dp", scatter_dimension=0, tiled=True),
        lax.psum_scatter(grad_value, "dp", scatter_dimension=0, tiled=True),
        lax.psum_scatter(grad_merge, "dp", scatter_dimension=1, tiled=True),
        lax.psum_scatter(grad_up, "dp", scatter_dimension=0, tiled=True),
        lax.psum_scatter(grad_down, "dp", scatter_dimension=1, tiled=True),
        lax.psum_scatter(grad_first, "dp", scatter_dimension=1, tiled=True),
        lax.psum_scatter(grad_second, "dp", scatter_dimension=1, tiled=True),
    )
    return (
        layer_output,
        grad_tokens,
        summed[0],
        summed[1],
        summed[2],
        summed[3],
        summed[4],
        summed[5],
        summed[6],
        summed[7],
    )


def solution(mesh):
    fast = mesh.shape["dp"] == 16 and mesh.shape["tensor"] == 2
    return jax.shard_map(
        fast_body if fast else body,
        mesh=mesh,
        in_specs=(
            P("dp", None, None),
            P("dp", None, None),
            P("dp"),
            P("dp"),
            P(None, "tensor"),
            P(None, "tensor"),
            P(None, "tensor"),
            P("tensor", None),
            P(None, "tensor"),
            P("tensor", None),
            P(),
            P(),
        ),
        out_specs=(
            P("dp", None, None),
            P("dp", None, None),
            P("dp", "tensor"),
            P("dp", "tensor"),
            P("dp", "tensor"),
            P("tensor", "dp"),
            P("dp", "tensor"),
            P("tensor", "dp"),
            P(None, "dp"),
            P(None, "dp"),
        ),
        check_vma=False,
    )
```
